32 devices in a mesh: dp: 32 (over z, y, x, core).
Axes of the slice: x: 2, y: 2, z: 4, core: 2. Of those that a mesh axis runs over, the one named last changes fastest.
Arguments:
- tokens: bfloat16 [12288, 2048], P('dp'), may hold values from -6 to 6
- seq_lengths: int32 [32, 3], P('dp'), may hold values from 1 to 256, 384 in all within a row
- ln1_gain: bfloat16 [2048], P('dp'), may hold values from 0.099609375 to 1.8984375
- ln1_bias: bfloat16 [2048], P('dp'), may hold values from -3 to 3
- ln2_gain: bfloat16 [2048], P('dp'), may hold values from 0.099609375 to 1.8984375
- ln2_bias: bfloat16 [2048], P('dp'), may hold values from -3 to 3
- qkv_weight: bfloat16 [2048, 6144], P('dp'), may hold values from -0.125 to 0.125
- qkv_bias: bfloat16 [6144], P('dp'), may hold values from -3 to 3
- dense_weight: bfloat16 [2048, 2048], P('dp'), may hold values from -0.5 to 0.5
- dense_bias: bfloat16 [2048], P('dp'), may hold values from -3 to 3
- expand_weight: bfloat16 [2048, 8192], P('dp'), may hold values from -0.125 to 0.125
- expand_bias: bfloat16 [8192], P('dp'), may hold values from -3 to 3
- contract_weight: bfloat16 [8192, 2048], P('dp'), may hold values from -0.0625 to 0.0625
- contract_bias: bfloat16 [2048], P('dp'), may hold values from -3 to 3
- cotangent: bfloat16 [12288, 2048], P('dp'), may hold values from -6 to 6
Outputs:
- layer_out: bfloat16 [12288, 2048], P('dp')
- input_grad: float32 [12288, 2048], P('dp')
- ln1_gain_grad: float32 [2048], P('dp')
- ln1_bias_grad: float32 [2048], P('dp')
- ln2_gain_grad: float32 [2048], P('dp')
- ln2_bias_grad: float32 [2048], P('dp')
- qkv_weight_grad: float32 [2048, 6144], P('dp')
- qkv_bias_grad: float32 [6144], P('dp')
- dense_weight_grad: float32 [2048, 2048], P('dp')
- dense_bias_grad: float32 [2048], P('dp')
- expand_weight_grad: float32 [2048, 8192], P('dp')
- expand_bias_grad: float32 [8192], P('dp')
- contract_weight_grad: float32 [8192, 2048], P('dp')
- contract_bias_grad: float32 [2048], P('dp')
The draws below stay inside these ranges and needn't reach their ends.
Inputs may be any that keep to these rules, and one draw needn't show every extreme that they name: `seq_lengths`: row d lists, in order, the lengths of the sequences packed into device d's 384 slots; each row sums to 384.
All inputs are finite; a program needn't handle non-finite values.
Results may differ from the reference program's by a relative error of at most 0.011.
Values may be sent and summed in bfloat16 or wider, within the bound.
No kernel may reach another device: no remote copies, remote signals or barrier semaphores. Data moves between devices by JAX's collectives and lax.ppermute only.
A program may use at most 640 MiB of HBM per device.

```python
import math
import jax
import jax.numpy as jnp
import numpy as np
from jax import lax

D = 2048
HEADS = 8
FF = 8192
ROT = 64
CAP = 384
SEQ_DEV = 3
MAXLEN = 256
TOKENS = 12288
N_DP = 32


def shard_levels(stream_key, dims, pieces, least, largest):
    factor_of = 1.0
    for dim, shards_of in pieces:
        draws = jax.random.uniform(jax.random.fold_in(jax.random.fold_in(stream_key, 6), dim), (shards_of,), jnp.float32, least / len(pieces), largest / len(pieces))
        factor_of = factor_of * jnp.repeat(jnp.exp(draws), dims[dim] // shards_of).reshape((-1,) + (1,) * (len(dims) - 1 - dim))
    return factor_of


def profile(amount, total, limit, slope):
    weights = [(1 << 20) // math.isqrt(rank ** slope) + 1 for rank in range(2, amount + 1)]
    surplus, given = total - limit - (amount - 1), [1] * (amount - 1)
    while surplus > 0:
        candidates = [i for i in range(amount - 1) if given[i] < limit]
        whole, remaining = sum([weights[i] for i in candidates]), surplus
        for i in candidates:
            addition = min(limit - given[i], max(1, remaining * weights[i] // whole), surplus)
            given[i] = given[i] + addition
            surplus = surplus - addition
    return np.array([limit] + given)


def ragged_sizes(own_key, count, total, bound, skew):
    if count == 2:
        one = jax.random.randint(own_key, (), max(1, total - bound), min(bound, total - 1) + 1)
        return jnp.stack([one, total - one])
    tallies = jnp.asarray(profile(count, total, bound, skew), jnp.int32)
    twos = (count - 1) // 2
    giver, sink = tallies[1:1 + 2 * twos:2], tallies[2:2 + 2 * twos:2]
    margin = jnp.minimum(giver - 1, bound - sink)
    passed = jax.random.randint(jax.random.fold_in(own_key, 1), (twos,), 0, 1 << 20) % (margin + 1)
    tallies = tallies.at[1:1 + 2 * twos:2].set(giver - passed).at[2:2 + 2 * twos:2].set(sink + passed)
    return tallies[jax.random.permutation(jax.random.fold_in(own_key, 2), count)]


def centred(rng, shape, scale, reach, shards=(), held_as=jnp.bfloat16):
    values = jax.random.normal(rng, shape, jnp.float32) * scale
    if len(shards) > 0:
        values = shard_levels(rng, shape, shards, -0.22, 0.18) * values
    return jnp.clip(values, min=-reach, max=reach).astype(held_as)


def setup_inputs(seed: int = 0) -> dict:
    streams_of = jax.random.split(jax.random.key(seed), 16)
    return {
        "tokens": centred(streams_of[0], (TOKENS, D), 1.0, 6.0, ((0, 32),)),
        "seq_lengths": jax.vmap(lambda own: ragged_sizes(own, SEQ_DEV, CAP, MAXLEN, 2))(jax.random.split(streams_of[1], N_DP)).reshape((N_DP, SEQ_DEV)).astype(jnp.int32),
        "ln1_gain": jnp.clip(1.0 + 0.18 * jax.random.normal(streams_of[2], (D,), jnp.float32), 0.099609375, 1.8984375).astype(jnp.bfloat16),
        "ln1_bias": centred(streams_of[3], (D,), 0.5, 3.0, ((0, 32),)),
        "ln2_gain": jnp.clip(1.0 + 0.18 * jax.random.normal(streams_of[4], (D,), jnp.float32), 0.099609375, 1.8984375).astype(jnp.bfloat16),
        "ln2_bias": centred(streams_of[5], (D,), 0.5, 3.0, ((0, 32),)),
        "qkv_weight": centred(streams_of[6], (D, 3 * D), D ** -0.5, 0.125, ((0, 32),)),
        "qkv_bias": centred(streams_of[7], (3 * D,), 0.5, 3.0, ((0, 32),)),
        "dense_weight": centred(streams_of[8], (D, D), (D // 16) ** -0.5, 0.5, ((0, 32),)),
        "dense_bias": centred(streams_of[9], (D,), 0.5, 3.0, ((0, 32),)),
        "expand_weight": centred(streams_of[10], (D, FF), D ** -0.5, 0.125, ((0, 32),)),
        "expand_bias": centred(streams_of[11], (FF,), 0.5, 3.0, ((0, 32),)),
        "contract_weight": centred(streams_of[12], (FF, D), FF ** -0.5, 0.0625, ((0, 32),)),
        "contract_bias": centred(streams_of[13], (D,), 0.5, 3.0, ((0, 32),)),
        "cotangent": centred(streams_of[14], (TOKENS, D), 1.0, 6.0, ((0, 32),)),
    }


@jax.custom_vjp
def low(v):
    return lax.optimization_barrier(v.astype(jnp.bfloat16)).astype(jnp.float32)

@jax.custom_vjp
def low_back(v):
    return v

def low_keep(v):
    return (low(v), None)

def low_pass(kept, grad):
    return (grad,)

def back_keep(v):
    return (v, None)

def back_low(kept, grad):
    return (low(grad),)
low.defvjp(low_keep, low_pass)
low_back.defvjp(back_keep, back_low)
EPSILON = 1e-05
HIGHEST = lax.Precision.HIGHEST
MASKED = -1e+30

def slot_layout(lengths, slots):
    place = jnp.arange(slots, dtype=jnp.int32)
    ends = jnp.cumsum(lengths, dtype=jnp.int32)
    after = (place[:, None] >= ends[None, :]).astype(jnp.int32)
    segment = lax.optimization_barrier(jnp.sum(after, axis=1, dtype=jnp.int32))
    offset = lax.optimization_barrier(jnp.sum(after * lengths[None, :], axis=1, dtype=jnp.int32))
    return (segment, place - offset)

def rotary_tables(position, rotated):
    half = rotated // 2
    ladder = jnp.arange(half, dtype=jnp.float32) * (-math.log(10000.0) / half)
    angle = position.astype(jnp.float32)[:, None] * jnp.exp(ladder)[None, :]
    return (jnp.cos(angle), jnp.sin(angle))

def rotate(value, cosine, sine, heads, rotated):
    count = value.shape[0]
    shaped = value.reshape(count, heads, -1)
    half = rotated // 2
    first = shaped[:, :, :half]
    second = shaped[:, :, half:rotated]
    across = cosine[:, None, :]
    upward = sine[:, None, :]
    turned = jnp.concatenate([first * across - second * upward, second * across + first * upward, shaped[:, :, rotated:]], axis=2)
    return turned.reshape(count, -1)

def norm_rows(value, gain, shift):
    centre = lax.optimization_barrier(jnp.mean(value, axis=1, keepdims=True))
    spread = value - centre
    variance = lax.optimization_barrier(jnp.mean(spread * spread, axis=1, keepdims=True))
    return spread * lax.rsqrt(variance + EPSILON) * gain + shift

def smooth_gate(value):
    return jax.nn.gelu(value, approximate=False)

def allowed_pairs(segment):
    place = jnp.arange(segment.shape[0], dtype=jnp.int32)
    return (segment[:, None] == segment[None, :]) & (place[None, :] <= place[:, None])

def attend_block(block):
    query, key, value, segment = block
    count, width = query.shape
    head_dim = width // HEADS
    query_heads = query.reshape(count, HEADS, head_dim)
    key_heads = key.reshape(count, HEADS, head_dim)
    value_heads = value.reshape(count, HEADS, head_dim)
    raw = jnp.einsum('qhd,khd->hqk', query_heads, key_heads, precision=HIGHEST)
    scores = low_back(raw * (1.0 / math.sqrt(head_dim)))
    masked = jnp.where(allowed_pairs(segment)[None], scores, MASKED)
    weights = low(jax.nn.softmax(masked, axis=-1))
    mixed = jnp.einsum('hqk,khd->qhd', weights, value_heads, precision=HIGHEST)
    return low(low_back(mixed.reshape(count, width)))

def reference(tokens, seq_lengths, ln1_gain, ln1_bias, ln2_gain, ln2_bias, qkv_weight, qkv_bias, dense_weight, dense_bias, expand_weight, expand_bias, contract_weight, contract_bias, cotangent):
    params = tuple((item.astype(jnp.float32) for item in (ln1_gain, ln1_bias, ln2_gain, ln2_bias, qkv_weight, qkv_bias, dense_weight, dense_bias, expand_weight, expand_bias, contract_weight, contract_bias)))
    segment, position = jax.vmap(lambda lengths: slot_layout(lengths, CAP))(seq_lengths)
    cosine, sine = rotary_tables(position.reshape(-1), ROT)

    def forward(inputs, gain_one, shift_one, gain_two, shift_two, w_qkv, b_qkv, w_dense, b_dense, w_expand, b_expand, w_contract, b_contract):
        normed_one = low(norm_rows(inputs, gain_one, shift_one))
        normed_two = low(norm_rows(inputs, gain_two, shift_two))
        projected = low_back(jnp.dot(normed_one, w_qkv, precision=HIGHEST, preferred_element_type=jnp.float32) + b_qkv)
        query = low(rotate(projected[:, :D], cosine, sine, HEADS, ROT))
        key = low(rotate(projected[:, D:2 * D], cosine, sine, HEADS, ROT))
        value = low(projected[:, 2 * D:])
        blocks = (query.reshape(N_DP, CAP, D), key.reshape(N_DP, CAP, D), value.reshape(N_DP, CAP, D), segment)
        attn = lax.map(jax.checkpoint(attend_block), blocks).reshape(TOKENS, D)
        hidden = low_back(jnp.dot(normed_two, w_expand, precision=HIGHEST, preferred_element_type=jnp.float32) + b_expand)
        active = low(smooth_gate(hidden))
        branch_attn = jnp.dot(attn, w_dense, precision=HIGHEST, preferred_element_type=jnp.float32) + b_dense
        branch_mlp = jnp.dot(active, w_contract, precision=HIGHEST, preferred_element_type=jnp.float32) + b_contract
        return inputs + branch_attn + branch_mlp
    result, pull = jax.vjp(forward, tokens.astype(jnp.float32), *params)
    grads = pull(cotangent.astype(jnp.float32))
    return (result.astype(jnp.bfloat16), grads[0], grads[1], grads[2], grads[3], grads[4], grads[5], grads[6], grads[7], grads[8], grads[9], grads[10], grads[11], grads[12])
```

```python
import math

import jax
import jax.numpy as jnp
from jax import lax
from jax.sharding import PartitionSpec as P


HEADS = 8

EPSILON = 1e-05
MASKED = -1e30
PAIRED = (((1,), (1,)), ((), ()))
LEADING = (((0,), (0,)), ((), ()))


class Plan:
    def __init__(self, count):
        self.count = count
        self.bits = count.bit_length() - 1
        self.inner = (3, 1, 0) if count == 32 else (2, 1, 0)
        self.outer = tuple(b for b in reversed(range(self.bits)) if b not in self.inner)
        self.groups = count // HEADS

    def device(self, group, slot):
        found = 0
        for place, bit in enumerate(reversed(self.outer)):
            found |= ((group >> place) & 1) << bit
        for place, bit in enumerate(reversed(self.inner)):
            found |= ((slot >> place) & 1) << bit
        return found

    def inner_groups(self):
        return [
            [self.device(group, slot) for slot in range(HEADS)] for group in range(self.groups)
        ]

    def flip(self, bit):
        return [(d, d ^ (1 << bit)) for d in range(self.count)]


def bit_of(index, bit):
    return (index >> bit) & 1


def gather_bits(value, bits, plan):
    pieces = [(0, value)]
    for bit in bits:
        pieces += [
            (mask | (1 << bit), lax.ppermute(piece, "dp", plan.flip(bit)))
            for mask, piece in pieces
        ]
    return pieces


def place_outer(pieces, me, plan):
    shape = pieces[0][1].shape
    held = jnp.zeros((2,) * len(plan.outer) + shape, pieces[0][1].dtype)
    for mask, piece in pieces:
        start = [bit_of(me ^ mask, bit) for bit in plan.outer] + [0] * len(shape)
        held = lax.dynamic_update_slice(held, piece.reshape((1,) * len(plan.outer) + shape), start)
    return held.reshape((plan.groups,) + shape)


def place_all(pieces, me, plan):
    rest = pieces[0][1].shape[1:]
    held = jnp.zeros((2,) * plan.bits + rest, pieces[0][1].dtype)
    order = list(reversed(range(plan.bits)))
    for mask, piece in pieces:
        start = [bit_of(me ^ mask, b) if b in plan.outer else 0 for b in order] + [0] * len(rest)
        block = piece.reshape(tuple(1 if b in plan.outer else 2 for b in order) + rest)
        held = lax.dynamic_update_slice(held, block, start)
    return held.reshape((plan.count,) + rest)


def reduce_outer(value, me, plan):
    rest = value.shape[1:]
    held = value.reshape((2,) * len(plan.outer) + rest)
    for place in reversed(range(len(plan.outer))):
        bit = plan.outer[place]
        mine = bit_of(me, bit)
        kept = lax.dynamic_index_in_dim(held, mine, place, keepdims=True)
        sent = lax.dynamic_index_in_dim(held, 1 - mine, place, keepdims=True)
        got = lax.ppermute(sent.astype(jnp.bfloat16), "dp", plan.flip(bit))
        held = kept.astype(jnp.float32) + got.astype(jnp.float32)
    return held.reshape(rest)


def slot_layout(lengths, slots):
    place = jnp.arange(slots, dtype=jnp.int32)
    ends = jnp.cumsum(lengths, dtype=jnp.int32)
    after = (place[:, None] >= ends[None, :]).astype(jnp.int32)
    segment = jnp.sum(after, axis=1, dtype=jnp.int32)
    offset = jnp.sum(after * lengths[None, :], axis=1, dtype=jnp.int32)
    return (segment, place - offset)


def rotary_tables(position, rotated):
    half = rotated // 2
    ladder = jnp.arange(half, dtype=jnp.float32) * (-math.log(10000.0) / half)
    angle = position.astype(jnp.float32)[:, None] * jnp.exp(ladder)[None, :]
    return (jnp.cos(angle), jnp.sin(angle))


def rotate(value, cosine, sine, sign):
    half = cosine.shape[-1]
    first = value[:, :half]
    second = value[:, half : 2 * half]
    return jnp.concatenate(
        [
            first * cosine - sign * second * sine,
            second * cosine + sign * first * sine,
            value[:, 2 * half :],
        ],
        axis=1,
    )


def norm_terms(value):
    centre = jnp.mean(value, axis=1, keepdims=True)
    spread = value - centre
    variance = jnp.mean(spread * spread, axis=1, keepdims=True)
    scale = lax.rsqrt(variance + EPSILON)
    return (spread * scale, scale)


def times_leading(left, right):
    return lax.dot_general(left, right, LEADING, preferred_element_type=jnp.float32)


def times_paired(left, right):
    return lax.dot_general(left, right, PAIRED, preferred_element_type=jnp.float32)


def attend(query, key, value, grad_attn, segment, scale):
    place = jnp.arange(segment.shape[1], dtype=jnp.int32)
    allowed = (segment[:, :, None] == segment[:, None, :]) & (
        place[None, None, :] <= place[None, :, None]
    )

    def batched(spec, left, right):
        return jnp.einsum(spec, left, right, preferred_element_type=jnp.float32)

    scores = batched("bqd,bkd->bqk", query, key) * scale
    masked = jnp.where(allowed, scores, MASKED)
    highest = jnp.max(masked, axis=2, keepdims=True)
    raised = jnp.exp(masked - highest)
    weights = raised / jnp.sum(raised, axis=2, keepdims=True)
    probs = weights.astype(jnp.bfloat16)
    attn = batched("bqk,bkd->bqd", probs, value).astype(jnp.bfloat16)
    grad_probs = batched("bqd,bkd->bqk", grad_attn, value)
    grad_value = batched("bqk,bqd->bkd", probs, grad_attn)
    inner = jnp.sum(weights * grad_probs, axis=2, keepdims=True)
    grad_score = (weights * (grad_probs - inner)).astype(jnp.bfloat16)
    grad_query = batched("bqk,bkd->bqd", grad_score, key) * scale
    grad_key = batched("bqk,bqd->bkd", grad_score, query) * scale
    return (attn, grad_query, grad_key, grad_value)


def per_device(
    plan,
    tokens,
    seq_lengths,
    ln1_gain,
    ln1_bias,
    ln2_gain,
    ln2_bias,
    qkv_weight,
    qkv_bias,
    dense_weight,
    dense_bias,
    expand_weight,
    expand_bias,
    contract_weight,
    contract_bias,
    cotangent,
):
    slots, width = tokens.shape
    rows = qkv_weight.shape[0]
    units = contract_weight.shape[0]
    count, groups = plan.count, plan.groups
    head_dim = width // HEADS
    rotated = head_dim // 4
    scale = 1.0 / math.sqrt(head_dim)
    me = lax.axis_index("dp")
    inner_groups = plan.inner_groups()
    slot = sum(bit_of(me, bit) << place for place, bit in enumerate(reversed(plan.inner)))

    parts = [
        ln1_gain,
        ln1_bias,
        ln2_gain,
        ln2_bias,
        dense_bias,
        contract_bias,
        qkv_bias,
        expand_bias,
        seq_lengths[0].astype(jnp.bfloat16),
    ]
    sizes = [item.shape[0] for item in parts]
    total = sum(sizes)
    padded = -(-total // 1024) * 1024
    small = jnp.concatenate(parts + [jnp.zeros((padded - total,), jnp.bfloat16)])
    every = lax.all_gather(small, "dp", axis=0, tiled=False).astype(jnp.float32)
    taken, at = [], 0
    for size in sizes:
        taken.append(every[:, at : at + size])
        at += size
    gain_one, shift_one, gain_two, shift_two, bias_dense, bias_contract = [
        item.reshape(1, width) for item in taken[:6]
    ]
    bias_qkv = lax.dynamic_index_in_dim(
        taken[6].reshape(3, HEADS, head_dim), slot, 1, keepdims=False
    ).reshape(1, 3 * head_dim)

    def of_slot(value):
        rest = value.shape[1:]
        shaped = value.reshape((2,) * plan.bits + rest)
        order = list(reversed(range(plan.bits)))
        for place, bit in enumerate(order):
            if bit in plan.inner:
                shaped = lax.dynamic_slice_in_dim(shaped, bit_of(me, bit), 1, place)
        return shaped.reshape((groups,) + rest)

    def of_group(value):
        rest = value.shape[1:]
        shaped = value.reshape((2,) * plan.bits + rest)
        order = list(reversed(range(plan.bits)))
        for place, bit in enumerate(order):
            if bit in plan.outer:
                shaped = lax.dynamic_slice_in_dim(shaped, bit_of(me, bit), 1, place)
        return shaped.reshape((HEADS,) + rest)

    bias_expand = of_slot(taken[7]).reshape(1, groups * units)
    lengths = of_group(taken[8]).astype(jnp.int32)

    group_tokens = lax.all_gather(
        tokens, "dp", axis=0, tiled=True, axis_index_groups=inner_groups
    )
    group_cotangent = lax.all_gather(
        cotangent, "dp", axis=0, tiled=True, axis_index_groups=inner_groups
    )

    columns = [plan.device(group, s) for s in range(HEADS) for group in range(groups)]
    qkv_parts = qkv_weight.reshape(rows, 3, HEADS, head_dim).transpose(2, 0, 1, 3)
    expand_parts = expand_weight.reshape(rows, count, units)[:, jnp.array(columns)]
    expand_parts = expand_parts.reshape(rows, HEADS, groups * units).transpose(1, 0, 2)
    both = jnp.concatenate([qkv_parts.reshape(HEADS, rows, 3 * head_dim), expand_parts], axis=2)
    both = lax.all_to_all(both, "dp", 0, 0, tiled=True, axis_index_groups=inner_groups)
    weight_in = place_all(gather_bits(both, plan.outer, plan), me, plan).reshape(width, -1)
    weight_qkv = weight_in[:, : 3 * head_dim]
    weight_expand = weight_in[:, 3 * head_dim :]

    to_slot = [(d, plan.device(d % groups, d // groups)) for d in range(count)]
    from_slot = [(target, source) for source, target in to_slot]
    dense_part = lax.ppermute(dense_weight, "dp", to_slot)
    weight_dense = place_outer(gather_bits(dense_part, plan.outer, plan), me, plan)
    weight_dense = weight_dense.reshape(head_dim, width)
    weight_contract = place_outer(gather_bits(contract_weight, plan.outer, plan), me, plan)
    weight_contract = weight_contract.reshape(groups * units, width)

    segment, position = jax.vmap(lambda item: slot_layout(item, slots))(lengths)
    cosine, sine = rotary_tables(position.reshape(-1), rotated)
    normed, _ = norm_terms(group_tokens.astype(jnp.float32))
    low_one = (normed * gain_one + shift_one).astype(jnp.bfloat16)
    low_two = (normed * gain_two + shift_two).astype(jnp.bfloat16)
    low_normed = normed.astype(jnp.bfloat16)
    projected = jnp.dot(low_one, weight_qkv, preferred_element_type=jnp.float32) + bias_qkv
    query = rotate(projected[:, :head_dim], cosine, sine, 1.0).astype(jnp.bfloat16)
    key = rotate(projected[:, head_dim : 2 * head_dim], cosine, sine, 1.0).astype(jnp.bfloat16)
    value = projected[:, 2 * head_dim :].astype(jnp.bfloat16)
    hidden = jnp.dot(low_two, weight_expand, preferred_element_type=jnp.float32) + bias_expand
    active_full, gate_pull = jax.vjp(lambda v: jax.nn.gelu(v, approximate=False), hidden)
    active = active_full.astype(jnp.bfloat16)
    grad_attn = times_paired(group_cotangent, weight_dense).astype(jnp.bfloat16)

    def blocked(item):
        return item.reshape(HEADS, slots, head_dim)

    attn, grad_query, grad_key, grad_value = attend(
        blocked(query), blocked(key), blocked(value), blocked(grad_attn), segment, scale
    )
    attn = attn.reshape(HEADS * slots, head_dim)
    grad_query, grad_key, grad_value = [
        item.reshape(HEADS * slots, head_dim) for item in (grad_query, grad_key, grad_value)
    ]
    branch = jnp.dot(attn, weight_dense, preferred_element_type=jnp.float32) + jnp.dot(
        active, weight_contract, preferred_element_type=jnp.float32
    )
    branch = lax.psum_scatter(
        branch.astype(jnp.bfloat16),
        "dp",
        scatter_dimension=0,
        tiled=True,
        axis_index_groups=inner_groups,
    )
    inputs = tokens.astype(jnp.float32)
    layer_out = (inputs + branch.astype(jnp.float32) + bias_dense + bias_contract).astype(
        jnp.bfloat16
    )

    grad_active = times_paired(group_cotangent, weight_contract)
    (grad_hidden,) = gate_pull(grad_active)
    grad_hidden = grad_hidden.astype(jnp.bfloat16)
    grad_qkv = jnp.concatenate(
        [
            rotate(grad_query, cosine, sine, -1.0),
            rotate(grad_key, cosine, sine, -1.0),
            grad_value,
        ],
        axis=1,
    ).astype(jnp.bfloat16)
    grad_both = (
        times_paired(grad_qkv, weight_qkv) * gain_one
        + times_paired(grad_hidden, weight_expand) * gain_two
    )
    grad_both = lax.psum_scatter(
        grad_both.astype(jnp.bfloat16),
        "dp",
        scatter_dimension=0,
        tiled=True,
        axis_index_groups=inner_groups,
    ).astype(jnp.float32)
    own_normed, own_scale = norm_terms(inputs)
    input_grad = (
        cotangent.astype(jnp.float32)
        + (
            grad_both
            - jnp.mean(grad_both, axis=1, keepdims=True)
            - own_normed * jnp.mean(grad_both * own_normed, axis=1, keepdims=True)
        )
        * own_scale
    )

    contract_terms = times_leading(active, group_cotangent).astype(jnp.bfloat16)
    contract_weight_grad = reduce_outer(contract_terms.reshape(groups, units, width), me, plan)
    dense_terms = times_leading(attn, group_cotangent).astype(jnp.bfloat16)
    dense_weight_grad = reduce_outer(dense_terms.reshape(groups, rows, width), me, plan)
    dense_weight_grad = lax.ppermute(
        dense_weight_grad.astype(jnp.bfloat16), "dp", from_slot
    ).astype(jnp.float32)
    bias_out_grad = lax.psum_scatter(
        jnp.sum(cotangent.astype(jnp.float32), axis=0), "dp", scatter_dimension=0, tiled=True
    )

    def input_terms(grad):
        terms = times_leading(low_normed, grad)
        shaped = terms.reshape((2,) * plan.bits + (rows, -1))
        order = list(reversed(range(plan.bits)))
        shaped = shaped.transpose(
            [order.index(b) for b in plan.outer]
            + [order.index(b) for b in plan.inner]
            + [plan.bits, plan.bits + 1]
        ).reshape(groups, HEADS * rows, -1)
        sums = jnp.sum(grad.astype(jnp.float32), axis=0)
        sums = jnp.broadcast_to(sums, (groups, 16, sums.shape[0]))
        return jnp.concatenate([shaped, sums], axis=1).astype(jnp.bfloat16)

    def finish(reduced):
        core = reduced[: HEADS * rows].reshape(HEADS, rows, -1)
        sums = jnp.broadcast_to(reduced[None, HEADS * rows :], (HEADS, 16, reduced.shape[1]))
        sent = jnp.concatenate([core, sums], axis=1).astype(jnp.bfloat16)
        got = lax.all_to_all(sent, "dp", 0, 0, tiled=True, axis_index_groups=inner_groups)
        got = got.astype(jnp.float32)
        return got[:, :rows], got[:, rows]

    expand_got, expand_sums = finish(reduce_outer(input_terms(grad_hidden), me, plan))
    qkv_got, qkv_sums = finish(reduce_outer(input_terms(grad_qkv), me, plan))
    qkv_got = qkv_got.reshape(HEADS, rows, 3, head_dim).transpose(1, 2, 0, 3)
    qkv_got = qkv_got.reshape(rows, 3 * width)
    qkv_sums = qkv_sums.reshape(HEADS, 3, head_dim).transpose(1, 0, 2).reshape(3 * width)
    inverse = [0] * count
    for place, device in enumerate(columns):
        inverse[device] = place
    inverse = jnp.array(inverse)
    expand_got = expand_got.reshape(HEADS, rows, groups, units).transpose(1, 0, 2, 3)
    expand_got = expand_got.reshape(rows, count, units)[:, inverse].reshape(rows, count * units)
    expand_sums = expand_sums.reshape(count, units)[inverse].reshape(count * units)

    def input_grads(got, sums, weight, gain, shift):
        weight = weight.astype(jnp.float32)
        gain = gain.astype(jnp.float32)
        shift = shift.astype(jnp.float32)
        return (
            got * gain[:, None] + shift[:, None] * sums[None, :],
            jnp.sum(weight * got, axis=1),
            jnp.sum(weight * sums[None, :], axis=1),
        )

    qkv_weight_grad, ln1_gain_grad, ln1_bias_grad = input_grads(
        qkv_got, qkv_sums, qkv_weight, ln1_gain, ln1_bias
    )
    expand_weight_grad, ln2_gain_grad, ln2_bias_grad = input_grads(
        expand_got, expand_sums, expand_weight, ln2_gain, ln2_bias
    )
    per = qkv_bias.shape[0]
    return (
        layer_out,
        input_grad,
        ln1_gain_grad,
        ln1_bias_grad,
        ln2_gain_grad,
        ln2_bias_grad,
        qkv_weight_grad,
        lax.dynamic_slice_in_dim(qkv_sums, me * per, per),
        dense_weight_grad,
        bias_out_grad,
        expand_weight_grad,
        lax.dynamic_slice_in_dim(expand_sums, me * units, units),
        contract_weight_grad,
        bias_out_grad,
    )


def solution(mesh):
    in_specs = (
        P("dp", None),
        P("dp", None),
        P("dp"),
        P("dp"),
        P("dp"),
        P("dp"),
        P("dp", None),
        P("dp"),
        P("dp", None),
        P("dp"),
        P("dp", None),
        P("dp"),
        P("dp", None),
        P("dp"),
        P("dp", None),
    )
    out_specs = (
        P("dp", None),
        P("dp", None),
        P("dp"),
        P("dp"),
        P("dp"),
        P("dp"),
        P("dp", None),
        P("dp"),
        P("dp", None),
        P("dp"),
        P("dp", None),
        P("dp"),
        P("dp", None),
        P("dp"),
    )
    plan = Plan(mesh.shape["dp"])

    def layer(*arrays):
        return per_device(plan, *arrays)

    return jax.shard_map(layer, mesh=mesh, in_specs=in_specs, out_specs=out_specs, check_vma=False)
```

```python
import math

import jax
import jax.numpy as jnp
from jax import lax
from jax.experimental import pallas as pl
from jax.experimental.pallas import tpu as pltpu
from jax.sharding import PartitionSpec as P


HEADS = 8

EPSILON = 1e-05
MASKED = -1e30
PAIRED = (((1,), (1,)), ((), ()))
LEADING = (((0,), (0,)), ((), ()))
VMEM_LIMIT = 60 * 2**20


class Plan:
    def __init__(self, count):
        self.count = count
        self.bits = count.bit_length() - 1
        self.inner = (3, 1, 0) if count == 32 else (2, 1, 0)
        self.outer = (2, 4) if count == 32 else tuple(range(self.bits - 1, 2, -1))
        self.order = tuple(reversed(range(self.bits)))
        self.groups = count // HEADS

    def device(self, group, slot):
        found = 0
        for place, bit in enumerate(reversed(self.outer)):
            found |= ((group >> place) & 1) << bit
        for place, bit in enumerate(reversed(self.inner)):
            found |= ((slot >> place) & 1) << bit
        return found

    def inner_groups(self):
        return [
            [self.device(group, slot) for slot in range(HEADS)] for group in range(self.groups)
        ]

    def flip(self, bit):
        return [(d, d ^ (1 << bit)) for d in range(self.count)]


def bit_of(index, bit):
    return (index >> bit) & 1


def swap(value, bit, plan):
    return lax.ppermute(value, "dp", plan.flip(bit))


def gather_outer(value, plan):
    pieces = [(0, value)]
    for bit in reversed(plan.outer):
        pieces += [(mask | (1 << bit), swap(piece, bit, plan)) for mask, piece in pieces]
    return pieces


def gather_small(value, bits, me, plan):
    for bit in reversed(bits):
        got = swap(value, bit, plan)
        low = bit_of(me, bit) == 0
        value = jnp.where(
            low, jnp.concatenate([value, got]), jnp.concatenate([got, value])
        )
    return value


def place_outer(pieces, me, plan):
    shape = pieces[0][1].shape
    held = jnp.zeros((2,) * len(plan.outer) + shape, pieces[0][1].dtype)
    for mask, piece in pieces:
        start = [bit_of(me ^ mask, bit) for bit in plan.outer] + [0] * len(shape)
        held = lax.dynamic_update_slice(held, piece.reshape((1,) * len(plan.outer) + shape), start)
    return held.reshape((plan.groups,) + shape)


def place_all(pieces, me, plan):
    rest = pieces[0][1].shape[1:]
    held = jnp.zeros((2,) * plan.bits + rest, pieces[0][1].dtype)
    for mask, piece in pieces:
        start = [bit_of(me ^ mask, b) if b in plan.outer else 0 for b in plan.order]
        block = piece.reshape(tuple(1 if b in plan.outer else 2 for b in plan.order) + rest)
        held = lax.dynamic_update_slice(held, block, start + [0] * len(rest))
    return held.reshape((plan.count,) + rest)


def reduce_rest(kept, got, me, plan):
    rest = kept.shape[1:]
    shape = (2,) * (len(plan.outer) - 1) + rest
    held = kept.reshape(shape).astype(jnp.float32) + got.reshape(shape).astype(jnp.float32)
    for bit in plan.outer[1:]:
        mine = bit_of(me, bit)
        sent = lax.dynamic_index_in_dim(held, 1 - mine, 0, keepdims=False).astype(jnp.bfloat16)
        held = lax.dynamic_index_in_dim(held, mine, 0, keepdims=False)
        held = held + swap(sent, bit, plan).astype(jnp.float32)
    return held


def slot_layout(lengths, slots):
    place = jnp.arange(slots, dtype=jnp.int32)
    ends = jnp.cumsum(lengths, dtype=jnp.int32)
    after = (place[:, None] >= ends[None, :]).astype(jnp.int32)
    segment = jnp.sum(after, axis=1, dtype=jnp.int32)
    offset = jnp.sum(after * lengths[None, :], axis=1, dtype=jnp.int32)
    return (segment, place - offset)


def rotary_tables(position, rotated, lanes):
    half = rotated // 2
    ladder = jnp.arange(half, dtype=jnp.float32) * (-math.log(10000.0) / half)
    angle = position.astype(jnp.float32)[:, None] * jnp.exp(ladder)[None, :]
    cosine, sine = jnp.cos(angle), jnp.sin(angle)
    rest = (position.shape[0], lanes - rotated)
    return (
        jnp.concatenate([cosine, cosine, jnp.ones(rest, jnp.float32)], axis=1),
        jnp.concatenate([-sine, sine, jnp.zeros(rest, jnp.float32)], axis=1),
    )


def norm_terms(value):
    centre = jnp.mean(value, axis=1, keepdims=True)
    spread = value - centre
    variance = jnp.mean(spread * spread, axis=1, keepdims=True)
    scale = lax.rsqrt(variance + EPSILON)
    return (spread * scale, scale)


def times(left, right):
    return jnp.dot(left, right, preferred_element_type=jnp.float32)


def times_leading(left, right):
    return lax.dot_general(left, right, LEADING, preferred_element_type=jnp.float32)


def times_paired(left, right):
    return lax.dot_general(left, right, PAIRED, preferred_element_type=jnp.float32)


def over_blocks(kernel, slots, blocked, whole, outs, flops):
    count = blocked[0].shape[0] // slots
    held = sum(item.size * item.dtype.itemsize for item in blocked + whole)
    made = sum(count * slots * columns * jnp.dtype(kind).itemsize for columns, kind in outs)
    return pl.pallas_call(
        kernel,
        grid=(count,),
        in_specs=[pl.BlockSpec((slots, item.shape[1]), lambda i: (i, 0)) for item in blocked]
        + [pl.BlockSpec(item.shape, lambda i: (0, 0)) for item in whole],
        out_specs=[pl.BlockSpec((slots, columns), lambda i: (i, 0)) for columns, _ in outs],
        out_shape=[jax.ShapeDtypeStruct((count * slots, columns), kind) for columns, kind in outs],
        compiler_params=pltpu.CompilerParams(vmem_limit_bytes=VMEM_LIMIT),
        cost_estimate=pl.CostEstimate(flops=flops, bytes_accessed=held + made, transcendentals=0),
    )(*blocked, *whole)


def turn(value, cosine, sine, half):
    lane = lax.broadcasted_iota(jnp.int32, value.shape, 1)
    lanes = value.shape[1]
    swapped = jnp.where(
        lane < half, pltpu.roll(value, lanes - half, 1), pltpu.roll(value, half, 1)
    )
    return value * cosine + swapped * sine


def turn_into(out, at, value, cosine, sine, half):
    lanes = cosine.shape[1]
    turned = turn(value[:, :lanes], cosine, sine, half)
    out[:, at : at + lanes] = turned.astype(jnp.bfloat16)
    out[:, at + lanes : at + value.shape[1]] = value[:, lanes:].astype(jnp.bfloat16)


def qkv_kernel(head_dim, x, cosine, sine, weight, bias, out):
    projected = times(x[...], weight[...]) + bias[...]
    half = head_dim // 8
    for part in range(2):
        at = part * head_dim
        turn_into(out, at, projected[:, at : at + head_dim], cosine[...], sine[...], half)
    out[:, 2 * head_dim :] = projected[:, 2 * head_dim :].astype(jnp.bfloat16)


def expand_kernel(x, weight, bias, active, slope):
    hidden = times(x[...], weight[...]) + bias[...]
    below = 0.5 * (1.0 + lax.erf(hidden * math.sqrt(0.5)))
    density = jnp.exp(-0.5 * hidden * hidden) * (1.0 / math.sqrt(2.0 * math.pi))
    active[...] = (hidden * below).astype(jnp.bfloat16)
    slope[...] = below + hidden * density


def grad_hidden_kernel(cotangent, slope, weight, out):
    out[...] = (times_paired(cotangent[...], weight[...]) * slope[...]).astype(jnp.bfloat16)


def branch_kernel(attn, active, dense, contract, out):
    total = times(attn[...], dense[...]) + times(active[...], contract[...])
    out[...] = total.astype(jnp.bfloat16)


def grad_norm_kernel(grad_qkv, grad_hidden, qkv, expand, gain_one, gain_two, out):
    total = (
        times_paired(grad_qkv[...], qkv[...]) * gain_one[...]
        + times_paired(grad_hidden[...], expand[...]) * gain_two[...]
    )
    out[...] = total.astype(jnp.bfloat16)


def attend_kernel(
    head_dim, qkv, cotangent, cosine, sine, segment, dense, segments, attn, grad_qkv
):
    scale = 1.0 / math.sqrt(head_dim)
    query = qkv[:, :head_dim]
    key = qkv[:, head_dim : 2 * head_dim]
    value = qkv[:, 2 * head_dim :]
    grad_attn = times_paired(cotangent[...], dense[...]).astype(jnp.bfloat16)
    slots = query.shape[0]
    row = lax.broadcasted_iota(jnp.int32, (slots, slots), 0)
    column = lax.broadcasted_iota(jnp.int32, (slots, slots), 1)
    block = pl.program_id(0)
    allowed = (segment[...] == segments[pl.ds(block, 1), :]) & (column <= row)
    masked = jnp.where(allowed, times_paired(query, key) * scale, MASKED)
    raised = jnp.exp(masked - jnp.max(masked, axis=1, keepdims=True))
    weights = raised / jnp.sum(raised, axis=1, keepdims=True)
    probs = weights.astype(jnp.bfloat16)
    attn[...] = times(probs, value).astype(jnp.bfloat16)
    grad_probs = times_paired(grad_attn, value)
    grad_value = times_leading(probs, grad_attn)
    inner = jnp.sum(weights * grad_probs, axis=1, keepdims=True)
    grad_score = (weights * (grad_probs - inner)).astype(jnp.bfloat16)
    half = head_dim // 8
    back = -sine[...]
    grad_query = times(grad_score, key) * scale
    turn_into(grad_qkv, 0, grad_query, cosine[...], back, half)
    grad_key = times_leading(grad_score, query) * scale
    turn_into(grad_qkv, head_dim, grad_key, cosine[...], back, half)
    grad_qkv[:, 2 * head_dim :] = grad_value.astype(jnp.bfloat16)


def input_terms_kernel(_, left, right, out):
    out[...] = times_leading(left[...], right[...]).astype(jnp.bfloat16)


def input_terms(normed, grad, blocks, block):
    depth, width = normed.shape
    columns = grad.shape[1]
    count = blocks.shape[0]
    rows = count * block
    return pl.pallas_call(
        input_terms_kernel,
        grid_spec=pltpu.PrefetchScalarGridSpec(
            num_scalar_prefetch=1,
            grid=(count,),
            in_specs=[
                pl.BlockSpec((depth, block), lambda i, blocks: (0, blocks[i])),
                pl.BlockSpec(
                    (depth, columns), lambda i, blocks: (0, 0), pipeline_mode=pl.Buffered(1)
                ),
            ],
            out_specs=pl.BlockSpec((block, columns), lambda i, blocks: (i, 0)),
        ),
        out_shape=jax.ShapeDtypeStruct((rows, columns), jnp.bfloat16),
        compiler_params=pltpu.CompilerParams(vmem_limit_bytes=VMEM_LIMIT),
        cost_estimate=pl.CostEstimate(
            flops=2 * depth * rows * columns,
            bytes_accessed=2 * (depth * (rows + columns) + rows * columns),
            transcendentals=0,
        ),
    )(blocks, normed, grad)


def unpack_kernel(places, got, sums, weight, gain, shift, grad, gain_grad, shift_grad):
    by_gain = jnp.zeros(gain.shape, jnp.float32)
    by_shift = jnp.zeros(gain.shape, jnp.float32)
    for slot, start, at, many in places:
        terms = got[slot, :, start : start + many].astype(jnp.float32)
        total = sums[slot : slot + 1, start : start + many]
        parts = weight[:, at : at + many].astype(jnp.float32)
        grad[:, at : at + many] = terms * gain[...] + total * shift[...]
        by_gain += jnp.sum(parts * terms, axis=1, keepdims=True)
        by_shift += jnp.sum(parts * total, axis=1, keepdims=True)
    gain_grad[...] = by_gain
    shift_grad[...] = by_shift


def unpack(places, got, sums, weight, gain, shift):
    rows, columns = weight.shape
    gain = gain.astype(jnp.float32).reshape(rows, 1)
    shift = shift.astype(jnp.float32).reshape(rows, 1)
    grad, gain_grad, shift_grad = pl.pallas_call(
        lambda *refs: unpack_kernel(places, *refs),
        out_shape=[
            jax.ShapeDtypeStruct((rows, columns), jnp.float32),
            jax.ShapeDtypeStruct((rows, 1), jnp.float32),
            jax.ShapeDtypeStruct((rows, 1), jnp.float32),
        ],
        compiler_params=pltpu.CompilerParams(vmem_limit_bytes=VMEM_LIMIT),
    )(got, sums, weight, gain, shift)
    return grad, gain_grad.reshape(rows), shift_grad.reshape(rows)


def per_device(
    plan,
    tokens,
    seq_lengths,
    ln1_gain,
    ln1_bias,
    ln2_gain,
    ln2_bias,
    qkv_weight,
    qkv_bias,
    dense_weight,
    dense_bias,
    expand_weight,
    expand_bias,
    contract_weight,
    contract_bias,
    cotangent,
):
    slots, width = tokens.shape
    rows = qkv_weight.shape[0]
    units = contract_weight.shape[0]
    count, groups = plan.count, plan.groups
    head_dim = width // HEADS
    rotated = head_dim // 4
    hidden_units = groups * units
    shared = HEADS * slots
    me = lax.axis_index("dp")
    inner_groups = plan.inner_groups()
    slot = sum(bit_of(me, bit) << place for place, bit in enumerate(reversed(plan.inner)))

    group_tokens = lax.all_gather(tokens, "dp", axis=0, tiled=True, axis_index_groups=inner_groups)
    group_cotangent = lax.all_gather(
        cotangent, "dp", axis=0, tiled=True, axis_index_groups=inner_groups
    )

    parts = [
        ln1_gain,
        ln1_bias,
        ln2_gain,
        ln2_bias,
        dense_bias,
        contract_bias,
        qkv_bias,
        expand_bias,
        seq_lengths[0].astype(jnp.bfloat16),
    ]
    sizes = [item.shape[0] for item in parts]
    total = sum(sizes)
    lines = -(-total // 1024) * 8
    small = jnp.concatenate(parts + [jnp.zeros((lines * 128 - total,), jnp.bfloat16)])
    every = gather_small(small.reshape(1, lines, 128), plan.order, me, plan)
    every = every.reshape(count, lines * 128).astype(jnp.float32)
    taken, at = [], 0
    for size in sizes:
        taken.append(every[:, at : at + size])
        at += size
    gain_one, shift_one, gain_two, shift_two, bias_dense, bias_contract = [
        item.reshape(1, width) for item in taken[:6]
    ]
    bias_qkv = lax.dynamic_index_in_dim(
        taken[6].reshape(3, HEADS, head_dim), slot, 1, keepdims=False
    ).reshape(1, 3 * head_dim)

    def fixed(value, bits):
        rest = value.shape[1:]
        value = value.reshape((2,) * plan.bits + rest)
        for place, bit in enumerate(plan.order):
            if bit in bits:
                value = lax.dynamic_slice_in_dim(value, bit_of(me, bit), 1, place)
        return value

    bias_expand = fixed(taken[7], plan.inner)
    kept = [bit for bit in plan.order if bit in plan.outer]
    bias_expand = bias_expand.reshape((2,) * len(kept) + (units,))
    bias_expand = bias_expand.transpose([kept.index(b) for b in plan.outer] + [len(kept)])
    bias_expand = bias_expand.reshape(1, hidden_units)
    lengths = fixed(taken[8], plan.outer).reshape(HEADS, -1).astype(jnp.int32)

    expand_places = [
        (s, group * units, plan.device(group, s) * units, units)
        for s in range(HEADS)
        for group in range(groups)
    ]
    qkv_places = [
        (s, part * head_dim, part * width + s * head_dim, head_dim)
        for s in range(HEADS)
        for part in range(3)
    ]

    def to_slots(weight, places):
        own = [
            jnp.concatenate(
                [weight[:, at : at + many] for s, _, at, many in places if s == which], axis=1
            )
            for which in range(HEADS)
        ]
        sent = jnp.stack(own)
        got = lax.all_to_all(sent, "dp", 0, 0, tiled=True, axis_index_groups=inner_groups)
        return place_all(gather_outer(got, plan), me, plan).reshape(width, -1)

    weight_expand = to_slots(expand_weight, expand_places)
    weight_qkv = to_slots(qkv_weight, qkv_places)

    to_slot = [(d, plan.device(d % groups, d // groups)) for d in range(count)]
    from_slot = [(target, source) for source, target in to_slot]
    weight_contract = place_outer(gather_outer(contract_weight, plan), me, plan)
    weight_contract = weight_contract.reshape(hidden_units, width)
    dense_part = lax.ppermute(dense_weight, "dp", to_slot)
    weight_dense = place_outer(gather_outer(dense_part, plan), me, plan)
    weight_dense = weight_dense.reshape(head_dim, width)

    segment, position = jax.vmap(lambda item: slot_layout(item, slots))(lengths)
    cosine, sine = rotary_tables(position.reshape(-1), rotated, head_dim // 2)
    normed, _ = norm_terms(group_tokens.astype(jnp.float32))
    low_one = (normed * gain_one + shift_one).astype(jnp.bfloat16)
    low_two = (normed * gain_two + shift_two).astype(jnp.bfloat16)
    low_normed = normed.astype(jnp.bfloat16)
    active, slope = over_blocks(
        expand_kernel,
        slots,
        [low_two],
        [weight_expand, bias_expand],
        [(hidden_units, jnp.bfloat16), (hidden_units, jnp.float32)],
        2 * shared * width * hidden_units,
    )
    (qkv,) = over_blocks(
        lambda *refs: qkv_kernel(head_dim, *refs),
        slots,
        [low_one, cosine, sine],
        [weight_qkv, bias_qkv],
        [(3 * head_dim, jnp.bfloat16)],
        2 * shared * width * 3 * head_dim,
    )

    first = bit_of(me, plan.outer[0])

    def reduce_output(left, width_of):
        def half_of(which):
            columns = left.shape[1] // 2
            taken = lax.dynamic_slice_in_dim(left, which * columns, columns, 1)
            terms = times_leading(taken, group_cotangent).astype(jnp.bfloat16)
            return terms.reshape(groups // 2, width_of, width)

        sent = swap(half_of(1 - first), plan.outer[0], plan)
        return reduce_rest(half_of(first), sent, me, plan)

    contract_weight_grad = reduce_output(active, units)

    (grad_hidden,) = over_blocks(
        grad_hidden_kernel,
        slots,
        [group_cotangent, slope],
        [weight_contract],
        [(hidden_units, jnp.bfloat16)],
        2 * shared * width * hidden_units,
    )

    block = 256
    numbers = jnp.arange(width // block // 2, dtype=jnp.int32)
    reach = (rows << plan.outer[0]) // block

    def reduce_input(grad):
        def half_of(which):
            blocks = (numbers // reach) * (2 * reach) + which * reach + numbers % reach
            terms = input_terms(low_normed, grad, blocks, block)
            return terms.reshape(groups // 2, HEADS * rows, grad.shape[1])

        sent = swap(half_of(1 - first), plan.outer[0], plan)
        reduced = reduce_rest(half_of(first), sent, me, plan)
        reduced = reduced.reshape(HEADS, rows, -1).astype(jnp.bfloat16)
        return lax.all_to_all(reduced, "dp", 0, 0, tiled=True, axis_index_groups=inner_groups)

    expand_got = reduce_input(grad_hidden)

    attn, grad_qkv = over_blocks(
        lambda *refs: attend_kernel(head_dim, *refs),
        slots,
        [qkv, group_cotangent, cosine, sine, segment.reshape(-1, 1)],
        [weight_dense, segment],
        [(head_dim, jnp.bfloat16), (3 * head_dim, jnp.bfloat16)],
        2 * shared * head_dim * (width + 7 * slots),
    )
    qkv_got = reduce_input(grad_qkv)
    dense_weight_grad = reduce_output(attn, rows)
    dense_weight_grad = lax.ppermute(
        dense_weight_grad.astype(jnp.bfloat16), "dp", from_slot
    ).astype(jnp.float32)

    sums = jnp.concatenate(
        [
            jnp.sum(grad_qkv.astype(jnp.float32), axis=0),
            jnp.sum(grad_hidden.astype(jnp.float32), axis=0),
            jnp.sum(group_cotangent.astype(jnp.float32), axis=0),
        ]
    ).reshape(-1, 128)
    for bit in plan.outer:
        sums = sums + swap(sums, bit, plan)
    own_sums = 3 * head_dim + hidden_units
    bias_out_grad = lax.dynamic_slice_in_dim(
        sums.reshape(-1), own_sums + me * (width // count), width // count
    )
    all_sums = gather_small(sums[None, : own_sums // 128], plan.inner, me, plan)
    all_sums = all_sums.reshape(HEADS, own_sums)
    qkv_sums, expand_sums = all_sums[:, : 3 * head_dim], all_sums[:, 3 * head_dim :]

    (branch,) = over_blocks(
        branch_kernel,
        slots,
        [attn, active],
        [weight_dense, weight_contract],
        [(width, jnp.bfloat16)],
        2 * shared * width * (head_dim + hidden_units),
    )
    branch = lax.psum_scatter(
        branch, "dp", scatter_dimension=0, tiled=True, axis_index_groups=inner_groups
    )
    inputs = tokens.astype(jnp.float32)
    layer_out = (inputs + branch.astype(jnp.float32) + bias_dense + bias_contract).astype(
        jnp.bfloat16
    )

    (grad_both,) = over_blocks(
        grad_norm_kernel,
        slots,
        [grad_qkv, grad_hidden],
        [weight_qkv, weight_expand, gain_one, gain_two],
        [(width, jnp.bfloat16)],
        2 * shared * width * (3 * head_dim + hidden_units),
    )
    grad_both = lax.psum_scatter(
        grad_both, "dp", scatter_dimension=0, tiled=True, axis_index_groups=inner_groups
    ).astype(jnp.float32)
    own_normed, own_scale = norm_terms(inputs)
    input_grad = (
        cotangent.astype(jnp.float32)
        + (
            grad_both
            - jnp.mean(grad_both, axis=1, keepdims=True)
            - own_normed * jnp.mean(grad_both * own_normed, axis=1, keepdims=True)
        )
        * own_scale
    )

    qkv_weight_grad, ln1_gain_grad, ln1_bias_grad = unpack(
        qkv_places, qkv_got, qkv_sums, qkv_weight, ln1_gain, ln1_bias
    )
    expand_weight_grad, ln2_gain_grad, ln2_bias_grad = unpack(
        expand_places, expand_got, expand_sums, expand_weight, ln2_gain, ln2_bias
    )
    qkv_bias_grad = qkv_sums.reshape(HEADS, 3, head_dim).transpose(1, 0, 2).reshape(3 * width)
    per = qkv_bias.shape[0]
    qkv_bias_grad = lax.dynamic_slice_in_dim(qkv_bias_grad, me * per, per)
    group = sum(bit_of(me, bit) << place for place, bit in enumerate(reversed(plan.outer)))
    expand_bias_grad = lax.dynamic_slice(expand_sums, (slot, group * units), (1, units))
    return (
        layer_out,
        input_grad,
        ln1_gain_grad,
        ln1_bias_grad,
        ln2_gain_grad,
        ln2_bias_grad,
        qkv_weight_grad,
        qkv_bias_grad,
        dense_weight_grad,
        bias_out_grad,
        expand_weight_grad,
        expand_bias_grad.reshape(units),
        contract_weight_grad,
        bias_out_grad,
    )


def solution(mesh):
    in_specs = (
        P("dp", None),
        P("dp", None),
        P("dp"),
        P("dp"),
        P("dp"),
        P("dp"),
        P("dp", None),
        P("dp"),
        P("dp", None),
        P("dp"),
        P("dp", None),
        P("dp"),
        P("dp", None),
        P("dp"),
        P("dp", None),
    )
    out_specs = (
        P("dp", None),
        P("dp", None),
        P("dp"),
        P("dp"),
        P("dp"),
        P("dp"),
        P("dp", None),
        P("dp"),
        P("dp", None),
        P("dp"),
        P("dp", None),
        P("dp"),
        P("dp", None),
        P("dp"),
    )
    plan = Plan(mesh.shape["dp"])

    def layer(*arrays):
        return per_device(plan, *arrays)

    return jax.shard_map(layer, mesh=mesh, in_specs=in_specs, out_specs=out_specs, check_vma=False)
```

```python
import math

import jax
import jax.numpy as jnp
from jax import lax
from jax.experimental import pallas as pl
from jax.experimental.pallas import tpu as pltpu
from jax.sharding import PartitionSpec as P


HEADS = 8

EPSILON = 1e-05
MASKED = -1e30
PAIRED = (((1,), (1,)), ((), ()))
LEADING = (((0,), (0,)), ((), ()))
VMEM_LIMIT = 60 * 2**20
ORDER = (0, 2, 4, 6, 1, 3, 5, 7)
BRIEF = pl.CostEstimate(flops=1, bytes_accessed=1, transcendentals=0)


class Plan:
    def __init__(self, count):
        self.count = count
        self.bits = count.bit_length() - 1
        self.groups = count // HEADS

    def device(self, group, slot):
        return group * HEADS + slot

    def sharing(self):
        return [[self.device(g, s) for s in range(HEADS)] for g in range(self.groups)]

    def across(self):
        return [[self.device(g, s) for g in range(self.groups)] for s in range(HEADS)]

    def flip(self, bit):
        return [(d, d ^ (1 << bit)) for d in range(self.count)]


def swap(value, bit, plan):
    return lax.ppermute(value, "dp", plan.flip(bit))


def gather_small(value, bits, me, plan):
    rest = value.shape
    order = sorted(bits, reverse=True)
    value = value.reshape((1,) * len(bits) + rest)
    for bit in bits:
        got = swap(value, bit, plan)
        place = order.index(bit)
        value = jnp.where(
            (me >> bit) & 1 == 0,
            jnp.concatenate([value, got], axis=place),
            jnp.concatenate([got, value], axis=place),
        )
    return value.reshape((-1,) + rest)


def gather_tokens(value, plan, last):
    pieces = {0: value}
    for bit in (1, 2):
        pieces[1 << bit] = swap(value, bit, plan)
    pieces[6] = swap(pieces[1 << (3 - last)], last, plan)
    for mask in (0, 2, 4, 6):
        pieces[mask | 1] = swap(pieces[mask], 0, plan)
    return jnp.concatenate([pieces[mask] for mask in ORDER])


class Chain:
    def __init__(self):
        self.waits = []

    def settle(self, *values):
        self.waits += values

    def launch(self, kernel, inputs, in_specs, outs, out_specs, grid=(1,), prefetch=(), **options):
        known = len(prefetch) + len(inputs)
        waits = self.waits

        def body(*refs):
            kernel(*refs[:known], *refs[known + len(waits) :])

        made = pl.pallas_call(
            body,
            grid_spec=pltpu.PrefetchScalarGridSpec(
                num_scalar_prefetch=len(prefetch),
                grid=grid,
                in_specs=in_specs + [pl.BlockSpec(memory_space=pl.ANY)] * len(waits),
                out_specs=out_specs,
                **options,
            ),
            out_shape=[jax.ShapeDtypeStruct(shape, kind) for shape, kind in outs],
            compiler_params=pltpu.CompilerParams(vmem_limit_bytes=VMEM_LIMIT),
            cost_estimate=BRIEF,
        )(*prefetch, *inputs, *waits)
        self.waits = [made[0]]
        return made


def whole(item):
    return pl.BlockSpec(item.shape, lambda i, *_: (0,) * len(item.shape))


def slot_layout(lengths, slots):
    place = jnp.arange(slots, dtype=jnp.int32)
    ends = jnp.cumsum(lengths, dtype=jnp.int32)
    after = (place[:, None] >= ends[None, :]).astype(jnp.int32)
    segment = jnp.sum(after, axis=1, dtype=jnp.int32)
    offset = jnp.sum(after * lengths[None, :], axis=1, dtype=jnp.int32)
    return (segment, place - offset)


def rotary_tables(position, rotated, lanes):
    half = rotated // 2
    ladder = jnp.arange(half, dtype=jnp.float32) * (-math.log(10000.0) / half)
    angle = position.astype(jnp.float32)[:, None] * jnp.exp(ladder)[None, :]
    cosine, sine = jnp.cos(angle), jnp.sin(angle)
    rest = (position.shape[0], lanes - rotated)
    return (
        jnp.concatenate([cosine, cosine, jnp.ones(rest, jnp.float32)], axis=1),
        jnp.concatenate([-sine, sine, jnp.zeros(rest, jnp.float32)], axis=1),
    )


def norm_terms(value):
    centre = jnp.mean(value, axis=1, keepdims=True)
    spread = value - centre
    variance = jnp.mean(spread * spread, axis=1, keepdims=True)
    scale = lax.rsqrt(variance + EPSILON)
    return (spread * scale, scale)


def times(left, right):
    return jnp.dot(left, right, preferred_element_type=jnp.float32)


def times_leading(left, right):
    return lax.dot_general(left, right, LEADING, preferred_element_type=jnp.float32)


def times_paired(left, right):
    return lax.dot_general(left, right, PAIRED, preferred_element_type=jnp.float32)


def over_blocks(chain, kernel, slots, blocked, known, outs, sums=(), rows=None):
    count = blocked[0].shape[0] // slots
    gathered, runs = rows or (None, [])
    extra = [gathered] if runs else []

    def body(*refs):
        given = len(blocked) + len(known)
        if not runs:
            kernel(*refs)
            return
        weight = refs[-1]

        @pl.when(pl.program_id(0) == 0)
        def _():
            place = 0
            for start, many in runs:
                weight[place : place + many, :] = refs[given][start : start + many, :]
                place += many

        kernel(*refs[:given], weight, *refs[given + 1 : -1])

    def moving(width):
        return pl.BlockSpec((slots, width), lambda i: (i, 0))

    shapes = [((count * slots, width), kind) for width, kind in outs]
    shapes += [((1, width), jnp.float32) for width in sums]
    specs = [moving(width) for width, _ in outs]
    specs += [pl.BlockSpec((1, width), lambda i: (0, 0)) for width in sums]
    if runs:
        shape = (sum(many for _, many in runs), gathered.shape[1])
        shapes.append((shape, jnp.bfloat16))
        specs.append(pl.BlockSpec(shape, lambda i: (0, 0)))
    return chain.launch(
        body,
        [*blocked, *known, *extra],
        [moving(item.shape[1]) for item in blocked]
        + [whole(item) for item in known]
        + [
            pl.BlockSpec(item.shape, lambda i: (0, 0), pipeline_mode=pl.Buffered(1))
            for item in extra
        ],
        shapes,
        specs,
        (count,),
    )


def add_columns(out, value):
    total = jnp.sum(value.astype(jnp.float32), axis=0, keepdims=True)
    block = pl.program_id(0)

    @pl.when(block == 0)
    def _():
        out[...] = total

    @pl.when(block > 0)
    def _():
        out[...] += total


def terms_of(chain, compute, slots, width, place, blocked, known, added, split):
    extra = [] if added is None else [added]

    def kernel(*refs):
        values = [ref[...] for ref in refs[: len(blocked) + len(known)]]
        total = compute(*values)
        if extra:
            total += refs[len(values)][...].astype(jnp.float32)
        outs = refs[len(values) + len(extra) :]
        if not split:
            outs[0][...] = total.astype(jnp.bfloat16)
            return
        for step, out in enumerate(outs):

            @pl.when(pl.program_id(0) == step)
            def _(out=out):
                out[...] = total.astype(jnp.bfloat16)

    outs = 4 if split else 1
    shape = (slots if split else 4 * slots, width)
    return chain.launch(
        kernel,
        [*blocked, *known, *extra],
        [pl.BlockSpec((slots, item.shape[1]), lambda i: (i + 4 * place, 0)) for item in blocked]
        + [whole(item) for item in known]
        + [pl.BlockSpec((slots, width), lambda i: (i, 0)) for _ in extra],
        [(shape, jnp.bfloat16)] * outs,
        [pl.BlockSpec((slots, width), lambda i: (0 if split else i, 0)) for _ in range(outs)],
        (4,),
    )


def join(chain, one, two, kind):
    rows, width = one.shape
    tile = rows // 2 if rows % 32 == 0 else rows

    def kernel(one, two, out):
        out[...] = (one[...].astype(jnp.float32) + two[...].astype(jnp.float32)).astype(kind)

    spec = pl.BlockSpec((tile, width), lambda i: (i, 0))
    return chain.launch(
        kernel, [one, two], [spec, spec], [((rows, width), kind)], [spec], (rows // tile,)
    )[0]


def split_output(chain, reduced, units, rows):
    width = reduced.shape[1]

    def kernel(reduced, contract, dense):
        contract[...] = reduced[:units].astype(jnp.float32)
        dense[...] = reduced[units:]

    shapes = [(units, width), (rows, width)]
    return chain.launch(
        kernel,
        [reduced],
        [whole(reduced)],
        list(zip(shapes, [jnp.float32, jnp.bfloat16])),
        [pl.BlockSpec(shape, lambda i: (0, 0)) for shape in shapes],
    )


def finish_input(chain, cotangent, tokens, own, one, two):
    slots, width = tokens.shape
    tile = slots // 4

    def kernel(cotangent, tokens, own, one, two, out):
        normed, scale = norm_terms(tokens[...].astype(jnp.float32))
        grad = own[...].astype(jnp.float32) + one[...].astype(jnp.float32)
        grad += two[...].astype(jnp.float32)
        along = jnp.mean(grad * normed, axis=1, keepdims=True)
        grad = grad - jnp.mean(grad, axis=1, keepdims=True) - normed * along
        out[...] = cotangent[...].astype(jnp.float32) + grad * scale

    spec = pl.BlockSpec((tile, width), lambda i: (i, 0))
    return chain.launch(
        kernel,
        [cotangent, tokens, own, one, two],
        [spec] * 5,
        [((slots, width), jnp.float32)],
        [spec],
        (slots // tile,),
    )[0]


def finish_output(chain, tokens, own, one, two, bias_one, bias_two):
    slots, width = tokens.shape
    tile = slots // 4

    def kernel(tokens, own, one, two, bias_one, bias_two, out):
        total = tokens[...].astype(jnp.float32) + own[...].astype(jnp.float32)
        total += one[...].astype(jnp.float32) + two[...].astype(jnp.float32)
        out[...] = (total + bias_one[...] + bias_two[...]).astype(jnp.bfloat16)

    spec = pl.BlockSpec((tile, width), lambda i: (i, 0))
    return chain.launch(
        kernel,
        [tokens, own, one, two, bias_one, bias_two],
        [spec] * 4 + [whole(bias_one), whole(bias_two)],
        [((slots, width), jnp.bfloat16)],
        [spec],
        (slots // tile,),
    )[0]


def norm_kernel(rows, out):
    out[...] = norm_terms(rows[...].astype(jnp.float32))[0].astype(jnp.bfloat16)


def scaled(normed, gain, shift):
    return (normed[...].astype(jnp.float32) * gain[...] + shift[...]).astype(jnp.bfloat16)


def turn(value, cosine, sine, half):
    lane = lax.broadcasted_iota(jnp.int32, value.shape, 1)
    lanes = value.shape[1]
    swapped = jnp.where(
        lane < half, pltpu.roll(value, lanes - half, 1), pltpu.roll(value, half, 1)
    )
    return value * cosine + swapped * sine


def turn_into(out, at, value, cosine, sine, half):
    lanes = cosine.shape[1]
    turned = turn(value[:, :lanes], cosine, sine, half)
    out[:, at : at + lanes] = turned.astype(jnp.bfloat16)
    out[:, at + lanes : at + value.shape[1]] = value[:, lanes:].astype(jnp.bfloat16)


def qkv_kernel(head_dim, normed, cosine, sine, gain, shift, bias, weight, out):
    projected = times(scaled(normed, gain, shift), weight[...]) + bias[...]
    half = head_dim // 8
    for part in range(2):
        at = part * head_dim
        turn_into(out, at, projected[:, at : at + head_dim], cosine[...], sine[...], half)
    out[:, 2 * head_dim :] = projected[:, 2 * head_dim :].astype(jnp.bfloat16)


def expand_kernel(normed, gain, shift, bias, weight, active, slope):
    hidden = times(scaled(normed, gain, shift), weight[...]) + bias[...]
    below = 0.5 * (1.0 + lax.erf(hidden * math.sqrt(0.5)))
    density = jnp.exp(-0.5 * hidden * hidden) * (1.0 / math.sqrt(2.0 * math.pi))
    active[...] = (hidden * below).astype(jnp.bfloat16)
    slope[...] = below + hidden * density


def grad_hidden_kernel(cotangent, slope, weight, out, out_sum, cotangent_sum):
    grad = (times_paired(cotangent[...], weight[...]) * slope[...]).astype(jnp.bfloat16)
    out[...] = grad
    add_columns(out_sum, grad)
    add_columns(cotangent_sum, cotangent[...])


def branch_terms(attn, active, dense, contract):
    return times(attn, dense) + times(active, contract)


def norm_grad_terms(grad_qkv, grad_hidden, qkv, expand, gain_one, gain_two):
    return times_paired(grad_qkv, qkv) * gain_one + times_paired(grad_hidden, expand) * gain_two


def attend_kernel(
    head_dim, qkv, cotangent, cosine, sine, segment, segments, dense, attn, grad_qkv, grad_sum
):
    scale = 1.0 / math.sqrt(head_dim)
    query = qkv[:, :head_dim]
    key = qkv[:, head_dim : 2 * head_dim]
    value = qkv[:, 2 * head_dim :]
    grad_attn = times_paired(cotangent[...], dense[...]).astype(jnp.bfloat16)
    slots = query.shape[0]
    row = lax.broadcasted_iota(jnp.int32, (slots, slots), 0)
    column = lax.broadcasted_iota(jnp.int32, (slots, slots), 1)
    block = pl.program_id(0)
    allowed = (segment[...] == segments[pl.ds(block, 1), :]) & (column <= row)
    masked = jnp.where(allowed, times_paired(query, key) * scale, MASKED)
    raised = jnp.exp(masked - jnp.max(masked, axis=1, keepdims=True))
    weights = raised / jnp.sum(raised, axis=1, keepdims=True)
    probs = weights.astype(jnp.bfloat16)
    attn[...] = times(probs, value).astype(jnp.bfloat16)
    grad_probs = times_paired(grad_attn, value)
    grad_value = times_leading(probs, grad_attn)
    inner = jnp.sum(weights * grad_probs, axis=1, keepdims=True)
    grad_score = (weights * (grad_probs - inner)).astype(jnp.bfloat16)
    half = head_dim // 8
    back = -sine[...]
    grad_query = times(grad_score, key) * scale
    turn_into(grad_qkv, 0, grad_query, cosine[...], back, half)
    grad_key = times_leading(grad_score, query) * scale
    turn_into(grad_qkv, head_dim, grad_key, cosine[...], back, half)
    grad_qkv[:, 2 * head_dim :] = grad_value.astype(jnp.bfloat16)
    add_columns(grad_sum, grad_qkv[...])


def input_terms(chain, normed, grad):
    depth, width = normed.shape
    columns = grad.shape[1]
    block = 256

    def kernel(left, right, out):
        out[...] = times_leading(left[...], right[...]).astype(jnp.bfloat16)

    return chain.launch(
        kernel,
        [normed, grad],
        [
            pl.BlockSpec((depth, block), lambda i: (0, i)),
            pl.BlockSpec((depth, columns), lambda i: (0, 0), pipeline_mode=pl.Buffered(1)),
        ],
        [((width, columns), jnp.bfloat16)],
        [pl.BlockSpec((block, columns), lambda i: (i, 0))],
        (width // block,),
    )[0]


def output_terms(chain, active, attn, groups, right):
    depth, width = right.shape
    tile = width // 4
    lefts = [active, attn]
    own = [item.shape[1] // groups for item in lefts]
    stride = sum(own)

    def kernel(active, attn, right, out):
        before = 0
        for left, many in zip((active, attn), own):
            terms = times_leading(left[...], right[...]).astype(jnp.bfloat16)
            for group in range(groups):
                at = group * stride + before
                out[at : at + many, :] = terms[group * many : (group + 1) * many]
            before = many

    return chain.launch(
        kernel,
        [active, attn, right],
        [
            pl.BlockSpec(item.shape, lambda i: (0, 0), pipeline_mode=pl.Buffered(1))
            for item in lefts
        ]
        + [pl.BlockSpec((depth, tile), lambda i: (0, i))],
        [((groups * stride, width), jnp.bfloat16)],
        [pl.BlockSpec((groups * stride, tile), lambda i: (0, i))],
        (width // tile,),
    )[0]


def pack(chain, arrays, moves, columns):
    rows = arrays[0].shape[0]

    def kernel(*refs):
        for slot, at, which, column, many in moves:
            refs[-1][slot, :, at : at + many] = refs[which][:, column : column + many]

    shape = (HEADS, rows, columns)
    return chain.launch(
        kernel,
        arrays,
        [whole(item) for item in arrays],
        [(shape, jnp.bfloat16)],
        [pl.BlockSpec(shape, lambda i: (0, 0, 0))],
    )[0]


def unpack(chain, places, got, sums, weight, gain, shift):
    rows, width = weight.shape
    gain = gain.astype(jnp.float32).reshape(rows, 1)
    shift = shift.astype(jnp.float32).reshape(rows, 1)

    def kernel(got, sums, weight, gain, shift, grad, gain_grad, shift_grad):
        by_gain = jnp.zeros((rows, 1), jnp.float32)
        by_shift = jnp.zeros((rows, 1), jnp.float32)
        for slot, start, at, many in places:
            terms = got[slot, :, start : start + many].astype(jnp.float32)
            total = sums[slot : slot + 1, start : start + many]
            parts = weight[:, at : at + many].astype(jnp.float32)
            grad[:, at : at + many] = terms * gain[...] + total * shift[...]
            by_gain += jnp.sum(parts * terms, axis=1, keepdims=True)
            by_shift += jnp.sum(parts * total, axis=1, keepdims=True)
        gain_grad[...] = by_gain
        shift_grad[...] = by_shift

    inputs = [got, sums, weight, gain, shift]
    shapes = [(rows, width), (rows, 1), (rows, 1)]
    grad, gain_grad, shift_grad = chain.launch(
        kernel,
        inputs,
        [whole(item) for item in inputs],
        [(shape, jnp.float32) for shape in shapes],
        [pl.BlockSpec(shape, lambda i: (0, 0)) for shape in shapes],
    )
    return grad, gain_grad.reshape(rows), shift_grad.reshape(rows)


def per_device(
    plan,
    tokens,
    seq_lengths,
    ln1_gain,
    ln1_bias,
    ln2_gain,
    ln2_bias,
    qkv_weight,
    qkv_bias,
    dense_weight,
    dense_bias,
    expand_weight,
    expand_bias,
    contract_weight,
    contract_bias,
    cotangent,
):
    slots, width = tokens.shape
    rows = qkv_weight.shape[0]
    units = contract_weight.shape[0]
    count, groups = plan.count, plan.groups
    head_dim = width // HEADS
    rotated = head_dim // 4
    hidden_units = groups * units
    me = lax.axis_index("dp")
    slot = me % HEADS
    sharing, across = plan.sharing(), plan.across()
    outer_bits = tuple(range(3, plan.bits))
    chain = Chain()

    def gather(value):
        return lax.all_gather(value, "dp", axis=0, tiled=True, axis_index_groups=across)

    def reduce(value):
        return lax.psum_scatter(
            value, "dp", scatter_dimension=0, tiled=True, axis_index_groups=across
        )

    def exchange(value):
        return lax.all_to_all(value, "dp", 0, 0, tiled=True, axis_index_groups=sharing)

    to_slot = [(d, plan.device(d % groups, d // groups)) for d in range(count)]
    from_slot = [(target, source) for source, target in to_slot]
    dense_part = lax.ppermute(dense_weight, "dp", to_slot)
    weight_out = gather(jnp.concatenate([contract_weight, dense_part]))
    contract_runs = [(group * (units + rows), units) for group in range(groups)]
    dense_runs = [(group * (units + rows) + units, rows) for group in range(groups)]

    expand_places = [
        (s, group * units, plan.device(group, s) * units, units)
        for s in range(HEADS)
        for group in range(groups)
    ]
    qkv_places = [
        (s, part * head_dim, part * width + s * head_dim, head_dim)
        for s in range(HEADS)
        for part in range(3)
    ]
    split = 3 * head_dim
    moves = [(s, at, 0, column, many) for s, at, column, many in qkv_places]
    moves += [(s, split + at, 1, column, many) for s, at, column, many in expand_places]
    own = exchange(pack(chain, [qkv_weight, expand_weight], moves, split + hidden_units))
    own = own.reshape(HEADS * rows, -1)
    weight_qkv = gather(own[:, :split])
    weight_expand = gather(own[:, split:])

    tile = slots // 4
    own_normed = chain.launch(
        norm_kernel,
        [tokens],
        [pl.BlockSpec((tile, width), lambda i: (i, 0))],
        [((slots, width), jnp.bfloat16)],
        [pl.BlockSpec((tile, width), lambda i: (i, 0))],
        (slots // tile,),
    )[0]
    normed = gather_tokens(own_normed, plan, 1)
    group_cotangent = gather_tokens(cotangent, plan, 2)

    parts = [
        ln1_gain,
        ln1_bias,
        ln2_gain,
        ln2_bias,
        dense_bias,
        contract_bias,
        qkv_bias,
        expand_bias,
        seq_lengths[0].astype(jnp.bfloat16),
    ]
    sizes = [item.shape[0] for item in parts]
    lines = -(-sum(sizes) // 1024) * 8
    small = jnp.concatenate(parts + [jnp.zeros((lines * 128 - sum(sizes),), jnp.bfloat16)])
    every = gather_small(small.reshape(lines, 128), outer_bits + (0, 1, 2), me, plan)
    every = every.reshape(count, lines * 128).astype(jnp.float32)
    taken, at = [], 0
    for size in sizes:
        taken.append(every[:, at : at + size])
        at += size
    gain_one, shift_one, gain_two, shift_two, bias_dense, bias_contract = [
        item.reshape(1, width) for item in taken[:6]
    ]
    bias_qkv = lax.dynamic_index_in_dim(
        taken[6].reshape(3, HEADS, head_dim), slot, 1, keepdims=False
    ).reshape(1, split)
    bias_expand = lax.dynamic_index_in_dim(
        taken[7].reshape(groups, HEADS, units), slot, 1, keepdims=False
    ).reshape(1, hidden_units)
    lengths = jnp.concatenate(
        [lax.dynamic_slice_in_dim(taken[8], me ^ mask, 1) for mask in ORDER]
    ).astype(jnp.int32)
    segment, position = jax.vmap(lambda item: slot_layout(item, slots))(lengths)
    cosine, sine = rotary_tables(position.reshape(-1), rotated, head_dim // 2)

    def sum_begin(compute, blocked, known):
        terms = terms_of(chain, compute, slots, width, 1, blocked, known, None, False)[0]
        return swap(terms, 0, plan)

    def sum_next(compute, blocked, known, got, near):
        own, of_x, of_y, of_both = terms_of(
            chain, compute, slots, width, 0, blocked, known, got, True
        )
        of_near, of_far = (of_x, of_y) if near == 1 else (of_y, of_x)
        return own, swap(of_both, near, plan), swap(of_near, near, plan), of_far

    def sum_last(own, from_both, from_near, of_far, near):
        of_far = join(chain, of_far, from_both, jnp.bfloat16)
        return own, from_near, swap(of_far, 3 - near, plan)

    (qkv,) = over_blocks(
        chain,
        lambda *refs: qkv_kernel(head_dim, *refs),
        slots,
        [normed, cosine, sine],
        [gain_one, shift_one, bias_qkv, weight_qkv],
        [(split, jnp.bfloat16)],
    )
    attn, grad_qkv, qkv_sum, weight_dense = over_blocks(
        chain,
        lambda *refs: attend_kernel(head_dim, *refs),
        slots,
        [qkv, group_cotangent, cosine, sine, segment.reshape(-1, 1)],
        [segment],
        [(head_dim, jnp.bfloat16), (split, jnp.bfloat16)],
        [split],
        (weight_out, dense_runs),
    )
    qkv_got = reduce(input_terms(chain, normed, grad_qkv))
    active, slope = over_blocks(
        chain,
        expand_kernel,
        slots,
        [normed],
        [gain_two, shift_two, bias_expand, weight_expand],
        [(hidden_units, jnp.bfloat16), (hidden_units, jnp.float32)],
    )
    output_got = reduce(output_terms(chain, active, attn, groups, group_cotangent))
    grad_hidden, hidden_sum, cotangent_sum, weight_contract = over_blocks(
        chain,
        grad_hidden_kernel,
        slots,
        [group_cotangent, slope],
        [],
        [(hidden_units, jnp.bfloat16)],
        [hidden_units, width],
        (weight_out, contract_runs),
    )
    expand_got = reduce(input_terms(chain, normed, grad_hidden))

    sums = jnp.concatenate([qkv_sum, hidden_sum, cotangent_sum], axis=1).reshape(-1, 128)
    for bit in outer_bits:
        sums = sums + swap(sums, bit, plan)
    own_lines = (split + hidden_units) // 128
    bias_out_grad = lax.dynamic_slice_in_dim(
        sums[own_lines:].reshape(-1), me * (width // count), width // count
    )
    sums = gather_small(sums[:own_lines], (0, 1, 2), me, plan).reshape(HEADS, -1)
    qkv_sums, expand_sums = sums[:, :split], sums[:, split:]

    branch_of = branch_terms, [attn, active], [weight_dense, weight_contract]
    norm_of = (
        norm_grad_terms,
        [grad_qkv, grad_hidden],
        [weight_qkv, weight_expand, gain_one, gain_two],
    )
    branch_got = sum_begin(*branch_of)
    norm_got = sum_begin(*norm_of)
    branch = sum_next(*branch_of, branch_got, 1)
    norm_parts = sum_next(*norm_of, norm_got, 2)
    branch = sum_last(*branch, 1)
    norm_parts = sum_last(*norm_parts, 2)
    layer_out = finish_output(chain, tokens, *branch, bias_dense, bias_contract)
    input_grad = finish_input(chain, cotangent, tokens, *norm_parts)

    qkv_got = exchange(qkv_got.reshape(HEADS, rows, split))
    qkv_weight_grad, ln1_gain_grad, ln1_bias_grad = unpack(
        chain, qkv_places, qkv_got, qkv_sums, qkv_weight, ln1_gain, ln1_bias
    )
    contract_weight_grad, dense_grad = split_output(chain, output_got, units, rows)
    dense_weight_grad = lax.ppermute(dense_grad, "dp", from_slot).astype(jnp.float32)
    expand_got = exchange(expand_got.reshape(HEADS, rows, hidden_units))
    expand_weight_grad, ln2_gain_grad, ln2_bias_grad = unpack(
        chain, expand_places, expand_got, expand_sums, expand_weight, ln2_gain, ln2_bias
    )
    qkv_bias_grad = qkv_sums.reshape(HEADS, 3, head_dim).transpose(1, 0, 2).reshape(3 * width)
    per = qkv_bias.shape[0]
    qkv_bias_grad = lax.dynamic_slice_in_dim(qkv_bias_grad, me * per, per)
    expand_bias_grad = lax.dynamic_slice(
        expand_sums, (slot, (me // HEADS) * units), (1, units)
    ).reshape(units)
    return (
        layer_out,
        input_grad,
        ln1_gain_grad,
        ln1_bias_grad,
        ln2_gain_grad,
        ln2_bias_grad,
        qkv_weight_grad,
        qkv_bias_grad,
        dense_weight_grad,
        bias_out_grad,
        expand_weight_grad,
        expand_bias_grad,
        contract_weight_grad,
        bias_out_grad,
    )


def solution(mesh):
    in_specs = (
        P("dp", None),
        P("dp", None),
        P("dp"),
        P("dp"),
        P("dp"),
        P("dp"),
        P("dp", None),
        P("dp"),
        P("dp", None),
        P("dp"),
        P("dp", None),
        P("dp"),
        P("dp", None),
        P("dp"),
        P("dp", None),
    )
    out_specs = (
        P("dp", None),
        P("dp", None),
        P("dp"),
        P("dp"),
        P("dp"),
        P("dp"),
        P("dp", None),
        P("dp"),
        P("dp", None),
        P("dp"),
        P("dp", None),
        P("dp"),
        P("dp", None),
        P("dp"),
    )
    plan = Plan(mesh.shape["dp"])

    def layer(*arrays):
        return per_device(plan, *arrays)

    return jax.shard_map(layer, mesh=mesh, in_specs=in_specs, out_specs=out_specs, check_vma=False)
```

```python
import math

import jax
import jax.numpy as jnp
from jax import lax
from jax.experimental import pallas as pl
from jax.experimental.pallas import tpu as pltpu
from jax.sharding import PartitionSpec as P


HEADS = 8

EPSILON = 1e-05
MASKED = -1e30
PAIRED = (((1,), (1,)), ((), ()))
LEADING = (((0,), (0,)), ((), ()))
VMEM_LIMIT = 60 * 2**20
ORDER = (0, 2, 4, 6, 1, 3, 5, 7)
BRIEF = pl.CostEstimate(flops=1, bytes_accessed=1, transcendentals=0)


class Plan:
    def __init__(self, count):
        self.count = count
        self.bits = count.bit_length() - 1
        self.groups = count // HEADS

    def device(self, group, slot):
        return group * HEADS + slot

    def sharing(self):
        return [[self.device(g, s) for s in range(HEADS)] for g in range(self.groups)]

    def across(self):
        return [[self.device(g, s) for g in range(self.groups)] for s in range(HEADS)]

    def flip(self, bit):
        return [(d, d ^ (1 << bit)) for d in range(self.count)]


def swap(value, bit, plan):
    return lax.ppermute(value, "dp", plan.flip(bit))


def gather_small(value, bits, me, plan):
    rest = value.shape
    order = sorted(bits, reverse=True)
    value = value.reshape((1,) * len(bits) + rest)
    for bit in bits:
        got = swap(value, bit, plan)
        place = order.index(bit)
        value = jnp.where(
            (me >> bit) & 1 == 0,
            jnp.concatenate([value, got], axis=place),
            jnp.concatenate([got, value], axis=place),
        )
    return value.reshape((-1,) + rest)


def own_pieces(value, plan):
    return {0: value, 2: swap(value, 1, plan), 4: swap(value, 2, plan)}


def all_pieces(pieces, passed, bit, plan):
    pieces = dict(pieces)
    pieces[6] = swap(passed, bit, plan)
    for mask in (0, 2, 4, 6):
        pieces[mask | 1] = swap(pieces[mask], 0, plan)
    return [(pieces[mask], 0) for mask in ORDER]


class Chain:
    def __init__(self):
        self.waits = []

    def settle(self, *values):
        self.waits += values

    def launch(self, kernel, inputs, in_specs, outs, out_specs, grid=(1,), prefetch=(), **options):
        known = len(prefetch) + len(inputs)
        waits = self.waits

        def body(*refs):
            kernel(*refs[:known], *refs[known + len(waits) :])

        made = pl.pallas_call(
            body,
            grid_spec=pltpu.PrefetchScalarGridSpec(
                num_scalar_prefetch=len(prefetch),
                grid=grid,
                in_specs=in_specs + [pl.BlockSpec(memory_space=pl.ANY)] * len(waits),
                out_specs=out_specs,
                **options,
            ),
            out_shape=[jax.ShapeDtypeStruct(shape, kind) for shape, kind in outs],
            compiler_params=pltpu.CompilerParams(vmem_limit_bytes=VMEM_LIMIT),
            cost_estimate=BRIEF,
        )(*prefetch, *inputs, *waits)
        self.waits = [made[0]]
        return made


def whole(item):
    return pl.BlockSpec(item.shape, lambda i, *_: (0,) * len(item.shape))


def slot_layout(lengths, slots):
    place = jnp.arange(slots, dtype=jnp.int32)
    ends = jnp.cumsum(lengths, dtype=jnp.int32)
    after = (place[:, None] >= ends[None, :]).astype(jnp.int32)
    segment = jnp.sum(after, axis=1, dtype=jnp.int32)
    offset = jnp.sum(after * lengths[None, :], axis=1, dtype=jnp.int32)
    return (segment, place - offset)


def rotary_tables(position, rotated, lanes):
    half = rotated // 2
    ladder = jnp.arange(half, dtype=jnp.float32) * (-math.log(10000.0) / half)
    angle = position.astype(jnp.float32)[:, None] * jnp.exp(ladder)[None, :]
    cosine, sine = jnp.cos(angle), jnp.sin(angle)
    rest = (position.shape[0], lanes - rotated)
    return (
        jnp.concatenate([cosine, cosine, jnp.ones(rest, jnp.float32)], axis=1),
        jnp.concatenate([-sine, sine, jnp.zeros(rest, jnp.float32)], axis=1),
    )


def norm_terms(value):
    centre = jnp.mean(value, axis=1, keepdims=True)
    spread = value - centre
    variance = jnp.mean(spread * spread, axis=1, keepdims=True)
    scale = lax.rsqrt(variance + EPSILON)
    return (spread * scale, scale)


def times(left, right):
    return jnp.dot(left, right, preferred_element_type=jnp.float32)


def times_leading(left, right):
    return lax.dot_general(left, right, LEADING, preferred_element_type=jnp.float32)


def times_paired(left, right):
    return lax.dot_general(left, right, PAIRED, preferred_element_type=jnp.float32)


def over_blocks(chain, kernel, slots, pieces, blocked, known, outs, sums=(), rows=None):
    count = HEADS
    gathered, runs = rows or (None, [])
    extra = [gathered] if runs else []

    def body(*refs):
        refs = list(refs)
        if pieces:
            held = refs.pop()
            for step, piece in enumerate(refs[: len(pieces)]):

                @pl.when(pl.program_id(0) == step)
                def _(piece=piece):
                    held[...] = piece[...]

            refs = [held] + refs[len(pieces) :]
        given = bool(pieces) + len(blocked) + len(known)
        if not runs:
            kernel(*refs)
            return
        weight = refs[-1]

        @pl.when(pl.program_id(0) == 0)
        def _():
            place = 0
            for start, many in runs:
                weight[place : place + many, :] = refs[given][start : start + many, :]
                place += many

        kernel(*refs[:given], weight, *refs[given + 1 : -1])

    def moving(width):
        return pl.BlockSpec((slots, width), lambda i: (i, 0))

    shapes = [((count * slots, width), kind) for width, kind in outs]
    shapes += [((1, width), jnp.float32) for width in sums]
    specs = [moving(width) for width, _ in outs]
    specs += [pl.BlockSpec((1, width), lambda i: (0, 0)) for width in sums]
    if runs:
        shape = (sum(many for _, many in runs), gathered.shape[1])
        shapes.append((shape, jnp.bfloat16))
        specs.append(pl.BlockSpec(shape, lambda i: (0, 0)))
    def once(item):
        return pl.BlockSpec(item.shape, lambda i: (0, 0), pipeline_mode=pl.Buffered(1))

    options = {}
    if pieces:
        item = pieces[0][0]
        options["scratch_shapes"] = [pltpu.VMEM((slots, item.shape[1]), item.dtype)]
    return chain.launch(
        body,
        [*[item for item, _ in pieces], *blocked, *known, *extra],
        [
            pl.BlockSpec(
                (slots, item.shape[1]),
                lambda i, place=place: (place, 0),
                pipeline_mode=pl.Buffered(1),
            )
            for item, place in pieces
        ]
        + [moving(item.shape[1]) for item in blocked]
        + [whole(item) for item in known]
        + [once(item) for item in extra],
        shapes,
        specs,
        (count,),
        **options,
    )


def add_columns(out, value):
    total = jnp.sum(value.astype(jnp.float32), axis=0, keepdims=True)
    block = pl.program_id(0)

    @pl.when(block == 0)
    def _():
        out[...] = total

    @pl.when(block > 0)
    def _():
        out[...] += total


def terms_of(chain, compute, slots, width, place, blocked, known, added, split):
    extra = [] if added is None else [added]

    def kernel(*refs):
        values = [ref[...] for ref in refs[: len(blocked) + len(known)]]
        total = compute(*values)
        if extra:
            total += refs[len(values)][...].astype(jnp.float32)
        outs = refs[len(values) + len(extra) :]
        if not split:
            outs[0][...] = total.astype(jnp.bfloat16)
            return
        for step, out in enumerate(outs[:3]):

            @pl.when(pl.program_id(0) == step)
            def _(out=out):
                out[...] = total.astype(jnp.bfloat16)

        @pl.when(pl.program_id(0) == 3)
        def _():
            outs[3][...] = total[:, : width // 2].astype(jnp.bfloat16)
            outs[4][...] = total[:, width // 2 :].astype(jnp.bfloat16)

    if split:
        shapes = [(slots, width)] * 3 + [(slots, width // 2)] * 2
    else:
        shapes = [(4 * slots, width)]
    return chain.launch(
        kernel,
        [*blocked, *known, *extra],
        [pl.BlockSpec((slots, item.shape[1]), lambda i: (i + 4 * place, 0)) for item in blocked]
        + [whole(item) for item in known]
        + [pl.BlockSpec((slots, width), lambda i: (i, 0)) for _ in extra],
        [(shape, jnp.bfloat16) for shape in shapes],
        [pl.BlockSpec((slots, shape[1]), lambda i: (0 if split else i, 0)) for shape in shapes],
        (4,),
    )


def pass_terms(chain, of_x, of_y, left, right):
    rows, width = of_x.shape
    half = width // 2

    def add(one, two):
        return (one.astype(jnp.float32) + two.astype(jnp.float32)).astype(jnp.bfloat16)

    def kernel(of_x, of_y, left, right, to_x, to_y):
        to_x[:, :half] = of_x[:, :half]
        to_x[:, half:] = add(of_x[:, half:], right[...])
        to_y[:, :half] = add(of_y[:, :half], left[...])
        to_y[:, half:] = of_y[:, half:]

    tile = rows // 2

    def spec(columns):
        return pl.BlockSpec((tile, columns), lambda i: (i, 0))

    return chain.launch(
        kernel,
        [of_x, of_y, left, right],
        [spec(width), spec(width), spec(half), spec(half)],
        [((rows, width), jnp.bfloat16)] * 2,
        [spec(width)] * 2,
        (2,),
    )


def split_output(chain, reduced, units, rows):
    width = reduced.shape[1]

    def kernel(reduced, contract, dense):
        contract[...] = reduced[:units].astype(jnp.float32)
        dense[...] = reduced[units:]

    shapes = [(units, width), (rows, width)]
    return chain.launch(
        kernel,
        [reduced],
        [whole(reduced)],
        list(zip(shapes, [jnp.float32, jnp.bfloat16])),
        [pl.BlockSpec(shape, lambda i: (0, 0)) for shape in shapes],
    )


def finish_input(chain, cotangent, tokens, own, one, two):
    slots, width = tokens.shape
    tile = slots // 4

    def kernel(cotangent, tokens, own, one, two, out):
        normed, scale = norm_terms(tokens[...].astype(jnp.float32))
        grad = own[...].astype(jnp.float32) + one[...].astype(jnp.float32)
        grad += two[...].astype(jnp.float32)
        along = jnp.mean(grad * normed, axis=1, keepdims=True)
        grad = grad - jnp.mean(grad, axis=1, keepdims=True) - normed * along
        out[...] = cotangent[...].astype(jnp.float32) + grad * scale

    spec = pl.BlockSpec((tile, width), lambda i: (i, 0))
    return chain.launch(
        kernel,
        [cotangent, tokens, own, one, two],
        [spec] * 5,
        [((slots, width), jnp.float32)],
        [spec],
        (slots // tile,),
    )[0]


def finish_output(chain, tokens, own, one, two, bias_one, bias_two):
    slots, width = tokens.shape
    tile = slots // 4

    def kernel(tokens, own, one, two, bias_one, bias_two, out):
        total = tokens[...].astype(jnp.float32) + own[...].astype(jnp.float32)
        total += one[...].astype(jnp.float32) + two[...].astype(jnp.float32)
        out[...] = (total + bias_one[...] + bias_two[...]).astype(jnp.bfloat16)

    spec = pl.BlockSpec((tile, width), lambda i: (i, 0))
    return chain.launch(
        kernel,
        [tokens, own, one, two, bias_one, bias_two],
        [spec] * 4 + [whole(bias_one), whole(bias_two)],
        [((slots, width), jnp.bfloat16)],
        [spec],
        (slots // tile,),
    )[0]


def split_columns(chain, value, split):
    rows, width = value.shape
    tile = rows // 4

    def kernel(value, one, two):
        one[...] = value[:, :split]
        two[...] = value[:, split:]

    def spec(columns):
        return pl.BlockSpec((tile, columns), lambda i: (i, 0))

    sizes = [split, width - split]
    return chain.launch(
        kernel,
        [value],
        [spec(width)],
        [((rows, size), value.dtype) for size in sizes],
        [spec(size) for size in sizes],
        (4,),
    )


def laid_together(chain, values):
    rows, width = values[0].shape

    def kernel(*refs):
        for step, value in enumerate(refs[:-1]):

            @pl.when(pl.program_id(0) == step)
            def _(value=value):
                refs[-1][...] = value[...]

    return chain.launch(
        kernel,
        values,
        [
            pl.BlockSpec((rows, width), lambda i: (0, 0), pipeline_mode=pl.Buffered(1))
            for _ in values
        ],
        [((len(values) * rows, width), values[0].dtype)],
        [pl.BlockSpec((rows, width), lambda i: (i, 0))],
        (len(values),),
    )[0]


def copied(chain, value):
    def kernel(value, out):
        out[...] = value[...]

    spec = pl.BlockSpec((value.shape[0] // 4, value.shape[1]), lambda i: (i, 0))
    return chain.launch(kernel, [value], [spec], [(value.shape, value.dtype)], [spec], (4,))[0]


def turn(value, cosine, sine, half):
    lane = lax.broadcasted_iota(jnp.int32, value.shape, 1)
    lanes = value.shape[1]
    swapped = jnp.where(
        lane < half, pltpu.roll(value, lanes - half, 1), pltpu.roll(value, half, 1)
    )
    return value * cosine + swapped * sine


def turn_into(out, at, value, cosine, sine, half):
    lanes = cosine.shape[1]
    turned = turn(value[:, :lanes], cosine, sine, half)
    out[:, at : at + lanes] = turned.astype(jnp.bfloat16)
    out[:, at + lanes : at + value.shape[1]] = value[:, lanes:].astype(jnp.bfloat16)


def norm_kernel(tokens, gain_one, shift_one, gain_two, shift_two, low_one, low_two, low):
    normed, _ = norm_terms(tokens[...].astype(jnp.float32))
    low_one[...] = (normed * gain_one[...] + shift_one[...]).astype(jnp.bfloat16)
    low_two[...] = (normed * gain_two[...] + shift_two[...]).astype(jnp.bfloat16)
    low[...] = normed.astype(jnp.bfloat16)


def qkv_kernel(head_dim, x, cosine, sine, bias, weight, out):
    projected = times(x[...], weight[...]) + bias[...]
    half = head_dim // 8
    for part in range(2):
        at = part * head_dim
        turn_into(out, at, projected[:, at : at + head_dim], cosine[...], sine[...], half)
    out[:, 2 * head_dim :] = projected[:, 2 * head_dim :].astype(jnp.bfloat16)


def expand_kernel(x, bias, weight, active, slope):
    hidden = times(x[...], weight[...]) + bias[...]
    below = 0.5 * (1.0 + lax.erf(hidden * math.sqrt(0.5)))
    density = jnp.exp(-0.5 * hidden * hidden) * (1.0 / math.sqrt(2.0 * math.pi))
    active[...] = (hidden * below).astype(jnp.bfloat16)
    slope[...] = below + hidden * density


def grad_hidden_kernel(
    cotangent, slope, weight, out, cotangent_out, out_sum, cotangent_sum
):
    grad = (times_paired(cotangent[...], weight[...]) * slope[...]).astype(jnp.bfloat16)
    out[...] = grad
    add_columns(out_sum, grad)
    add_columns(cotangent_sum, cotangent[...])
    cotangent_out[...] = cotangent[...]


def branch_terms(attn, active, dense, contract):
    return times(attn, dense) + times(active, contract)


def norm_grad_terms(grad_qkv, grad_hidden, qkv, expand, gain_one, gain_two):
    return times_paired(grad_qkv, qkv) * gain_one + times_paired(grad_hidden, expand) * gain_two


def attend_kernel(
    head_dim,
    qkv,
    cotangent,
    cosine,
    sine,
    segment,
    segments,
    dense,
    attn,
    grad_qkv,
    grad_sum,
):
    scale = 1.0 / math.sqrt(head_dim)
    query = qkv[:, :head_dim]
    key = qkv[:, head_dim : 2 * head_dim]
    value = qkv[:, 2 * head_dim :]
    grad_attn = times_paired(cotangent[...], dense[...]).astype(jnp.bfloat16)
    slots = query.shape[0]
    row = lax.broadcasted_iota(jnp.int32, (slots, slots), 0)
    column = lax.broadcasted_iota(jnp.int32, (slots, slots), 1)
    block = pl.program_id(0)
    allowed = (segment[...] == segments[pl.ds(block, 1), :]) & (column <= row)
    masked = jnp.where(allowed, times_paired(query, key) * scale, MASKED)
    raised = jnp.exp(masked - jnp.max(masked, axis=1, keepdims=True))
    weights = raised / jnp.sum(raised, axis=1, keepdims=True)
    probs = weights.astype(jnp.bfloat16)
    attn[...] = times(probs, value).astype(jnp.bfloat16)
    grad_probs = times_paired(grad_attn, value)
    grad_value = times_leading(probs, grad_attn)
    inner = jnp.sum(weights * grad_probs, axis=1, keepdims=True)
    grad_score = (weights * (grad_probs - inner)).astype(jnp.bfloat16)
    half = head_dim // 8
    back = -sine[...]
    grad_query = times(grad_score, key) * scale
    turn_into(grad_qkv, 0, grad_query, cosine[...], back, half)
    grad_key = times_leading(grad_score, query) * scale
    turn_into(grad_qkv, head_dim, grad_key, cosine[...], back, half)
    grad_qkv[:, 2 * head_dim :] = grad_value.astype(jnp.bfloat16)
    add_columns(grad_sum, grad_qkv[...])


def input_terms(chain, normed, grad):
    depth, width = normed.shape
    columns = grad.shape[1]
    block = 256

    def kernel(left, right, out):
        out[...] = times_leading(left[...], right[...]).astype(jnp.bfloat16)

    return chain.launch(
        kernel,
        [normed, grad],
        [
            pl.BlockSpec((depth, block), lambda i: (0, i)),
            pl.BlockSpec((depth, columns), lambda i: (0, 0), pipeline_mode=pl.Buffered(1)),
        ],
        [((width, columns), jnp.bfloat16)],
        [pl.BlockSpec((block, columns), lambda i: (i, 0))],
        (width // block,),
    )[0]


def output_terms(chain, active, attn, groups, right):
    depth, width = right.shape
    tile = width // 4
    lefts = [active, attn]
    own = [item.shape[1] // groups for item in lefts]
    stride = sum(own)

    def kernel(active, attn, right, out):
        before = 0
        for left, many in zip((active, attn), own):
            terms = times_leading(left[...], right[...]).astype(jnp.bfloat16)
            for group in range(groups):
                at = group * stride + before
                out[at : at + many, :] = terms[group * many : (group + 1) * many]
            before = many

    return chain.launch(
        kernel,
        [active, attn, right],
        [
            pl.BlockSpec(item.shape, lambda i: (0, 0), pipeline_mode=pl.Buffered(1))
            for item in lefts
        ]
        + [pl.BlockSpec((depth, tile), lambda i: (0, i))],
        [((groups * stride, width), jnp.bfloat16)],
        [pl.BlockSpec((groups * stride, tile), lambda i: (0, i))],
        (width // tile,),
    )[0]


def pack(chain, arrays, moves, columns):
    rows = arrays[0].shape[0]

    def kernel(*refs):
        for slot, at, which, column, many in moves:
            refs[-1][slot, :, at : at + many] = refs[which][:, column : column + many]

    shape = (HEADS, rows, columns)
    return chain.launch(
        kernel,
        arrays,
        [whole(item) for item in arrays],
        [(shape, jnp.bfloat16)],
        [pl.BlockSpec(shape, lambda i: (0, 0, 0))],
    )[0]


def unpack(chain, places, got, sums, weight, gain, shift):
    rows, width = weight.shape
    gain = gain.astype(jnp.float32).reshape(rows, 1)
    shift = shift.astype(jnp.float32).reshape(rows, 1)

    def kernel(got, sums, weight, gain, shift, grad, gain_grad, shift_grad):
        by_gain = jnp.zeros((rows, 1), jnp.float32)
        by_shift = jnp.zeros((rows, 1), jnp.float32)
        for slot, start, at, many in places:
            terms = got[slot, :, start : start + many].astype(jnp.float32)
            total = sums[slot : slot + 1, start : start + many]
            parts = weight[:, at : at + many].astype(jnp.float32)
            grad[:, at : at + many] = terms * gain[...] + total * shift[...]
            by_gain += jnp.sum(parts * terms, axis=1, keepdims=True)
            by_shift += jnp.sum(parts * total, axis=1, keepdims=True)
        gain_grad[...] = by_gain
        shift_grad[...] = by_shift

    inputs = [got, sums, weight, gain, shift]
    shapes = [(rows, width), (rows, 1), (rows, 1)]
    grad, gain_grad, shift_grad = chain.launch(
        kernel,
        inputs,
        [whole(item) for item in inputs],
        [(shape, jnp.float32) for shape in shapes],
        [pl.BlockSpec(shape, lambda i: (0, 0)) for shape in shapes],
    )
    return grad, gain_grad.reshape(rows), shift_grad.reshape(rows)


def per_device(
    plan,
    tokens,
    seq_lengths,
    ln1_gain,
    ln1_bias,
    ln2_gain,
    ln2_bias,
    qkv_weight,
    qkv_bias,
    dense_weight,
    dense_bias,
    expand_weight,
    expand_bias,
    contract_weight,
    contract_bias,
    cotangent,
):
    slots, width = tokens.shape
    rows = qkv_weight.shape[0]
    units = contract_weight.shape[0]
    count, groups = plan.count, plan.groups
    head_dim = width // HEADS
    rotated = head_dim // 4
    hidden_units = groups * units
    me = lax.axis_index("dp")
    slot = me % HEADS
    sharing, across = plan.sharing(), plan.across()
    outer_bits = tuple(range(3, plan.bits))
    chain = Chain()

    def gather(value):
        return lax.all_gather(value, "dp", axis=0, tiled=True, axis_index_groups=across)

    def reduce(value):
        return lax.psum_scatter(
            value, "dp", scatter_dimension=0, tiled=True, axis_index_groups=across
        )

    def exchange(value):
        return lax.all_to_all(value, "dp", 0, 0, tiled=True, axis_index_groups=sharing)

    to_slot = [(d, plan.device(d % groups, d // groups)) for d in range(count)]
    from_slot = [(target, source) for source, target in to_slot]
    dense_part = lax.ppermute(dense_weight, "dp", to_slot)
    out_part = jnp.concatenate([contract_weight, dense_part])
    weight_out = gather(out_part)
    chain.settle(out_part)
    contract_runs = [(group * (units + rows), units) for group in range(groups)]
    dense_runs = [(group * (units + rows) + units, rows) for group in range(groups)]

    own_tokens = own_pieces(tokens, plan)

    parts = [
        ln1_gain,
        ln1_bias,
        ln2_gain,
        ln2_bias,
        dense_bias,
        contract_bias,
        qkv_bias,
        expand_bias,
        seq_lengths[0].astype(jnp.bfloat16),
    ]
    sizes = [item.shape[0] for item in parts]
    lines = -(-sum(sizes) // 1024) * 8
    small = jnp.concatenate(parts + [jnp.zeros((lines * 128 - sum(sizes),), jnp.bfloat16)])
    every = gather_small(small.reshape(lines, 128), outer_bits + (0, 2, 1), me, plan)
    every = every.reshape(count, lines * 128).astype(jnp.float32)

    expand_places = [
        (s, group * units, plan.device(group, s) * units, units)
        for s in range(HEADS)
        for group in range(groups)
    ]
    qkv_places = [
        (s, part * head_dim, part * width + s * head_dim, head_dim)
        for s in range(HEADS)
        for part in range(3)
    ]
    split = 3 * head_dim
    moves = [(s, at, 0, column, many) for s, at, column, many in qkv_places]
    moves += [(s, split + at, 1, column, many) for s, at, column, many in expand_places]
    own = exchange(pack(chain, [qkv_weight, expand_weight], moves, split + hidden_units))
    token_pieces = all_pieces(own_tokens, own_tokens[4], 1, plan)
    own_cotangent = own_pieces(cotangent, plan)
    early = [weight_out] + [piece for piece, _ in token_pieces[1:]]
    taken, at = [], 0
    for size in sizes:
        taken.append(every[:, at : at + size])
        at += size
    gain_one, shift_one, gain_two, shift_two, bias_dense, bias_contract = [
        item.reshape(1, width) for item in taken[:6]
    ]
    bias_qkv = lax.dynamic_index_in_dim(
        taken[6].reshape(3, HEADS, head_dim), slot, 1, keepdims=False
    ).reshape(1, split)
    bias_expand = lax.dynamic_index_in_dim(
        taken[7].reshape(groups, HEADS, units), slot, 1, keepdims=False
    ).reshape(1, hidden_units)
    lengths = jnp.concatenate(
        [lax.dynamic_slice_in_dim(taken[8], me ^ mask, 1) for mask in ORDER]
    ).astype(jnp.int32)
    segment, position = jax.vmap(lambda item: slot_layout(item, slots))(lengths)
    cosine, sine = rotary_tables(position.reshape(-1), rotated, head_dim // 2)
    chain.settle(cosine, *early)
    qkv_own, expand_own = split_columns(chain, own.reshape(HEADS * rows, -1), split)
    weight_expand, weight_qkv = gather(expand_own), gather(qkv_own)

    def sum_begin(compute, blocked, known):
        terms = terms_of(chain, compute, slots, width, 1, blocked, known, None, False)[0]
        return swap(terms, 0, plan)

    def sum_next(compute, blocked, known, got):
        own, of_x, of_y, left, right = terms_of(
            chain, compute, slots, width, 0, blocked, known, got, True
        )
        return own, of_x, of_y, swap(left, 1, plan), swap(right, 2, plan)

    def sum_last(own, *parts):
        to_x, to_y = pass_terms(chain, *parts)
        return own, swap(to_x, 1, plan), swap(to_y, 2, plan)

    low_one, low_two, normed = over_blocks(
        chain,
        norm_kernel,
        slots,
        token_pieces,
        [],
        [gain_one, shift_one, gain_two, shift_two],
        [(width, jnp.bfloat16)] * 3,
    )

    passed = swap(copied(chain, own_cotangent[2]), 2, plan)
    half = laid_together(
        chain, [own_cotangent[0], own_cotangent[2], own_cotangent[4], passed]
    )
    other_half = swap(half, 0, plan)
    cotangent_pieces = [(item, place) for item in (half, other_half) for place in range(4)]

    active, slope = over_blocks(
        chain,
        expand_kernel,
        slots,
        [],
        [low_two],
        [bias_expand, weight_expand],
        [(hidden_units, jnp.bfloat16), (hidden_units, jnp.float32)],
    )
    grad_hidden, group_cotangent, hidden_sum, cotangent_sum, weight_contract = over_blocks(
        chain,
        grad_hidden_kernel,
        slots,
        cotangent_pieces,
        [slope],
        [],
        [(hidden_units, jnp.bfloat16), (width, jnp.bfloat16)],
        [hidden_units, width],
        (weight_out, contract_runs),
    )
    expand_got = reduce(input_terms(chain, normed, grad_hidden))

    (qkv,) = over_blocks(
        chain,
        lambda *refs: qkv_kernel(head_dim, *refs),
        slots,
        [],
        [low_one, cosine, sine],
        [bias_qkv, weight_qkv],
        [(split, jnp.bfloat16)],
    )
    attn, grad_qkv, qkv_sum, weight_dense = over_blocks(
        chain,
        lambda *refs: attend_kernel(head_dim, *refs),
        slots,
        [],
        [qkv, group_cotangent, cosine, sine, segment.reshape(-1, 1)],
        [segment],
        [(head_dim, jnp.bfloat16), (split, jnp.bfloat16)],
        [split],
        (weight_out, dense_runs),
    )


    branch_of = branch_terms, [attn, active], [weight_dense, weight_contract]
    norm_of = (
        norm_grad_terms,
        [grad_qkv, grad_hidden],
        [weight_qkv, weight_expand, gain_one, gain_two],
    )
    branch_got = sum_begin(*branch_of)
    norm_got = sum_begin(*norm_of)
    qkv_got = reduce(input_terms(chain, normed, grad_qkv))
    branch = sum_next(*branch_of, branch_got)

    sums = jnp.concatenate([qkv_sum, hidden_sum, cotangent_sum], axis=1).reshape(-1, 128)
    for bit in outer_bits:
        sums = sums + swap(sums, bit, plan)
    own_lines = (split + hidden_units) // 128
    bias_out_grad = lax.dynamic_slice_in_dim(
        sums[own_lines:].reshape(-1), me * (width // count), width // count
    )
    sums = gather_small(sums[:own_lines], (0, 1, 2), me, plan)
    chain.settle(sums)
    sums = sums.reshape(HEADS, -1)
    qkv_sums, expand_sums = sums[:, :split], sums[:, split:]

    branch = sum_last(*branch)
    output_got = reduce(output_terms(chain, active, attn, groups, group_cotangent))
    norm_parts = sum_next(*norm_of, norm_got)
    layer_out = finish_output(chain, tokens, *branch, bias_dense, bias_contract)
    expand_got = exchange(expand_got.reshape(HEADS, rows, hidden_units))
    qkv_got = exchange(qkv_got.reshape(HEADS, rows, split))
    chain.settle(expand_got)
    norm_parts = sum_last(*norm_parts)
    expand_weight_grad, ln2_gain_grad, ln2_bias_grad = unpack(
        chain, expand_places, expand_got, expand_sums, expand_weight, ln2_gain, ln2_bias
    )
    contract_weight_grad, dense_grad = split_output(chain, output_got, units, rows)
    dense_weight_grad = lax.ppermute(dense_grad, "dp", from_slot).astype(jnp.float32)
    input_grad = finish_input(chain, cotangent, tokens, *norm_parts)
    qkv_weight_grad, ln1_gain_grad, ln1_bias_grad = unpack(
        chain, qkv_places, qkv_got, qkv_sums, qkv_weight, ln1_gain, ln1_bias
    )
    qkv_bias_grad = qkv_sums.reshape(HEADS, 3, head_dim).transpose(1, 0, 2).reshape(3 * width)
    per = qkv_bias.shape[0]
    qkv_bias_grad = lax.dynamic_slice_in_dim(qkv_bias_grad, me * per, per)
    expand_bias_grad = lax.dynamic_slice(
        expand_sums, (slot, (me // HEADS) * units), (1, units)
    ).reshape(units)
    return (
        layer_out,
        input_grad,
        ln1_gain_grad,
        ln1_bias_grad,
        ln2_gain_grad,
        ln2_bias_grad,
        qkv_weight_grad,
        qkv_bias_grad,
        dense_weight_grad,
        bias_out_grad,
        expand_weight_grad,
        expand_bias_grad,
        contract_weight_grad,
        bias_out_grad,
    )


def solution(mesh):
    in_specs = (
        P("dp", None),
        P("dp", None),
        P("dp"),
        P("dp"),
        P("dp"),
        P("dp"),
        P("dp", None),
        P("dp"),
        P("dp", None),
        P("dp"),
        P("dp", None),
        P("dp"),
        P("dp", None),
        P("dp"),
        P("dp", None),
    )
    out_specs = (
        P("dp", None),
        P("dp", None),
        P("dp"),
        P("dp"),
        P("dp"),
        P("dp"),
        P("dp", None),
        P("dp"),
        P("dp", None),
        P("dp"),
        P("dp", None),
        P("dp"),
        P("dp", None),
        P("dp"),
    )
    plan = Plan(mesh.shape["dp"])

    def layer(*arrays):
        return per_device(plan, *arrays)

    return jax.shard_map(layer, mesh=mesh, in_specs=in_specs, out_specs=out_specs, check_vma=False)
```

```python
import math

import jax
import jax.numpy as jnp
from jax import lax
from jax.experimental import pallas as pl
from jax.experimental.pallas import tpu as pltpu
from jax.sharding import PartitionSpec as P


HEADS = 8

EPSILON = 1e-05
MASKED = -1e30
PAIRED = (((1,), (1,)), ((), ()))
LEADING = (((0,), (0,)), ((), ()))
VMEM_LIMIT = 60 * 2**20
ORDER = (0, 2, 4, 6, 1, 3, 5, 7)
BRIEF = pl.CostEstimate(flops=1, bytes_accessed=1, transcendentals=0)


class Plan:
    def __init__(self, count):
        self.count = count
        self.bits = count.bit_length() - 1
        self.groups = count // HEADS

    def device(self, group, slot):
        return group * HEADS + slot

    def sharing(self):
        return [[self.device(g, s) for s in range(HEADS)] for g in range(self.groups)]

    def across(self):
        return [[self.device(g, s) for g in range(self.groups)] for s in range(HEADS)]

    def flip(self, bit):
        return [(d, d ^ (1 << bit)) for d in range(self.count)]


def swap(value, bit, plan):
    return lax.ppermute(value, "dp", plan.flip(bit))


def gather_small(value, bits, me, plan):
    rest = value.shape
    order = sorted(bits, reverse=True)
    value = value.reshape((1,) * len(bits) + rest)
    for bit in bits:
        got = swap(value, bit, plan)
        place = order.index(bit)
        value = jnp.where(
            (me >> bit) & 1 == 0,
            jnp.concatenate([value, got], axis=place),
            jnp.concatenate([got, value], axis=place),
        )
    return value.reshape((-1,) + rest)


def own_pieces(value, plan):
    return {0: value, 2: swap(value, 1, plan), 4: swap(value, 2, plan)}


def all_pieces(pieces, passed, bit, plan):
    pieces = dict(pieces)
    pieces[6] = swap(passed, bit, plan)
    for mask in (0, 2, 4, 6):
        pieces[mask | 1] = swap(pieces[mask], 0, plan)
    return [(pieces[mask], 0) for mask in ORDER]


class Chain:
    def __init__(self):
        self.waits = []

    def settle(self, *values):
        self.waits += values

    def launch(self, kernel, inputs, in_specs, outs, out_specs, grid=(1,), prefetch=(), **options):
        known = len(prefetch) + len(inputs)
        waits = self.waits

        def body(*refs):
            kernel(*refs[:known], *refs[known + len(waits) :])

        made = pl.pallas_call(
            body,
            grid_spec=pltpu.PrefetchScalarGridSpec(
                num_scalar_prefetch=len(prefetch),
                grid=grid,
                in_specs=in_specs + [pl.BlockSpec(memory_space=pl.ANY)] * len(waits),
                out_specs=out_specs,
                **options,
            ),
            out_shape=[jax.ShapeDtypeStruct(shape, kind) for shape, kind in outs],
            compiler_params=pltpu.CompilerParams(vmem_limit_bytes=VMEM_LIMIT),
            cost_estimate=BRIEF,
        )(*prefetch, *inputs, *waits)
        self.waits = [made[0]]
        return made


def whole(item):
    return pl.BlockSpec(item.shape, lambda i, *_: (0,) * len(item.shape))


def slot_layout(lengths, slots):
    place = jnp.arange(slots, dtype=jnp.int32)
    ends = jnp.cumsum(lengths, dtype=jnp.int32)
    after = (place[:, None] >= ends[None, :]).astype(jnp.int32)
    segment = jnp.sum(after, axis=1, dtype=jnp.int32)
    offset = jnp.sum(after * lengths[None, :], axis=1, dtype=jnp.int32)
    return (segment, place - offset)


def rotary_tables(position, rotated, lanes):
    half = rotated // 2
    ladder = jnp.arange(half, dtype=jnp.float32) * (-math.log(10000.0) / half)
    angle = position.astype(jnp.float32)[:, None] * jnp.exp(ladder)[None, :]
    cosine, sine = jnp.cos(angle), jnp.sin(angle)
    rest = (position.shape[0], lanes - rotated)
    return (
        jnp.concatenate([cosine, cosine, jnp.ones(rest, jnp.float32)], axis=1),
        jnp.concatenate([-sine, sine, jnp.zeros(rest, jnp.float32)], axis=1),
    )


def norm_terms(value):
    centre = jnp.mean(value, axis=1, keepdims=True)
    spread = value - centre
    variance = jnp.mean(spread * spread, axis=1, keepdims=True)
    scale = lax.rsqrt(variance + EPSILON)
    return (spread * scale, scale)


def times(left, right):
    return jnp.dot(left, right, preferred_element_type=jnp.float32)


def times_leading(left, right):
    return lax.dot_general(left, right, LEADING, preferred_element_type=jnp.float32)


def times_paired(left, right):
    return lax.dot_general(left, right, PAIRED, preferred_element_type=jnp.float32)


def over_blocks(
    chain, kernel, slots, pieces, blocked, known, outs, sums=(), rows=None, pair=()
):
    count = HEADS
    gathered, runs = rows or (None, [])
    extra = [gathered] if runs else []

    def body(*refs):
        refs = list(refs)
        step = pl.program_id(0)
        if pieces or pair:
            held = refs.pop()
            for place, piece in enumerate(refs[: len(pieces) + len(pair)]):

                @pl.when(step == place if pieces else step // (count // 2) == place)
                def _(piece=piece):
                    held[...] = piece[...]

            refs = [held] + refs[len(pieces) + len(pair) :]
        given = bool(pieces or pair) + len(blocked) + len(known)
        if not runs:
            kernel(*refs)
            return
        weight = refs[-1]

        @pl.when(pl.program_id(0) == 0)
        def _():
            place = 0
            for start, many in runs:
                weight[place : place + many, :] = refs[given][start : start + many, :]
                place += many

        kernel(*refs[:given], weight, *refs[given + 1 : -1])

    def moving(width):
        return pl.BlockSpec((slots, width), lambda i: (i, 0))

    shapes = [((count * slots, width), kind) for width, kind in outs]
    shapes += [((1, width), jnp.float32) for width in sums]
    specs = [moving(width) for width, _ in outs]
    specs += [pl.BlockSpec((1, width), lambda i: (0, 0)) for width in sums]
    if runs:
        shape = (sum(many for _, many in runs), gathered.shape[1])
        shapes.append((shape, jnp.bfloat16))
        specs.append(pl.BlockSpec(shape, lambda i: (0, 0)))
    def half_of(item, place):
        half = count // 2
        return pl.BlockSpec(
            (slots, item.shape[1]), lambda i: (jnp.clip(i - place * half, 0, half - 1), 0)
        )

    def once(item):
        return pl.BlockSpec(item.shape, lambda i: (0, 0), pipeline_mode=pl.Buffered(1))

    options = {}
    if pieces or pair:
        item = pair[0] if pair else pieces[0][0]
        options["scratch_shapes"] = [pltpu.VMEM((slots, item.shape[1]), item.dtype)]
    return chain.launch(
        body,
        [*[item for item, _ in pieces], *pair, *blocked, *known, *extra],
        [
            pl.BlockSpec(
                (slots, item.shape[1]),
                lambda i, place=place: (place, 0),
                pipeline_mode=pl.Buffered(1),
            )
            for item, place in pieces
        ]
        + [half_of(item, place) for place, item in enumerate(pair)]
        + [moving(item.shape[1]) for item in blocked]
        + [whole(item) for item in known]
        + [once(item) for item in extra],
        shapes,
        specs,
        (count,),
        **options,
    )


def add_columns(out, value):
    total = jnp.sum(value.astype(jnp.float32), axis=0, keepdims=True)
    block = pl.program_id(0)

    @pl.when(block == 0)
    def _():
        out[...] = total

    @pl.when(block > 0)
    def _():
        out[...] += total


def terms_of(chain, compute, slots, width, place, blocked, known, added, split):
    extra = list(added)

    def kernel(*refs):
        values = [ref[...] for ref in refs[: len(blocked) + len(known)]]
        total = compute(*values)
        step = pl.program_id(0)
        outs = refs[len(values) + len(extra) :]
        if extra:
            one, two = [ref[...] for ref in refs[len(values) : len(values) + 2]]
            total += jnp.where(step < 2, one, two).astype(jnp.float32)
        if not split:
            for place, out in enumerate(outs):

                @pl.when(step // 2 == place)
                def _(out=out):
                    out[...] = total.astype(jnp.bfloat16)

            return
        for place, out in enumerate(outs[:3]):

            @pl.when(step == place)
            def _(out=out):
                out[...] = total.astype(jnp.bfloat16)

        @pl.when(step == 3)
        def _():
            outs[3][...] = total[:, : width // 2].astype(jnp.bfloat16)
            outs[4][...] = total[:, width // 2 :].astype(jnp.bfloat16)

    def half_of(place):
        return pl.BlockSpec((slots, width), lambda i: (jnp.clip(i - 2 * place, 0, 1), 0))

    if split:
        shapes = [(slots, width)] * 3 + [(slots, width // 2)] * 2
    else:
        shapes = [(2 * slots, width)] * 2
    return chain.launch(
        kernel,
        [*blocked, *known, *extra],
        [pl.BlockSpec((slots, item.shape[1]), lambda i: (i + 4 * place, 0)) for item in blocked]
        + [whole(item) for item in known]
        + [half_of(place) for place in range(len(extra))],
        [(shape, jnp.bfloat16) for shape in shapes],
        [
            pl.BlockSpec((slots, shape[1]), lambda i: (0, 0)) if split else half_of(place)
            for place, shape in enumerate(shapes)
        ],
        (4,),
    )


def pass_terms(chain, of_x, of_y, left, right):
    rows, width = of_x.shape
    half = width // 2

    def add(one, two):
        return (one.astype(jnp.float32) + two.astype(jnp.float32)).astype(jnp.bfloat16)

    def kernel(of_x, of_y, left, right, to_x, to_y):
        to_x[:, :half] = of_x[:, :half]
        to_x[:, half:] = add(of_x[:, half:], right[...])
        to_y[:, :half] = add(of_y[:, :half], left[...])
        to_y[:, half:] = of_y[:, half:]

    tile = rows // 2

    def spec(columns):
        return pl.BlockSpec((tile, columns), lambda i: (i, 0))

    return chain.launch(
        kernel,
        [of_x, of_y, left, right],
        [spec(width), spec(width), spec(half), spec(half)],
        [((rows, width), jnp.bfloat16)] * 2,
        [spec(width)] * 2,
        (2,),
    )


def split_output(chain, reduced, units, rows):
    width = reduced.shape[1]

    def kernel(reduced, contract, dense):
        contract[...] = reduced[:units].astype(jnp.float32)
        dense[...] = reduced[units:]

    shapes = [(units, width), (rows, width)]
    return chain.launch(
        kernel,
        [reduced],
        [whole(reduced)],
        list(zip(shapes, [jnp.float32, jnp.bfloat16])),
        [pl.BlockSpec(shape, lambda i: (0, 0)) for shape in shapes],
    )


def finish_input(chain, cotangent, tokens, own, one, two):
    slots, width = tokens.shape
    tile = slots // 4

    def kernel(cotangent, tokens, own, one, two, out):
        normed, scale = norm_terms(tokens[...].astype(jnp.float32))
        grad = own[...].astype(jnp.float32) + one[...].astype(jnp.float32)
        grad += two[...].astype(jnp.float32)
        along = jnp.mean(grad * normed, axis=1, keepdims=True)
        grad = grad - jnp.mean(grad, axis=1, keepdims=True) - normed * along
        out[...] = cotangent[...].astype(jnp.float32) + grad * scale

    spec = pl.BlockSpec((tile, width), lambda i: (i, 0))
    return chain.launch(
        kernel,
        [cotangent, tokens, own, one, two],
        [spec] * 5,
        [((slots, width), jnp.float32)],
        [spec],
        (slots // tile,),
    )[0]


def finish_output(chain, tokens, own, one, two, bias_one, bias_two):
    slots, width = tokens.shape
    tile = slots // 4

    def kernel(tokens, own, one, two, bias_one, bias_two, out):
        total = tokens[...].astype(jnp.float32) + own[...].astype(jnp.float32)
        total += one[...].astype(jnp.float32) + two[...].astype(jnp.float32)
        out[...] = (total + bias_one[...] + bias_two[...]).astype(jnp.bfloat16)

    spec = pl.BlockSpec((tile, width), lambda i: (i, 0))
    return chain.launch(
        kernel,
        [tokens, own, one, two, bias_one, bias_two],
        [spec] * 4 + [whole(bias_one), whole(bias_two)],
        [((slots, width), jnp.bfloat16)],
        [spec],
        (slots // tile,),
    )[0]


def split_columns(chain, value, split):
    rows, width = value.shape
    tile = rows // 4

    def kernel(value, one, two):
        one[...] = value[:, :split]
        two[...] = value[:, split:]

    def spec(columns):
        return pl.BlockSpec((tile, columns), lambda i: (i, 0))

    sizes = [split, width - split]
    return chain.launch(
        kernel,
        [value],
        [spec(width)],
        [((rows, size), value.dtype) for size in sizes],
        [spec(size) for size in sizes],
        (4,),
    )


def laid_together(chain, values):
    rows, width = values[0].shape

    def kernel(*refs):
        for step, value in enumerate(refs[:-1]):

            @pl.when(pl.program_id(0) == step)
            def _(value=value):
                refs[-1][...] = value[...]

    return chain.launch(
        kernel,
        values,
        [
            pl.BlockSpec((rows, width), lambda i: (0, 0), pipeline_mode=pl.Buffered(1))
            for _ in values
        ],
        [((len(values) * rows, width), values[0].dtype)],
        [pl.BlockSpec((rows, width), lambda i: (i, 0))],
        (len(values),),
    )[0]


def copied(chain, value):
    def kernel(value, out):
        out[...] = value[...]

    spec = pl.BlockSpec((value.shape[0] // 4, value.shape[1]), lambda i: (i, 0))
    return chain.launch(kernel, [value], [spec], [(value.shape, value.dtype)], [spec], (4,))[0]


def turn(value, cosine, sine, half):
    lane = lax.broadcasted_iota(jnp.int32, value.shape, 1)
    lanes = value.shape[1]
    swapped = jnp.where(
        lane < half, pltpu.roll(value, lanes - half, 1), pltpu.roll(value, half, 1)
    )
    return value * cosine + swapped * sine


def turn_into(out, at, value, cosine, sine, half):
    lanes = cosine.shape[1]
    turned = turn(value[:, :lanes], cosine, sine, half)
    out[:, at : at + lanes] = turned.astype(jnp.bfloat16)
    out[:, at + lanes : at + value.shape[1]] = value[:, lanes:].astype(jnp.bfloat16)


def norm_kernel(tokens, gain_one, shift_one, gain_two, shift_two, low_one, low_two, low):
    normed, _ = norm_terms(tokens[...].astype(jnp.float32))
    low_one[...] = (normed * gain_one[...] + shift_one[...]).astype(jnp.bfloat16)
    low_two[...] = (normed * gain_two[...] + shift_two[...]).astype(jnp.bfloat16)
    low[...] = normed.astype(jnp.bfloat16)


def qkv_kernel(head_dim, x, cosine, sine, bias, weight, out):
    projected = times(x[...], weight[...]) + bias[...]
    half = head_dim // 8
    for part in range(2):
        at = part * head_dim
        turn_into(out, at, projected[:, at : at + head_dim], cosine[...], sine[...], half)
    out[:, 2 * head_dim :] = projected[:, 2 * head_dim :].astype(jnp.bfloat16)


def expand_kernel(x, bias, weight, active, slope):
    hidden = times(x[...], weight[...]) + bias[...]
    below = 0.5 * (1.0 + lax.erf(hidden * math.sqrt(0.5)))
    density = jnp.exp(-0.5 * hidden * hidden) * (1.0 / math.sqrt(2.0 * math.pi))
    active[...] = (hidden * below).astype(jnp.bfloat16)
    slope[...] = below + hidden * density


def grad_hidden_kernel(cotangent, slope, weight, out, out_sum, cotangent_sum):
    grad = (times_paired(cotangent[...], weight[...]) * slope[...]).astype(jnp.bfloat16)
    out[...] = grad
    add_columns(out_sum, grad)
    add_columns(cotangent_sum, cotangent[...])


def branch_terms(attn, active, dense, contract):
    return times(attn, dense) + times(active, contract)


def norm_grad_terms(grad_qkv, grad_hidden, qkv, expand, gain_one, gain_two):
    return times_paired(grad_qkv, qkv) * gain_one + times_paired(grad_hidden, expand) * gain_two


def attend_kernel(
    head_dim,
    cotangent,
    qkv,
    cosine,
    sine,
    segment,
    segments,
    dense,
    attn,
    grad_qkv,
    grad_sum,
):
    scale = 1.0 / math.sqrt(head_dim)
    query = qkv[:, :head_dim]
    key = qkv[:, head_dim : 2 * head_dim]
    value = qkv[:, 2 * head_dim :]
    grad_attn = times_paired(cotangent[...], dense[...]).astype(jnp.bfloat16)
    slots = query.shape[0]
    row = lax.broadcasted_iota(jnp.int32, (slots, slots), 0)
    column = lax.broadcasted_iota(jnp.int32, (slots, slots), 1)
    block = pl.program_id(0)
    allowed = (segment[...] == segments[pl.ds(block, 1), :]) & (column <= row)
    masked = jnp.where(allowed, times_paired(query, key) * scale, MASKED)
    raised = jnp.exp(masked - jnp.max(masked, axis=1, keepdims=True))
    weights = raised / jnp.sum(raised, axis=1, keepdims=True)
    probs = weights.astype(jnp.bfloat16)
    attn[...] = times(probs, value).astype(jnp.bfloat16)
    grad_probs = times_paired(grad_attn, value)
    grad_value = times_leading(probs, grad_attn)
    inner = jnp.sum(weights * grad_probs, axis=1, keepdims=True)
    grad_score = (weights * (grad_probs - inner)).astype(jnp.bfloat16)
    half = head_dim // 8
    back = -sine[...]
    grad_query = times(grad_score, key) * scale
    turn_into(grad_qkv, 0, grad_query, cosine[...], back, half)
    grad_key = times_leading(grad_score, query) * scale
    turn_into(grad_qkv, head_dim, grad_key, cosine[...], back, half)
    grad_qkv[:, 2 * head_dim :] = grad_value.astype(jnp.bfloat16)
    add_columns(grad_sum, grad_qkv[...])


def input_terms(chain, normed, grad):
    depth, width = normed.shape
    columns = grad.shape[1]
    block = 256

    def kernel(left, right, out):
        out[...] = times_leading(left[...], right[...]).astype(jnp.bfloat16)

    return chain.launch(
        kernel,
        [normed, grad],
        [
            pl.BlockSpec((depth, block), lambda i: (0, i)),
            pl.BlockSpec((depth, columns), lambda i: (0, 0), pipeline_mode=pl.Buffered(1)),
        ],
        [((width, columns), jnp.bfloat16)],
        [pl.BlockSpec((block, columns), lambda i: (i, 0))],
        (width // block,),
    )[0]


def output_terms(chain, active, attn, groups, pair):
    depth, width = pair[0].shape
    tile = width // 4
    lefts = [active, attn]
    own = [item.shape[1] // groups for item in lefts]
    stride = sum(own)

    def kernel(active, attn, one, two, out):
        before = 0
        for left, many in zip((active, attn), own):
            terms = times_leading(left[:depth], one[...]) + times_leading(left[depth:], two[...])
            terms = terms.astype(jnp.bfloat16)
            for group in range(groups):
                at = group * stride + before
                out[at : at + many, :] = terms[group * many : (group + 1) * many]
            before = many

    return chain.launch(
        kernel,
        [active, attn, *pair],
        [
            pl.BlockSpec(item.shape, lambda i: (0, 0), pipeline_mode=pl.Buffered(1))
            for item in lefts
        ]
        + [pl.BlockSpec((depth, tile), lambda i: (0, i))] * 2,
        [((groups * stride, width), jnp.bfloat16)],
        [pl.BlockSpec((groups * stride, tile), lambda i: (0, i))],
        (width // tile,),
    )[0]


def pack(chain, arrays, moves, columns):
    rows = arrays[0].shape[0]

    def kernel(*refs):
        for slot, at, which, column, many in moves:
            refs[-1][slot, :, at : at + many] = refs[which][:, column : column + many]

    shape = (HEADS, rows, columns)
    return chain.launch(
        kernel,
        arrays,
        [whole(item) for item in arrays],
        [(shape, jnp.bfloat16)],
        [pl.BlockSpec(shape, lambda i: (0, 0, 0))],
    )[0]


def unpack(chain, places, got, sums, weight, gain, shift):
    rows, width = weight.shape
    gain = gain.astype(jnp.float32).reshape(rows, 1)
    shift = shift.astype(jnp.float32).reshape(rows, 1)

    def kernel(got, sums, weight, gain, shift, grad, gain_grad, shift_grad):
        by_gain = jnp.zeros((rows, 1), jnp.float32)
        by_shift = jnp.zeros((rows, 1), jnp.float32)
        for slot, start, at, many in places:
            terms = got[slot, :, start : start + many].astype(jnp.float32)
            total = sums[slot : slot + 1, start : start + many]
            parts = weight[:, at : at + many].astype(jnp.float32)
            grad[:, at : at + many] = terms * gain[...] + total * shift[...]
            by_gain += jnp.sum(parts * terms, axis=1, keepdims=True)
            by_shift += jnp.sum(parts * total, axis=1, keepdims=True)
        gain_grad[...] = by_gain
        shift_grad[...] = by_shift

    inputs = [got, sums, weight, gain, shift]
    shapes = [(rows, width), (rows, 1), (rows, 1)]
    grad, gain_grad, shift_grad = chain.launch(
        kernel,
        inputs,
        [whole(item) for item in inputs],
        [(shape, jnp.float32) for shape in shapes],
        [pl.BlockSpec(shape, lambda i: (0, 0)) for shape in shapes],
    )
    return grad, gain_grad.reshape(rows), shift_grad.reshape(rows)


def per_device(
    plan,
    tokens,
    seq_lengths,
    ln1_gain,
    ln1_bias,
    ln2_gain,
    ln2_bias,
    qkv_weight,
    qkv_bias,
    dense_weight,
    dense_bias,
    expand_weight,
    expand_bias,
    contract_weight,
    contract_bias,
    cotangent,
):
    slots, width = tokens.shape
    rows = qkv_weight.shape[0]
    units = contract_weight.shape[0]
    count, groups = plan.count, plan.groups
    head_dim = width // HEADS
    rotated = head_dim // 4
    hidden_units = groups * units
    me = lax.axis_index("dp")
    slot = me % HEADS
    sharing, across = plan.sharing(), plan.across()
    outer_bits = tuple(range(3, plan.bits))
    chain = Chain()

    def gather(value):
        return lax.all_gather(value, "dp", axis=0, tiled=True, axis_index_groups=across)

    def reduce(value):
        return lax.psum_scatter(
            value, "dp", scatter_dimension=0, tiled=True, axis_index_groups=across
        )

    def exchange(value):
        return lax.all_to_all(value, "dp", 0, 0, tiled=True, axis_index_groups=sharing)

    to_slot = [(d, plan.device(d % groups, d // groups)) for d in range(count)]
    from_slot = [(target, source) for source, target in to_slot]
    dense_part = lax.ppermute(dense_weight, "dp", to_slot)
    out_part = jnp.concatenate([contract_weight, dense_part])
    weight_out = gather(out_part)
    chain.settle(out_part)
    contract_runs = [(group * (units + rows), units) for group in range(groups)]
    dense_runs = [(group * (units + rows) + units, rows) for group in range(groups)]

    own_tokens = own_pieces(tokens, plan)

    parts = [
        ln1_gain,
        ln1_bias,
        ln2_gain,
        ln2_bias,
        dense_bias,
        contract_bias,
        qkv_bias,
        expand_bias,
        seq_lengths[0].astype(jnp.bfloat16),
    ]
    sizes = [item.shape[0] for item in parts]
    lines = -(-sum(sizes) // 1024) * 8
    small = jnp.concatenate(parts + [jnp.zeros((lines * 128 - sum(sizes),), jnp.bfloat16)])
    every = gather_small(small.reshape(lines, 128), (1, 2, 0) + outer_bits, me, plan)
    every = every.reshape(count, lines * 128).astype(jnp.float32)

    expand_places = [
        (s, group * units, plan.device(group, s) * units, units)
        for s in range(HEADS)
        for group in range(groups)
    ]
    qkv_places = [
        (s, part * head_dim, part * width + s * head_dim, head_dim)
        for s in range(HEADS)
        for part in range(3)
    ]
    split = 3 * head_dim
    moves = [(s, at, 0, column, many) for s, at, column, many in qkv_places]
    moves += [(s, split + at, 1, column, many) for s, at, column, many in expand_places]
    own = exchange(pack(chain, [qkv_weight, expand_weight], moves, split + hidden_units))
    token_pieces = all_pieces(own_tokens, own_tokens[4], 1, plan)
    own_cotangent = own_pieces(cotangent, plan)
    taken, at = [], 0
    for size in sizes:
        taken.append(every[:, at : at + size])
        at += size
    gain_one, shift_one, gain_two, shift_two, bias_dense, bias_contract = [
        item.reshape(1, width) for item in taken[:6]
    ]
    bias_qkv = lax.dynamic_index_in_dim(
        taken[6].reshape(3, HEADS, head_dim), slot, 1, keepdims=False
    ).reshape(1, split)
    bias_expand = lax.dynamic_index_in_dim(
        taken[7].reshape(groups, HEADS, units), slot, 1, keepdims=False
    ).reshape(1, hidden_units)
    lengths = jnp.concatenate(
        [lax.dynamic_slice_in_dim(taken[8], me ^ mask, 1) for mask in ORDER]
    ).astype(jnp.int32)
    segment, position = jax.vmap(lambda item: slot_layout(item, slots))(lengths)
    cosine, sine = rotary_tables(position.reshape(-1), rotated, head_dim // 2)
    chain.settle(every, *[piece for piece, _ in token_pieces[4:7]])
    qkv_own, expand_own = split_columns(chain, own.reshape(HEADS * rows, -1), split)
    weight_expand, weight_qkv = gather(expand_own), gather(qkv_own)
    chain.settle(cosine, weight_out)

    def sum_begin(compute, blocked, known):
        terms = terms_of(chain, compute, slots, width, 1, blocked, known, (), False)
        return [swap(item, 0, plan) for item in terms]

    def sum_next(compute, blocked, known, got):
        own, of_x, of_y, left, right = terms_of(
            chain, compute, slots, width, 0, blocked, known, got, True
        )
        return own, of_x, of_y, swap(left, 1, plan), swap(right, 2, plan)

    def sum_last(own, *parts):
        to_x, to_y = pass_terms(chain, *parts)
        return own, swap(to_x, 1, plan), swap(to_y, 2, plan)

    low_one, low_two, normed = over_blocks(
        chain,
        norm_kernel,
        slots,
        token_pieces,
        [],
        [gain_one, shift_one, gain_two, shift_two],
        [(width, jnp.bfloat16)] * 3,
    )

    passed = swap(copied(chain, own_cotangent[2]), 2, plan)
    half = laid_together(
        chain, [own_cotangent[0], own_cotangent[2], own_cotangent[4], passed]
    )
    other_half = swap(half, 0, plan)
    group_cotangent = (half, other_half)

    active, slope = over_blocks(
        chain,
        expand_kernel,
        slots,
        [],
        [low_two],
        [bias_expand, weight_expand],
        [(hidden_units, jnp.bfloat16), (hidden_units, jnp.float32)],
    )
    grad_hidden, hidden_sum, cotangent_sum, weight_contract = over_blocks(
        chain,
        grad_hidden_kernel,
        slots,
        [],
        [slope],
        [],
        [(hidden_units, jnp.bfloat16)],
        [hidden_units, width],
        (weight_out, contract_runs),
        group_cotangent,
    )
    expand_got = reduce(input_terms(chain, normed, grad_hidden))

    (qkv,) = over_blocks(
        chain,
        lambda *refs: qkv_kernel(head_dim, *refs),
        slots,
        [],
        [low_one, cosine, sine],
        [bias_qkv, weight_qkv],
        [(split, jnp.bfloat16)],
    )
    attn, grad_qkv, qkv_sum, weight_dense = over_blocks(
        chain,
        lambda *refs: attend_kernel(head_dim, *refs),
        slots,
        [],
        [qkv, cosine, sine, segment.reshape(-1, 1)],
        [segment],
        [(head_dim, jnp.bfloat16), (split, jnp.bfloat16)],
        [split],
        (weight_out, dense_runs),
        group_cotangent,
    )


    branch_of = branch_terms, [attn, active], [weight_dense, weight_contract]
    norm_of = (
        norm_grad_terms,
        [grad_qkv, grad_hidden],
        [weight_qkv, weight_expand, gain_one, gain_two],
    )
    qkv_got = reduce(input_terms(chain, normed, grad_qkv))
    branch_got = sum_begin(*branch_of)
    norm_got = sum_begin(*norm_of)
    branch = sum_next(*branch_of, branch_got)
    expand_got = exchange(expand_got.reshape(HEADS, rows, hidden_units))
    chain.settle(expand_got)
    output_got = reduce(output_terms(chain, active, attn, groups, group_cotangent))

    sums = jnp.concatenate([qkv_sum, hidden_sum, cotangent_sum], axis=1).reshape(-1, 128)
    for bit in outer_bits:
        sums = sums + swap(sums, bit, plan)
    own_lines = (split + hidden_units) // 128
    bias_out_grad = lax.dynamic_slice_in_dim(
        sums[own_lines:].reshape(-1), me * (width // count), width // count
    )
    sums = gather_small(sums[:own_lines], (0, 1, 2), me, plan)
    chain.settle(sums)
    sums = sums.reshape(HEADS, -1)
    qkv_sums, expand_sums = sums[:, :split], sums[:, split:]

    branch = sum_last(*branch)
    norm_parts = sum_next(*norm_of, norm_got)
    layer_out = finish_output(chain, tokens, *branch, bias_dense, bias_contract)
    qkv_got = exchange(qkv_got.reshape(HEADS, rows, split))
    norm_parts = sum_last(*norm_parts)
    expand_weight_grad, ln2_gain_grad, ln2_bias_grad = unpack(
        chain, expand_places, expand_got, expand_sums, expand_weight, ln2_gain, ln2_bias
    )
    contract_weight_grad, dense_grad = split_output(chain, output_got, units, rows)
    dense_weight_grad = lax.ppermute(dense_grad, "dp", from_slot).astype(jnp.float32)
    input_grad = finish_input(chain, cotangent, tokens, *norm_parts)
    qkv_weight_grad, ln1_gain_grad, ln1_bias_grad = unpack(
        chain, qkv_places, qkv_got, qkv_sums, qkv_weight, ln1_gain, ln1_bias
    )
    qkv_bias_grad = qkv_sums.reshape(HEADS, 3, head_dim).transpose(1, 0, 2).reshape(3 * width)
    per = qkv_bias.shape[0]
    qkv_bias_grad = lax.dynamic_slice_in_dim(qkv_bias_grad, me * per, per)
    expand_bias_grad = lax.dynamic_slice(
        expand_sums, (slot, (me // HEADS) * units), (1, units)
    ).reshape(units)
    return (
        layer_out,
        input_grad,
        ln1_gain_grad,
        ln1_bias_grad,
        ln2_gain_grad,
        ln2_bias_grad,
        qkv_weight_grad,
        qkv_bias_grad,
        dense_weight_grad,
        bias_out_grad,
        expand_weight_grad,
        expand_bias_grad,
        contract_weight_grad,
        bias_out_grad,
    )


def solution(mesh):
    in_specs = (
        P("dp", None),
        P("dp", None),
        P("dp"),
        P("dp"),
        P("dp"),
        P("dp"),
        P("dp", None),
        P("dp"),
        P("dp", None),
        P("dp"),
        P("dp", None),
        P("dp"),
        P("dp", None),
        P("dp"),
        P("dp", None),
    )
    out_specs = (
        P("dp", None),
        P("dp", None),
        P("dp"),
        P("dp"),
        P("dp"),
        P("dp"),
        P("dp", None),
        P("dp"),
        P("dp", None),
        P("dp"),
        P("dp", None),
        P("dp"),
        P("dp", None),
        P("dp"),
    )
    plan = Plan(mesh.shape["dp"])

    def layer(*arrays):
        return per_device(plan, *arrays)

    return jax.shard_map(layer, mesh=mesh, in_specs=in_specs, out_specs=out_specs, check_vma=False)
```

```python
import math

import jax
import jax.numpy as jnp
from jax import lax
from jax.experimental import pallas as pl
from jax.experimental.pallas import tpu as pltpu
from jax.sharding import PartitionSpec as P


HEADS = 8

EPSILON = 1e-05
MASKED = -1e30
PAIRED = (((1,), (1,)), ((), ()))
LEADING = (((0,), (0,)), ((), ()))
VMEM_LIMIT = 60 * 2**20
ORDER = (0, 2, 4, 6, 1, 3, 5, 7)
LONG = 400_000_000_000
BRIEF = pl.CostEstimate(flops=1, bytes_accessed=1, transcendentals=0)


class Plan:
    def __init__(self, count):
        self.count = count
        self.bits = count.bit_length() - 1
        self.groups = count // HEADS

    def device(self, group, slot):
        return group * HEADS + slot

    def sharing(self):
        return [[self.device(g, s) for s in range(HEADS)] for g in range(self.groups)]

    def across(self):
        return [[self.device(g, s) for g in range(self.groups)] for s in range(HEADS)]

    def flip(self, bit):
        return [(d, d ^ (1 << bit)) for d in range(self.count)]


def swap(value, bit, plan):
    return lax.ppermute(value, "dp", plan.flip(bit))


def gather_small(value, bits, me, plan):
    rest = value.shape
    order = sorted(bits, reverse=True)
    value = value.reshape((1,) * len(bits) + rest)
    for bit in bits:
        got = swap(value, bit, plan)
        place = order.index(bit)
        value = jnp.where(
            (me >> bit) & 1 == 0,
            jnp.concatenate([value, got], axis=place),
            jnp.concatenate([got, value], axis=place),
        )
    return value.reshape((-1,) + rest)


def own_pieces(value, plan):
    return {0: value, 2: swap(value, 1, plan), 4: swap(value, 2, plan)}


def all_pieces(pieces, passed, bit, plan):
    pieces = dict(pieces)
    pieces[6] = swap(passed, bit, plan)
    for mask in (0, 2, 4, 6):
        pieces[mask | 1] = swap(pieces[mask], 0, plan)
    return [(pieces[mask], 0) for mask in ORDER]


class Chain:
    def __init__(self):
        self.waits = []

    def settle(self, *values):
        self.waits += values

    def launch(
        self,
        kernel,
        inputs,
        in_specs,
        outs,
        out_specs,
        grid=(1,),
        prefetch=(),
        estimate=1,
        **options,
    ):
        known = len(prefetch) + len(inputs)
        waits = self.waits

        def body(*refs):
            kernel(*refs[:known], *refs[known + len(waits) :])

        made = pl.pallas_call(
            body,
            grid_spec=pltpu.PrefetchScalarGridSpec(
                num_scalar_prefetch=len(prefetch),
                grid=grid,
                in_specs=in_specs + [pl.BlockSpec(memory_space=pl.ANY)] * len(waits),
                out_specs=out_specs,
                **options,
            ),
            out_shape=[jax.ShapeDtypeStruct(shape, kind) for shape, kind in outs],
            compiler_params=pltpu.CompilerParams(vmem_limit_bytes=VMEM_LIMIT),
            cost_estimate=pl.CostEstimate(flops=estimate, bytes_accessed=1, transcendentals=0),
        )(*prefetch, *inputs, *waits)
        self.waits = [made[0]]
        return made


def whole(item):
    return pl.BlockSpec(item.shape, lambda i, *_: (0,) * len(item.shape))


def slot_layout(lengths, slots):
    place = jnp.arange(slots, dtype=jnp.int32)
    ends = jnp.cumsum(lengths, dtype=jnp.int32)
    after = (place[:, None] >= ends[None, :]).astype(jnp.int32)
    segment = jnp.sum(after, axis=1, dtype=jnp.int32)
    offset = jnp.sum(after * lengths[None, :], axis=1, dtype=jnp.int32)
    return (segment, place - offset)


def rotary_tables(position, rotated, lanes):
    half = rotated // 2
    ladder = jnp.arange(half, dtype=jnp.float32) * (-math.log(10000.0) / half)
    angle = position.astype(jnp.float32)[:, None] * jnp.exp(ladder)[None, :]
    cosine, sine = jnp.cos(angle), jnp.sin(angle)
    rest = (position.shape[0], lanes - rotated)
    return (
        jnp.concatenate([cosine, cosine, jnp.ones(rest, jnp.float32)], axis=1),
        jnp.concatenate([-sine, sine, jnp.zeros(rest, jnp.float32)], axis=1),
    )


def norm_terms(value):
    centre = jnp.mean(value, axis=1, keepdims=True)
    spread = value - centre
    variance = jnp.mean(spread * spread, axis=1, keepdims=True)
    scale = lax.rsqrt(variance + EPSILON)
    return (spread * scale, scale)


def times(left, right):
    return jnp.dot(left, right, preferred_element_type=jnp.float32)


def times_leading(left, right):
    return lax.dot_general(left, right, LEADING, preferred_element_type=jnp.float32)


def times_paired(left, right):
    return lax.dot_general(left, right, PAIRED, preferred_element_type=jnp.float32)


def over_blocks(
    chain, kernel, slots, pieces, blocked, known, outs, sums=(), rows=None, pair=()
):
    count = HEADS
    gathered, runs = rows or (None, [])
    extra = [gathered] if runs else []

    def body(*refs):
        refs = list(refs)
        step = pl.program_id(0)
        if pieces or pair:
            held = refs.pop()
            for place, piece in enumerate(refs[: len(pieces) + len(pair)]):

                @pl.when(step == place if pieces else step // (count // 2) == place)
                def _(piece=piece):
                    held[...] = piece[...]

            refs = [held] + refs[len(pieces) + len(pair) :]
        given = bool(pieces or pair) + len(blocked) + len(known)
        if not runs:
            kernel(*refs)
            return
        weight = refs[-1]

        @pl.when(pl.program_id(0) == 0)
        def _():
            place = 0
            for start, many in runs:
                weight[place : place + many, :] = refs[given][start : start + many, :]
                place += many

        kernel(*refs[:given], weight, *refs[given + 1 : -1])

    def moving(width):
        return pl.BlockSpec((slots, width), lambda i: (i, 0))

    shapes = [((count * slots, width), kind) for width, kind in outs]
    shapes += [((1, width), jnp.float32) for width in sums]
    specs = [moving(width) for width, _ in outs]
    specs += [pl.BlockSpec((1, width), lambda i: (0, 0)) for width in sums]
    if runs:
        shape = (sum(many for _, many in runs), gathered.shape[1])
        shapes.append((shape, jnp.bfloat16))
        specs.append(pl.BlockSpec(shape, lambda i: (0, 0)))
    def half_of(item, place):
        half = count // 2
        return pl.BlockSpec(
            (slots, item.shape[1]), lambda i: (jnp.clip(i - place * half, 0, half - 1), 0)
        )

    def once(item):
        return pl.BlockSpec(item.shape, lambda i: (0, 0), pipeline_mode=pl.Buffered(1))

    options = {}
    if pieces or pair:
        item = pair[0] if pair else pieces[0][0]
        options["scratch_shapes"] = [pltpu.VMEM((slots, item.shape[1]), item.dtype)]
    return chain.launch(
        body,
        [*[item for item, _ in pieces], *pair, *blocked, *known, *extra],
        [
            pl.BlockSpec(
                (slots, item.shape[1]),
                lambda i, place=place: (place, 0),
                pipeline_mode=pl.Buffered(1),
            )
            for item, place in pieces
        ]
        + [half_of(item, place) for place, item in enumerate(pair)]
        + [moving(item.shape[1]) for item in blocked]
        + [whole(item) for item in known]
        + [once(item) for item in extra],
        shapes,
        specs,
        (count,),
        **options,
    )


def add_columns(out, value):
    total = jnp.sum(value.astype(jnp.float32), axis=0, keepdims=True)
    block = pl.program_id(0)

    @pl.when(block == 0)
    def _():
        out[...] = total

    @pl.when(block > 0)
    def _():
        out[...] += total


def terms_of(chain, compute, slots, width, place, blocked, known, added, split):
    extra = list(added)

    def kernel(*refs):
        values = [ref[...] for ref in refs[: len(blocked) + len(known)]]
        total = compute(*values)
        step = pl.program_id(0)
        outs = refs[len(values) + len(extra) :]
        if extra:
            one, two = [ref[...] for ref in refs[len(values) : len(values) + 2]]
            total += jnp.where(step < 2, one, two).astype(jnp.float32)
        if not split:
            for place, out in enumerate(outs):

                @pl.when(step // 2 == place)
                def _(out=out):
                    out[...] = total.astype(jnp.bfloat16)

            return
        for place, out in enumerate(outs[:3]):

            @pl.when(step == place)
            def _(out=out):
                out[...] = total.astype(jnp.bfloat16)

        @pl.when(step == 3)
        def _():
            outs[3][...] = total[:, : width // 2].astype(jnp.bfloat16)
            outs[4][...] = total[:, width // 2 :].astype(jnp.bfloat16)

    def half_of(place):
        return pl.BlockSpec((slots, width), lambda i: (jnp.clip(i - 2 * place, 0, 1), 0))

    if split:
        shapes = [(slots, width)] * 3 + [(slots, width // 2)] * 2
    else:
        shapes = [(2 * slots, width)] * 2
    return chain.launch(
        kernel,
        [*blocked, *known, *extra],
        [pl.BlockSpec((slots, item.shape[1]), lambda i: (i + 4 * place, 0)) for item in blocked]
        + [whole(item) for item in known]
        + [half_of(place) for place in range(len(extra))],
        [(shape, jnp.bfloat16) for shape in shapes],
        [
            pl.BlockSpec((slots, shape[1]), lambda i: (0, 0)) if split else half_of(place)
            for place, shape in enumerate(shapes)
        ],
        (4,),
    )


def pass_terms(chain, of_x, of_y, left, right):
    rows, width = of_x.shape
    half = width // 2

    def add(one, two):
        return (one.astype(jnp.float32) + two.astype(jnp.float32)).astype(jnp.bfloat16)

    def kernel(of_x, of_y, left, right, to_x, to_y):
        to_x[:, :half] = of_x[:, :half]
        to_x[:, half:] = add(of_x[:, half:], right[...])
        to_y[:, :half] = add(of_y[:, :half], left[...])
        to_y[:, half:] = of_y[:, half:]

    tile = rows // 2

    def spec(columns):
        return pl.BlockSpec((tile, columns), lambda i: (i, 0))

    return chain.launch(
        kernel,
        [of_x, of_y, left, right],
        [spec(width), spec(width), spec(half), spec(half)],
        [((rows, width), jnp.bfloat16)] * 2,
        [spec(width)] * 2,
        (2,),
    )


def split_output(chain, reduced, units, rows):
    width = reduced.shape[1]

    def kernel(reduced, contract, dense):
        contract[...] = reduced[:units].astype(jnp.float32)
        dense[...] = reduced[units:]

    shapes = [(units, width), (rows, width)]
    return chain.launch(
        kernel,
        [reduced],
        [whole(reduced)],
        list(zip(shapes, [jnp.float32, jnp.bfloat16])),
        [pl.BlockSpec(shape, lambda i: (0, 0)) for shape in shapes],
    )


def finish_input(chain, cotangent, tokens, own, one, two):
    slots, width = tokens.shape
    tile = slots // 4

    def kernel(cotangent, tokens, own, one, two, out):
        normed, scale = norm_terms(tokens[...].astype(jnp.float32))
        grad = own[...].astype(jnp.float32) + one[...].astype(jnp.float32)
        grad += two[...].astype(jnp.float32)
        along = jnp.mean(grad * normed, axis=1, keepdims=True)
        grad = grad - jnp.mean(grad, axis=1, keepdims=True) - normed * along
        out[...] = cotangent[...].astype(jnp.float32) + grad * scale

    spec = pl.BlockSpec((tile, width), lambda i: (i, 0))
    return chain.launch(
        kernel,
        [cotangent, tokens, own, one, two],
        [spec] * 5,
        [((slots, width), jnp.float32)],
        [spec],
        (slots // tile,),
    )[0]


def finish_output(chain, tokens, own, one, two, bias_one, bias_two):
    slots, width = tokens.shape
    tile = slots // 4

    def kernel(tokens, own, one, two, bias_one, bias_two, out):
        total = tokens[...].astype(jnp.float32) + own[...].astype(jnp.float32)
        total += one[...].astype(jnp.float32) + two[...].astype(jnp.float32)
        out[...] = (total + bias_one[...] + bias_two[...]).astype(jnp.bfloat16)

    spec = pl.BlockSpec((tile, width), lambda i: (i, 0))
    return chain.launch(
        kernel,
        [tokens, own, one, two, bias_one, bias_two],
        [spec] * 4 + [whole(bias_one), whole(bias_two)],
        [((slots, width), jnp.bfloat16)],
        [spec],
        (slots // tile,),
        estimate=LONG,
    )[0]


def split_columns(chain, value, split):
    rows, width = value.shape
    tile = rows // 4

    def kernel(value, one, two):
        one[...] = value[:, :split]
        two[...] = value[:, split:]

    def spec(columns):
        return pl.BlockSpec((tile, columns), lambda i: (i, 0))

    sizes = [split, width - split]
    return chain.launch(
        kernel,
        [value],
        [spec(width)],
        [((rows, size), value.dtype) for size in sizes],
        [spec(size) for size in sizes],
        (4,),
    )


def laid_together(chain, values):
    rows, width = values[0].shape

    def kernel(*refs):
        for step, value in enumerate(refs[:-1]):

            @pl.when(pl.program_id(0) == step)
            def _(value=value):
                refs[-1][...] = value[...]

    return chain.launch(
        kernel,
        values,
        [
            pl.BlockSpec((rows, width), lambda i: (0, 0), pipeline_mode=pl.Buffered(1))
            for _ in values
        ],
        [((len(values) * rows, width), values[0].dtype)],
        [pl.BlockSpec((rows, width), lambda i: (i, 0))],
        (len(values),),
    )[0]


def copied(chain, value):
    def kernel(value, out):
        out[...] = value[...]

    spec = pl.BlockSpec((value.shape[0] // 4, value.shape[1]), lambda i: (i, 0))
    return chain.launch(kernel, [value], [spec], [(value.shape, value.dtype)], [spec], (4,))[0]


def turn(value, cosine, sine, half):
    lane = lax.broadcasted_iota(jnp.int32, value.shape, 1)
    lanes = value.shape[1]
    swapped = jnp.where(
        lane < half, pltpu.roll(value, lanes - half, 1), pltpu.roll(value, half, 1)
    )
    return value * cosine + swapped * sine


def turn_into(out, at, value, cosine, sine, half):
    lanes = cosine.shape[1]
    turned = turn(value[:, :lanes], cosine, sine, half)
    out[:, at : at + lanes] = turned.astype(jnp.bfloat16)
    out[:, at + lanes : at + value.shape[1]] = value[:, lanes:].astype(jnp.bfloat16)


def norm_kernel(tokens, gain_one, shift_one, gain_two, shift_two, low_one, low_two, low):
    normed, _ = norm_terms(tokens[...].astype(jnp.float32))
    low_one[...] = (normed * gain_one[...] + shift_one[...]).astype(jnp.bfloat16)
    low_two[...] = (normed * gain_two[...] + shift_two[...]).astype(jnp.bfloat16)
    low[...] = normed.astype(jnp.bfloat16)


def qkv_kernel(head_dim, x, cosine, sine, bias, weight, out):
    projected = times(x[...], weight[...]) + bias[...]
    half = head_dim // 8
    for part in range(2):
        at = part * head_dim
        turn_into(out, at, projected[:, at : at + head_dim], cosine[...], sine[...], half)
    out[:, 2 * head_dim :] = projected[:, 2 * head_dim :].astype(jnp.bfloat16)


def expand_kernel(x, bias, weight, active, slope):
    hidden = times(x[...], weight[...]) + bias[...]
    below = 0.5 * (1.0 + lax.erf(hidden * math.sqrt(0.5)))
    density = jnp.exp(-0.5 * hidden * hidden) * (1.0 / math.sqrt(2.0 * math.pi))
    active[...] = (hidden * below).astype(jnp.bfloat16)
    slope[...] = below + hidden * density


def grad_hidden_kernel(cotangent, slope, weight, out, out_sum, cotangent_sum):
    grad = (times_paired(cotangent[...], weight[...]) * slope[...]).astype(jnp.bfloat16)
    out[...] = grad
    add_columns(out_sum, grad)
    add_columns(cotangent_sum, cotangent[...])


def branch_terms(attn, active, dense, contract):
    return times(attn, dense) + times(active, contract)


def norm_grad_terms(grad_qkv, grad_hidden, qkv, expand, gain_one, gain_two):
    return times_paired(grad_qkv, qkv) * gain_one + times_paired(grad_hidden, expand) * gain_two


def attend_kernel(
    head_dim,
    cotangent,
    qkv,
    cosine,
    sine,
    segment,
    segments,
    dense,
    attn,
    grad_qkv,
    grad_sum,
):
    scale = 1.0 / math.sqrt(head_dim)
    query = qkv[:, :head_dim]
    key = qkv[:, head_dim : 2 * head_dim]
    value = qkv[:, 2 * head_dim :]
    grad_attn = times_paired(cotangent[...], dense[...]).astype(jnp.bfloat16)
    slots = query.shape[0]
    row = lax.broadcasted_iota(jnp.int32, (slots, slots), 0)
    column = lax.broadcasted_iota(jnp.int32, (slots, slots), 1)
    block = pl.program_id(0)
    allowed = (segment[...] == segments[pl.ds(block, 1), :]) & (column <= row)
    masked = jnp.where(allowed, times_paired(query, key) * scale, MASKED)
    raised = jnp.exp(masked - jnp.max(masked, axis=1, keepdims=True))
    weights = raised / jnp.sum(raised, axis=1, keepdims=True)
    probs = weights.astype(jnp.bfloat16)
    attn[...] = times(probs, value).astype(jnp.bfloat16)
    grad_probs = times_paired(grad_attn, value)
    grad_value = times_leading(probs, grad_attn)
    inner = jnp.sum(weights * grad_probs, axis=1, keepdims=True)
    grad_score = (weights * (grad_probs - inner)).astype(jnp.bfloat16)
    half = head_dim // 8
    back = -sine[...]
    grad_query = times(grad_score, key) * scale
    turn_into(grad_qkv, 0, grad_query, cosine[...], back, half)
    grad_key = times_leading(grad_score, query) * scale
    turn_into(grad_qkv, head_dim, grad_key, cosine[...], back, half)
    grad_qkv[:, 2 * head_dim :] = grad_value.astype(jnp.bfloat16)
    add_columns(grad_sum, grad_qkv[...])


def input_terms(chain, normed, grad):
    depth, width = normed.shape
    columns = grad.shape[1]
    block = 256

    def kernel(left, right, out):
        out[...] = times_leading(left[...], right[...]).astype(jnp.bfloat16)

    return chain.launch(
        kernel,
        [normed, grad],
        [
            pl.BlockSpec((depth, block), lambda i: (0, i)),
            pl.BlockSpec((depth, columns), lambda i: (0, 0), pipeline_mode=pl.Buffered(1)),
        ],
        [((width, columns), jnp.bfloat16)],
        [pl.BlockSpec((block, columns), lambda i: (i, 0))],
        (width // block,),
    )[0]


def output_terms(chain, active, attn, groups, pair):
    depth, width = pair[0].shape
    tile = width // 4
    lefts = [active, attn]
    own = [item.shape[1] // groups for item in lefts]
    stride = sum(own)

    def kernel(active, attn, one, two, out):
        before = 0
        for left, many in zip((active, attn), own):
            terms = times_leading(left[:depth], one[...]) + times_leading(left[depth:], two[...])
            terms = terms.astype(jnp.bfloat16)
            for group in range(groups):
                at = group * stride + before
                out[at : at + many, :] = terms[group * many : (group + 1) * many]
            before = many

    return chain.launch(
        kernel,
        [active, attn, *pair],
        [
            pl.BlockSpec(item.shape, lambda i: (0, 0), pipeline_mode=pl.Buffered(1))
            for item in lefts
        ]
        + [pl.BlockSpec((depth, tile), lambda i: (0, i))] * 2,
        [((groups * stride, width), jnp.bfloat16)],
        [pl.BlockSpec((groups * stride, tile), lambda i: (0, i))],
        (width // tile,),
    )[0]


def pack(chain, arrays, moves, columns):
    rows = arrays[0].shape[0]

    def kernel(*refs):
        for slot, at, which, column, many in moves:
            refs[-1][slot, :, at : at + many] = refs[which][:, column : column + many]

    shape = (HEADS, rows, columns)
    return chain.launch(
        kernel,
        arrays,
        [whole(item) for item in arrays],
        [(shape, jnp.bfloat16)],
        [pl.BlockSpec(shape, lambda i: (0, 0, 0))],
    )[0]


def unpack(chain, places, got, sums, weight, gain, shift):
    rows, width = weight.shape
    gain = gain.astype(jnp.float32).reshape(rows, 1)
    shift = shift.astype(jnp.float32).reshape(rows, 1)

    def kernel(got, sums, weight, gain, shift, grad, gain_grad, shift_grad):
        by_gain = jnp.zeros((rows, 1), jnp.float32)
        by_shift = jnp.zeros((rows, 1), jnp.float32)
        for slot, start, at, many in places:
            terms = got[slot, :, start : start + many].astype(jnp.float32)
            total = sums[slot : slot + 1, start : start + many]
            parts = weight[:, at : at + many].astype(jnp.float32)
            grad[:, at : at + many] = terms * gain[...] + total * shift[...]
            by_gain += jnp.sum(parts * terms, axis=1, keepdims=True)
            by_shift += jnp.sum(parts * total, axis=1, keepdims=True)
        gain_grad[...] = by_gain
        shift_grad[...] = by_shift

    inputs = [got, sums, weight, gain, shift]
    shapes = [(rows, width), (rows, 1), (rows, 1)]
    grad, gain_grad, shift_grad = chain.launch(
        kernel,
        inputs,
        [whole(item) for item in inputs],
        [(shape, jnp.float32) for shape in shapes],
        [pl.BlockSpec(shape, lambda i: (0, 0)) for shape in shapes],
    )
    return grad, gain_grad.reshape(rows), shift_grad.reshape(rows)


def per_device(
    plan,
    tokens,
    seq_lengths,
    ln1_gain,
    ln1_bias,
    ln2_gain,
    ln2_bias,
    qkv_weight,
    qkv_bias,
    dense_weight,
    dense_bias,
    expand_weight,
    expand_bias,
    contract_weight,
    contract_bias,
    cotangent,
):
    slots, width = tokens.shape
    rows = qkv_weight.shape[0]
    units = contract_weight.shape[0]
    count, groups = plan.count, plan.groups
    head_dim = width // HEADS
    rotated = head_dim // 4
    hidden_units = groups * units
    me = lax.axis_index("dp")
    slot = me % HEADS
    sharing, across = plan.sharing(), plan.across()
    outer_bits = tuple(range(3, plan.bits))
    chain = Chain()

    def gather(value):
        return lax.all_gather(value, "dp", axis=0, tiled=True, axis_index_groups=across)

    def reduce(value):
        return lax.psum_scatter(
            value, "dp", scatter_dimension=0, tiled=True, axis_index_groups=across
        )

    def exchange(value):
        return lax.all_to_all(value, "dp", 0, 0, tiled=True, axis_index_groups=sharing)

    to_slot = [(d, plan.device(d % groups, d // groups)) for d in range(count)]
    from_slot = [(target, source) for source, target in to_slot]
    dense_part = lax.ppermute(dense_weight, "dp", to_slot)
    out_part = jnp.concatenate([contract_weight, dense_part])
    weight_out = gather(out_part)
    chain.settle(out_part)
    contract_runs = [(group * (units + rows), units) for group in range(groups)]
    dense_runs = [(group * (units + rows) + units, rows) for group in range(groups)]

    own_tokens = own_pieces(tokens, plan)

    parts = [
        ln1_gain,
        ln1_bias,
        ln2_gain,
        ln2_bias,
        dense_bias,
        contract_bias,
        qkv_bias,
        expand_bias,
        seq_lengths[0].astype(jnp.bfloat16),
    ]
    sizes = [item.shape[0] for item in parts]
    lines = -(-sum(sizes) // 1024) * 8
    small = jnp.concatenate(parts + [jnp.zeros((lines * 128 - sum(sizes),), jnp.bfloat16)])
    every = gather_small(small.reshape(lines, 128), (1, 2, 0) + outer_bits, me, plan)
    every = every.reshape(count, lines * 128).astype(jnp.float32)

    expand_places = [
        (s, group * units, plan.device(group, s) * units, units)
        for s in range(HEADS)
        for group in range(groups)
    ]
    qkv_places = [
        (s, part * head_dim, part * width + s * head_dim, head_dim)
        for s in range(HEADS)
        for part in range(3)
    ]
    split = 3 * head_dim
    moves = [(s, at, 0, column, many) for s, at, column, many in qkv_places]
    moves += [(s, split + at, 1, column, many) for s, at, column, many in expand_places]
    own = exchange(pack(chain, [qkv_weight, expand_weight], moves, split + hidden_units))
    token_pieces = all_pieces(own_tokens, own_tokens[4], 1, plan)
    own_cotangent = own_pieces(cotangent, plan)
    taken, at = [], 0
    for size in sizes:
        taken.append(every[:, at : at + size])
        at += size
    gain_one, shift_one, gain_two, shift_two, bias_dense, bias_contract = [
        item.reshape(1, width) for item in taken[:6]
    ]
    bias_qkv = lax.dynamic_index_in_dim(
        taken[6].reshape(3, HEADS, head_dim), slot, 1, keepdims=False
    ).reshape(1, split)
    bias_expand = lax.dynamic_index_in_dim(
        taken[7].reshape(groups, HEADS, units), slot, 1, keepdims=False
    ).reshape(1, hidden_units)
    lengths = jnp.concatenate(
        [lax.dynamic_slice_in_dim(taken[8], me ^ mask, 1) for mask in ORDER]
    ).astype(jnp.int32)
    segment, position = jax.vmap(lambda item: slot_layout(item, slots))(lengths)
    cosine, sine = rotary_tables(position.reshape(-1), rotated, head_dim // 2)
    chain.settle(every, *[piece for piece, _ in token_pieces[4:7]])
    qkv_own, expand_own = split_columns(chain, own.reshape(HEADS * rows, -1), split)
    weight_expand, weight_qkv = gather(expand_own), gather(qkv_own)
    chain.settle(cosine, weight_out)

    def sum_begin(compute, blocked, known):
        terms = terms_of(chain, compute, slots, width, 1, blocked, known, (), False)
        return [swap(item, 0, plan) for item in terms]

    def sum_next(compute, blocked, known, got):
        own, of_x, of_y, left, right = terms_of(
            chain, compute, slots, width, 0, blocked, known, got, True
        )
        return own, of_x, of_y, swap(left, 1, plan), swap(right, 2, plan)

    def sum_last(own, *parts):
        to_x, to_y = pass_terms(chain, *parts)
        return own, swap(to_x, 1, plan), swap(to_y, 2, plan)

    low_one, low_two, normed = over_blocks(
        chain,
        norm_kernel,
        slots,
        token_pieces,
        [],
        [gain_one, shift_one, gain_two, shift_two],
        [(width, jnp.bfloat16)] * 3,
    )

    passed = swap(copied(chain, own_cotangent[2]), 2, plan)
    half = laid_together(
        chain, [own_cotangent[0], own_cotangent[2], own_cotangent[4], passed]
    )
    other_half = swap(half, 0, plan)
    group_cotangent = (half, other_half)

    active, slope = over_blocks(
        chain,
        expand_kernel,
        slots,
        [],
        [low_two],
        [bias_expand, weight_expand],
        [(hidden_units, jnp.bfloat16), (hidden_units, jnp.float32)],
    )
    grad_hidden, hidden_sum, cotangent_sum, weight_contract = over_blocks(
        chain,
        grad_hidden_kernel,
        slots,
        [],
        [slope],
        [],
        [(hidden_units, jnp.bfloat16)],
        [hidden_units, width],
        (weight_out, contract_runs),
        group_cotangent,
    )
    expand_got = reduce(input_terms(chain, normed, grad_hidden))

    (qkv,) = over_blocks(
        chain,
        lambda *refs: qkv_kernel(head_dim, *refs),
        slots,
        [],
        [low_one, cosine, sine],
        [bias_qkv, weight_qkv],
        [(split, jnp.bfloat16)],
    )
    attn, grad_qkv, qkv_sum, weight_dense = over_blocks(
        chain,
        lambda *refs: attend_kernel(head_dim, *refs),
        slots,
        [],
        [qkv, cosine, sine, segment.reshape(-1, 1)],
        [segment],
        [(head_dim, jnp.bfloat16), (split, jnp.bfloat16)],
        [split],
        (weight_out, dense_runs),
        group_cotangent,
    )


    branch_of = branch_terms, [attn, active], [weight_dense, weight_contract]
    norm_of = (
        norm_grad_terms,
        [grad_qkv, grad_hidden],
        [weight_qkv, weight_expand, gain_one, gain_two],
    )
    qkv_got = reduce(input_terms(chain, normed, grad_qkv))
    branch_got = sum_begin(*branch_of)
    norm_got = sum_begin(*norm_of)
    branch = sum_next(*branch_of, branch_got)
    expand_got = exchange(expand_got.reshape(HEADS, rows, hidden_units))
    chain.settle(expand_got)
    output_got = reduce(output_terms(chain, active, attn, groups, group_cotangent))
    branch = sum_last(*branch)
    chain.settle(qkv_got)
    norm_parts = sum_next(*norm_of, norm_got)
    layer_out = finish_output(chain, tokens, *branch, bias_dense, bias_contract)

    norm_parts = sum_last(*norm_parts)
    input_grad = finish_input(chain, cotangent, tokens, *norm_parts)
    contract_weight_grad, dense_grad = split_output(chain, output_got, units, rows)
    dense_weight_grad = lax.ppermute(dense_grad, "dp", from_slot).astype(jnp.float32)

    sums = jnp.concatenate([qkv_sum, hidden_sum, cotangent_sum], axis=1).reshape(-1, 128)
    for bit in outer_bits:
        sums = sums + swap(sums, bit, plan)
    own_lines = (split + hidden_units) // 128
    bias_out_grad = lax.dynamic_slice_in_dim(
        sums[own_lines:].reshape(-1), me * (width // count), width // count
    )
    sums = gather_small(sums[:own_lines], (0, 1, 2), me, plan)
    chain.settle(sums)
    sums = sums.reshape(HEADS, -1)
    qkv_sums, expand_sums = sums[:, :split], sums[:, split:]

    expand_weight_grad, ln2_gain_grad, ln2_bias_grad = unpack(
        chain, expand_places, expand_got, expand_sums, expand_weight, ln2_gain, ln2_bias
    )
    qkv_got = exchange(qkv_got.reshape(HEADS, rows, split))
    qkv_weight_grad, ln1_gain_grad, ln1_bias_grad = unpack(
        chain, qkv_places, qkv_got, qkv_sums, qkv_weight, ln1_gain, ln1_bias
    )
    qkv_bias_grad = qkv_sums.reshape(HEADS, 3, head_dim).transpose(1, 0, 2).reshape(3 * width)
    per = qkv_bias.shape[0]
    qkv_bias_grad = lax.dynamic_slice_in_dim(qkv_bias_grad, me * per, per)
    expand_bias_grad = lax.dynamic_slice(
        expand_sums, (slot, (me // HEADS) * units), (1, units)
    ).reshape(units)
    return (
        layer_out,
        input_grad,
        ln1_gain_grad,
        ln1_bias_grad,
        ln2_gain_grad,
        ln2_bias_grad,
        qkv_weight_grad,
        qkv_bias_grad,
        dense_weight_grad,
        bias_out_grad,
        expand_weight_grad,
        expand_bias_grad,
        contract_weight_grad,
        bias_out_grad,
    )


def solution(mesh):
    in_specs = (
        P("dp", None),
        P("dp", None),
        P("dp"),
        P("dp"),
        P("dp"),
        P("dp"),
        P("dp", None),
        P("dp"),
        P("dp", None),
        P("dp"),
        P("dp", None),
        P("dp"),
        P("dp", None),
        P("dp"),
        P("dp", None),
    )
    out_specs = (
        P("dp", None),
        P("dp", None),
        P("dp"),
        P("dp"),
        P("dp"),
        P("dp"),
        P("dp", None),
        P("dp"),
        P("dp", None),
        P("dp"),
        P("dp", None),
        P("dp"),
        P("dp", None),
        P("dp"),
    )
    plan = Plan(mesh.shape["dp"])

    def layer(*arrays):
        return per_device(plan, *arrays)

    return jax.shard_map(layer, mesh=mesh, in_specs=in_specs, out_specs=out_specs, check_vma=False)
```

```python
import math

import jax
import jax.numpy as jnp
from jax import lax
from jax.experimental import pallas as pl
from jax.experimental.pallas import tpu as pltpu
from jax.sharding import PartitionSpec as P


HEADS = 8

EPSILON = 1e-05
MASKED = -1e30
PAIRED = (((1,), (1,)), ((), ()))
LEADING = (((0,), (0,)), ((), ()))
VMEM_LIMIT = 60 * 2**20
ORDER = (0, 2, 4, 6, 1, 3, 5, 7)
LONG = 400_000_000_000
BRIEF = pl.CostEstimate(flops=1, bytes_accessed=1, transcendentals=0)


class Plan:
    def __init__(self, count):
        self.count = count
        self.bits = count.bit_length() - 1
        self.groups = count // HEADS

    def device(self, group, slot):
        return group * HEADS + slot

    def sharing(self):
        return [[self.device(g, s) for s in range(HEADS)] for g in range(self.groups)]

    def across(self):
        return [[self.device(g, s) for g in range(self.groups)] for s in range(HEADS)]

    def flip(self, bit):
        return [(d, d ^ (1 << bit)) for d in range(self.count)]


def swap(value, bit, plan):
    return lax.ppermute(value, "dp", plan.flip(bit))


def gather_small(value, bits, me, plan):
    rest = value.shape
    order = sorted(bits, reverse=True)
    value = value.reshape((1,) * len(bits) + rest)
    for bit in bits:
        got = swap(value, bit, plan)
        place = order.index(bit)
        value = jnp.where(
            (me >> bit) & 1 == 0,
            jnp.concatenate([value, got], axis=place),
            jnp.concatenate([got, value], axis=place),
        )
    return value.reshape((-1,) + rest)


def own_pieces(value, plan):
    return {0: value, 2: swap(value, 1, plan), 4: swap(value, 2, plan)}


def all_pieces(pieces, passed, bit, plan):
    pieces = dict(pieces)
    pieces[6] = swap(passed, bit, plan)
    for mask in (0, 2, 4, 6):
        pieces[mask | 1] = swap(pieces[mask], 0, plan)
    return [(pieces[mask], 0) for mask in ORDER]


class Chain:
    def __init__(self):
        self.waits = []

    def settle(self, *values):
        self.waits += values

    def launch(
        self,
        kernel,
        inputs,
        in_specs,
        outs,
        out_specs,
        grid=(1,),
        prefetch=(),
        estimate=1,
        **options,
    ):
        known = len(prefetch) + len(inputs)
        waits = self.waits

        def body(*refs):
            kernel(*refs[:known], *refs[known + len(waits) :])

        made = pl.pallas_call(
            body,
            grid_spec=pltpu.PrefetchScalarGridSpec(
                num_scalar_prefetch=len(prefetch),
                grid=grid,
                in_specs=in_specs + [pl.BlockSpec(memory_space=pl.ANY)] * len(waits),
                out_specs=out_specs,
                **options,
            ),
            out_shape=[jax.ShapeDtypeStruct(shape, kind) for shape, kind in outs],
            compiler_params=pltpu.CompilerParams(vmem_limit_bytes=VMEM_LIMIT),
            cost_estimate=pl.CostEstimate(flops=estimate, bytes_accessed=1, transcendentals=0),
        )(*prefetch, *inputs, *waits)
        self.waits = [made[0]]
        return made


def whole(item):
    return pl.BlockSpec(item.shape, lambda i, *_: (0,) * len(item.shape))


def slot_layout(lengths, slots):
    place = jnp.arange(slots, dtype=jnp.int32)
    ends = jnp.cumsum(lengths, dtype=jnp.int32)
    after = (place[:, None] >= ends[None, :]).astype(jnp.int32)
    segment = jnp.sum(after, axis=1, dtype=jnp.int32)
    offset = jnp.sum(after * lengths[None, :], axis=1, dtype=jnp.int32)
    return (segment, place - offset)


def rotary_tables(position, rotated, lanes):
    half = rotated // 2
    ladder = jnp.arange(half, dtype=jnp.float32) * (-math.log(10000.0) / half)
    angle = position.astype(jnp.float32)[:, None] * jnp.exp(ladder)[None, :]
    cosine, sine = jnp.cos(angle), jnp.sin(angle)
    rest = (position.shape[0], lanes - rotated)
    return (
        jnp.concatenate([cosine, cosine, jnp.ones(rest, jnp.float32)], axis=1),
        jnp.concatenate([-sine, sine, jnp.zeros(rest, jnp.float32)], axis=1),
    )


def norm_terms(value):
    centre = jnp.mean(value, axis=1, keepdims=True)
    spread = value - centre
    variance = jnp.mean(spread * spread, axis=1, keepdims=True)
    scale = lax.rsqrt(variance + EPSILON)
    return (spread * scale, scale)


def times(left, right):
    return jnp.dot(left, right, preferred_element_type=jnp.float32)


def times_leading(left, right):
    return lax.dot_general(left, right, LEADING, preferred_element_type=jnp.float32)


def times_paired(left, right):
    return lax.dot_general(left, right, PAIRED, preferred_element_type=jnp.float32)


def over_blocks(
    chain, kernel, slots, pieces, blocked, known, outs, sums=(), rows=None, pair=()
):
    count = HEADS
    gathered, runs = rows or (None, [])
    extra = [gathered] if runs else []

    def body(*refs):
        refs = list(refs)
        step = pl.program_id(0)
        if pieces or pair:
            held = refs.pop()
            for place, piece in enumerate(refs[: len(pieces) + len(pair)]):

                @pl.when(step == place if pieces else step // (count // 2) == place)
                def _(piece=piece):
                    held[...] = piece[...]

            refs = [held] + refs[len(pieces) + len(pair) :]
        given = bool(pieces or pair) + len(blocked) + len(known)
        if not runs:
            kernel(*refs)
            return
        weight = refs[-1]

        @pl.when(pl.program_id(0) == 0)
        def _():
            place = 0
            for start, many in runs:
                weight[place : place + many, :] = refs[given][start : start + many, :]
                place += many

        kernel(*refs[:given], weight, *refs[given + 1 : -1])

    def moving(width):
        return pl.BlockSpec((slots, width), lambda i: (i, 0))

    shapes = [((count * slots, width), kind) for width, kind in outs]
    shapes += [((1, width), jnp.float32) for width in sums]
    specs = [moving(width) for width, _ in outs]
    specs += [pl.BlockSpec((1, width), lambda i: (0, 0)) for width in sums]
    if runs:
        shape = (sum(many for _, many in runs), gathered.shape[1])
        shapes.append((shape, jnp.bfloat16))
        specs.append(pl.BlockSpec(shape, lambda i: (0, 0)))
    def half_of(item, place):
        half = count // 2
        return pl.BlockSpec(
            (slots, item.shape[1]), lambda i: (jnp.clip(i - place * half, 0, half - 1), 0)
        )

    def once(item):
        return pl.BlockSpec(item.shape, lambda i: (0, 0), pipeline_mode=pl.Buffered(1))

    options = {}
    if pieces or pair:
        item = pair[0] if pair else pieces[0][0]
        options["scratch_shapes"] = [pltpu.VMEM((slots, item.shape[1]), item.dtype)]
    return chain.launch(
        body,
        [*[item for item, _ in pieces], *pair, *blocked, *known, *extra],
        [
            pl.BlockSpec(
                (slots, item.shape[1]),
                lambda i, place=place: (place, 0),
                pipeline_mode=pl.Buffered(1),
            )
            for item, place in pieces
        ]
        + [half_of(item, place) for place, item in enumerate(pair)]
        + [moving(item.shape[1]) for item in blocked]
        + [whole(item) for item in known]
        + [once(item) for item in extra],
        shapes,
        specs,
        (count,),
        **options,
    )


def add_columns(out, value):
    total = jnp.sum(value.astype(jnp.float32), axis=0, keepdims=True)
    block = pl.program_id(0)

    @pl.when(block == 0)
    def _():
        out[...] = total

    @pl.when(block > 0)
    def _():
        out[...] += total


def terms_of(chain, compute, slots, width, place, blocked, known, added, split):
    extra = list(added)

    def kernel(*refs):
        values = [ref[...] for ref in refs[: len(blocked) + len(known)]]
        total = compute(*values)
        step = pl.program_id(0)
        outs = refs[len(values) + len(extra) :]
        if extra:
            one, two = [ref[...] for ref in refs[len(values) : len(values) + 2]]
            total += jnp.where(step < 2, one, two).astype(jnp.float32)
        if not split:
            for place, out in enumerate(outs):

                @pl.when(step // 2 == place)
                def _(out=out):
                    out[...] = total.astype(jnp.bfloat16)

            return
        for place, out in enumerate(outs[:3]):

            @pl.when(step == place)
            def _(out=out):
                out[...] = total.astype(jnp.bfloat16)

        @pl.when(step == 3)
        def _():
            outs[3][...] = total[:, : width // 2].astype(jnp.bfloat16)
            outs[4][...] = total[:, width // 2 :].astype(jnp.bfloat16)

    def half_of(place):
        return pl.BlockSpec((slots, width), lambda i: (jnp.clip(i - 2 * place, 0, 1), 0))

    if split:
        shapes = [(slots, width)] * 3 + [(slots, width // 2)] * 2
    else:
        shapes = [(2 * slots, width)] * 2
    return chain.launch(
        kernel,
        [*blocked, *known, *extra],
        [pl.BlockSpec((slots, item.shape[1]), lambda i: (i + 4 * place, 0)) for item in blocked]
        + [whole(item) for item in known]
        + [half_of(place) for place in range(len(extra))],
        [(shape, jnp.bfloat16) for shape in shapes],
        [
            pl.BlockSpec((slots, shape[1]), lambda i: (0, 0)) if split else half_of(place)
            for place, shape in enumerate(shapes)
        ],
        (4,),
    )


def pass_terms(chain, of_x, of_y, left, right):
    rows, width = of_x.shape
    half = width // 2

    def add(one, two):
        return (one.astype(jnp.float32) + two.astype(jnp.float32)).astype(jnp.bfloat16)

    def kernel(of_x, of_y, left, right, to_x, to_y):
        to_x[:, :half] = of_x[:, :half]
        to_x[:, half:] = add(of_x[:, half:], right[...])
        to_y[:, :half] = add(of_y[:, :half], left[...])
        to_y[:, half:] = of_y[:, half:]

    tile = rows // 2

    def spec(columns):
        return pl.BlockSpec((tile, columns), lambda i: (i, 0))

    return chain.launch(
        kernel,
        [of_x, of_y, left, right],
        [spec(width), spec(width), spec(half), spec(half)],
        [((rows, width), jnp.bfloat16)] * 2,
        [spec(width)] * 2,
        (2,),
    )


def split_output(chain, reduced, units, rows):
    width = reduced.shape[1]

    def kernel(reduced, contract, dense):
        contract[...] = reduced[:units].astype(jnp.float32)
        dense[...] = reduced[units:]

    shapes = [(units, width), (rows, width)]
    return chain.launch(
        kernel,
        [reduced],
        [whole(reduced)],
        list(zip(shapes, [jnp.float32, jnp.bfloat16])),
        [pl.BlockSpec(shape, lambda i: (0, 0)) for shape in shapes],
    )


def finish_input(chain, cotangent, tokens, own, one, two):
    slots, width = tokens.shape
    tile = slots // 4

    def kernel(cotangent, tokens, own, one, two, out):
        normed, scale = norm_terms(tokens[...].astype(jnp.float32))
        grad = own[...].astype(jnp.float32) + one[...].astype(jnp.float32)
        grad += two[...].astype(jnp.float32)
        along = jnp.mean(grad * normed, axis=1, keepdims=True)
        grad = grad - jnp.mean(grad, axis=1, keepdims=True) - normed * along
        out[...] = cotangent[...].astype(jnp.float32) + grad * scale

    spec = pl.BlockSpec((tile, width), lambda i: (i, 0))
    return chain.launch(
        kernel,
        [cotangent, tokens, own, one, two],
        [spec] * 5,
        [((slots, width), jnp.float32)],
        [spec],
        (slots // tile,),
    )[0]


def finish_output(chain, tokens, own, one, two, bias):
    slots, width = tokens.shape
    tile = slots // 4

    def kernel(tokens, own, one, two, bias, out):
        total = tokens[...].astype(jnp.float32) + own[...].astype(jnp.float32)
        total += one[...].astype(jnp.float32) + two[...].astype(jnp.float32)
        out[...] = (total + bias[...]).astype(jnp.bfloat16)

    spec = pl.BlockSpec((tile, width), lambda i: (i, 0))
    return chain.launch(
        kernel,
        [tokens, own, one, two, bias],
        [spec] * 4 + [whole(bias)],
        [((slots, width), jnp.bfloat16)],
        [spec],
        (slots // tile,),
        estimate=LONG,
    )[0]


def split_columns(chain, value, split):
    rows, width = value.shape
    tile = rows // 4

    def kernel(value, one, two):
        one[...] = value[:, :split]
        two[...] = value[:, split:]

    def spec(columns):
        return pl.BlockSpec((tile, columns), lambda i: (i, 0))

    sizes = [split, width - split]
    return chain.launch(
        kernel,
        [value],
        [spec(width)],
        [((rows, size), value.dtype) for size in sizes],
        [spec(size) for size in sizes],
        (4,),
    )


def laid_together(chain, values):
    rows, width = values[0].shape

    def kernel(*refs):
        for step, value in enumerate(refs[:-1]):

            @pl.when(pl.program_id(0) == step)
            def _(value=value):
                refs[-1][...] = value[...]

    return chain.launch(
        kernel,
        values,
        [
            pl.BlockSpec((rows, width), lambda i: (0, 0), pipeline_mode=pl.Buffered(1))
            for _ in values
        ],
        [((len(values) * rows, width), values[0].dtype)],
        [pl.BlockSpec((rows, width), lambda i: (i, 0))],
        (len(values),),
    )[0]


def copied(chain, value):
    def kernel(value, out):
        out[...] = value[...]

    spec = pl.BlockSpec((value.shape[0] // 4, value.shape[1]), lambda i: (i, 0))
    return chain.launch(kernel, [value], [spec], [(value.shape, value.dtype)], [spec], (4,))[0]


def turn(value, cosine, sine, half):
    lane = lax.broadcasted_iota(jnp.int32, value.shape, 1)
    lanes = value.shape[1]
    swapped = jnp.where(
        lane < half, pltpu.roll(value, lanes - half, 1), pltpu.roll(value, half, 1)
    )
    return value * cosine + swapped * sine


def turn_into(out, at, value, cosine, sine, half):
    lanes = cosine.shape[1]
    turned = turn(value[:, :lanes], cosine, sine, half)
    out[:, at : at + lanes] = turned.astype(jnp.bfloat16)
    out[:, at + lanes : at + value.shape[1]] = value[:, lanes:].astype(jnp.bfloat16)


def norm_kernel(tokens, gain_one, shift_one, gain_two, shift_two, low_one, low_two, low):
    normed, _ = norm_terms(tokens[...].astype(jnp.float32))
    low_one[...] = (normed * gain_one[...] + shift_one[...]).astype(jnp.bfloat16)
    low_two[...] = (normed * gain_two[...] + shift_two[...]).astype(jnp.bfloat16)
    low[...] = normed.astype(jnp.bfloat16)


def expand_kernel(x, bias, weight, active, slope):
    hidden = times(x[...], weight[...]) + bias[...]
    below = 0.5 * (1.0 + lax.erf(hidden * math.sqrt(0.5)))
    density = jnp.exp(-0.5 * hidden * hidden) * (1.0 / math.sqrt(2.0 * math.pi))
    active[...] = (hidden * below).astype(jnp.bfloat16)
    slope[...] = below + hidden * density


def grad_hidden_kernel(cotangent, slope, weight, out, out_sum, cotangent_sum):
    grad = (times_paired(cotangent[...], weight[...]) * slope[...]).astype(jnp.bfloat16)
    out[...] = grad
    add_columns(out_sum, grad)
    add_columns(cotangent_sum, cotangent[...])


def branch_terms(attn, active, dense, contract):
    return times(attn, dense) + times(active, contract)


def norm_grad_terms(grad_qkv, grad_hidden, qkv, expand, gain_one, gain_two):
    return times_paired(grad_qkv, qkv) * gain_one + times_paired(grad_hidden, expand) * gain_two


def attend_kernel(
    head_dim,
    cotangent,
    x,
    cosine,
    sine,
    segment,
    segments,
    bias,
    weight,
    dense,
    attn,
    grad_qkv,
    grad_sum,
):
    scale = 1.0 / math.sqrt(head_dim)
    half = head_dim // 8
    projected = times(x[...], weight[...]) + bias[...]
    for part in range(2):
        at = part * head_dim
        turn_into(grad_qkv, at, projected[:, at : at + head_dim], cosine[...], sine[...], half)
    query = grad_qkv[:, :head_dim]
    key = grad_qkv[:, head_dim : 2 * head_dim]
    value = projected[:, 2 * head_dim :].astype(jnp.bfloat16)
    grad_attn = times_paired(cotangent[...], dense[...]).astype(jnp.bfloat16)
    slots = query.shape[0]
    row = lax.broadcasted_iota(jnp.int32, (slots, slots), 0)
    column = lax.broadcasted_iota(jnp.int32, (slots, slots), 1)
    block = pl.program_id(0)
    allowed = (segment[...] == segments[pl.ds(block, 1), :]) & (column <= row)
    masked = jnp.where(allowed, times_paired(query, key) * scale, MASKED)
    raised = jnp.exp(masked - jnp.max(masked, axis=1, keepdims=True))
    weights = raised / jnp.sum(raised, axis=1, keepdims=True)
    probs = weights.astype(jnp.bfloat16)
    attn[...] = times(probs, value).astype(jnp.bfloat16)
    grad_probs = times_paired(grad_attn, value)
    grad_value = times_leading(probs, grad_attn)
    inner = jnp.sum(weights * grad_probs, axis=1, keepdims=True)
    grad_score = (weights * (grad_probs - inner)).astype(jnp.bfloat16)
    back = -sine[...]
    grad_query = times(grad_score, key) * scale
    turn_into(grad_qkv, 0, grad_query, cosine[...], back, half)
    grad_key = times_leading(grad_score, query) * scale
    turn_into(grad_qkv, head_dim, grad_key, cosine[...], back, half)
    grad_qkv[:, 2 * head_dim :] = grad_value.astype(jnp.bfloat16)
    add_columns(grad_sum, grad_qkv[...])


def input_terms(chain, normed, grad):
    depth, width = normed.shape
    columns = grad.shape[1]
    block = 256

    def kernel(left, right, out):
        out[...] = times_leading(left[...], right[...]).astype(jnp.bfloat16)

    return chain.launch(
        kernel,
        [normed, grad],
        [
            pl.BlockSpec((depth, block), lambda i: (0, i)),
            pl.BlockSpec((depth, columns), lambda i: (0, 0), pipeline_mode=pl.Buffered(1)),
        ],
        [((width, columns), jnp.bfloat16)],
        [pl.BlockSpec((block, columns), lambda i: (i, 0))],
        (width // block,),
    )[0]


def output_terms(chain, active, attn, groups, pair):
    depth, width = pair[0].shape
    tile = width // 4
    lefts = [active, attn]
    own = [item.shape[1] // groups for item in lefts]
    stride = sum(own)

    def kernel(active, attn, one, two, out):
        before = 0
        for left, many in zip((active, attn), own):
            terms = times_leading(left[:depth], one[...]) + times_leading(left[depth:], two[...])
            terms = terms.astype(jnp.bfloat16)
            for group in range(groups):
                at = group * stride + before
                out[at : at + many, :] = terms[group * many : (group + 1) * many]
            before = many

    return chain.launch(
        kernel,
        [active, attn, *pair],
        [
            pl.BlockSpec(item.shape, lambda i: (0, 0), pipeline_mode=pl.Buffered(1))
            for item in lefts
        ]
        + [pl.BlockSpec((depth, tile), lambda i: (0, i))] * 2,
        [((groups * stride, width), jnp.bfloat16)],
        [pl.BlockSpec((groups * stride, tile), lambda i: (0, i))],
        (width // tile,),
    )[0]


def pack(chain, arrays, moves, columns):
    rows = arrays[0].shape[0]

    def kernel(*refs):
        for slot, at, which, column, many in moves:
            refs[-1][slot, :, at : at + many] = refs[which][:, column : column + many]

    shape = (HEADS, rows, columns)
    return chain.launch(
        kernel,
        arrays,
        [whole(item) for item in arrays],
        [(shape, jnp.bfloat16)],
        [pl.BlockSpec(shape, lambda i: (0, 0, 0))],
    )[0]


def unpack(chain, places, got, sums, weight, gain, shift):
    rows, width = weight.shape
    gain = gain.astype(jnp.float32).reshape(rows, 1)
    shift = shift.astype(jnp.float32).reshape(rows, 1)

    lanes = min(128, places[0][3])

    def kernel(got, sums, weight, gain, shift, grad, gain_grad, shift_grad):
        by_gain = jnp.zeros((rows, lanes), jnp.float32)
        by_shift = jnp.zeros((rows, lanes), jnp.float32)
        for slot, start, at, many in places:
            terms = got[slot, :, start : start + many].astype(jnp.float32)
            total = sums[slot : slot + 1, start : start + many]
            parts = weight[:, at : at + many].astype(jnp.float32)
            grad[:, at : at + many] = terms * gain[...] + total * shift[...]
            for lane in range(0, many, lanes):
                span = slice(lane, lane + lanes)
                by_gain += parts[:, span] * terms[:, span]
                by_shift += parts[:, span] * total[:, span]
        gain_grad[...] = jnp.sum(by_gain.T, axis=0, keepdims=True)
        shift_grad[...] = jnp.sum(by_shift.T, axis=0, keepdims=True)

    inputs = [got, sums, weight, gain, shift]
    shapes = [(rows, width), (1, rows), (1, rows)]
    grad, gain_grad, shift_grad = chain.launch(
        kernel,
        inputs,
        [whole(item) for item in inputs],
        [(shape, jnp.float32) for shape in shapes],
        [pl.BlockSpec(shape, lambda i: (0, 0)) for shape in shapes],
    )
    return grad, gain_grad.reshape(rows), shift_grad.reshape(rows)


def per_device(
    plan,
    tokens,
    seq_lengths,
    ln1_gain,
    ln1_bias,
    ln2_gain,
    ln2_bias,
    qkv_weight,
    qkv_bias,
    dense_weight,
    dense_bias,
    expand_weight,
    expand_bias,
    contract_weight,
    contract_bias,
    cotangent,
):
    slots, width = tokens.shape
    rows = qkv_weight.shape[0]
    units = contract_weight.shape[0]
    count, groups = plan.count, plan.groups
    head_dim = width // HEADS
    rotated = head_dim // 4
    hidden_units = groups * units
    me = lax.axis_index("dp")
    slot = me % HEADS
    sharing, across = plan.sharing(), plan.across()
    outer_bits = tuple(range(3, plan.bits))
    chain = Chain()

    def gather(value):
        return lax.all_gather(value, "dp", axis=0, tiled=True, axis_index_groups=across)

    def reduce(value):
        return lax.psum_scatter(
            value, "dp", scatter_dimension=0, tiled=True, axis_index_groups=across
        )

    def exchange(value):
        return lax.all_to_all(value, "dp", 0, 0, tiled=True, axis_index_groups=sharing)

    to_slot = [(d, plan.device(d % groups, d // groups)) for d in range(count)]
    from_slot = [(target, source) for source, target in to_slot]
    dense_part = lax.ppermute(dense_weight, "dp", to_slot)
    out_part = jnp.concatenate([contract_weight, dense_part])
    weight_out = gather(out_part)
    chain.settle(out_part)
    contract_runs = [(group * (units + rows), units) for group in range(groups)]
    dense_runs = [(group * (units + rows) + units, rows) for group in range(groups)]

    own_tokens = own_pieces(tokens, plan)

    parts = [
        ln1_gain,
        ln1_bias,
        ln2_gain,
        ln2_bias,
        dense_bias,
        contract_bias,
        qkv_bias,
        expand_bias,
        seq_lengths[0].astype(jnp.bfloat16),
    ]
    sizes = [item.shape[0] for item in parts]
    lines = -(-sum(sizes) // 1024) * 8
    small = jnp.concatenate(parts + [jnp.zeros((lines * 128 - sum(sizes),), jnp.bfloat16)])
    every = gather_small(small.reshape(lines, 128), (1, 2, 0) + outer_bits, me, plan)
    every = every.reshape(count, lines * 128).astype(jnp.float32)

    expand_places = [
        (s, group * units, plan.device(group, s) * units, units)
        for s in range(HEADS)
        for group in range(groups)
    ]
    qkv_places = [
        (s, part * head_dim, part * width + s * head_dim, head_dim)
        for s in range(HEADS)
        for part in range(3)
    ]
    split = 3 * head_dim
    moves = [(s, at, 0, column, many) for s, at, column, many in qkv_places]
    moves += [(s, split + at, 1, column, many) for s, at, column, many in expand_places]
    own = exchange(pack(chain, [qkv_weight, expand_weight], moves, split + hidden_units))
    token_pieces = all_pieces(own_tokens, own_tokens[4], 1, plan)
    own_cotangent = own_pieces(cotangent, plan)
    taken, at = [], 0
    for size in sizes:
        taken.append(every[:, at : at + size])
        at += size
    gain_one, shift_one, gain_two, shift_two, bias_dense, bias_contract = [
        item.reshape(1, width) for item in taken[:6]
    ]
    bias_qkv = lax.dynamic_index_in_dim(
        taken[6].reshape(3, HEADS, head_dim), slot, 1, keepdims=False
    ).reshape(1, split)
    bias_expand = lax.dynamic_index_in_dim(
        taken[7].reshape(groups, HEADS, units), slot, 1, keepdims=False
    ).reshape(1, hidden_units)
    lengths = jnp.concatenate(
        [lax.dynamic_slice_in_dim(taken[8], me ^ mask, 1) for mask in ORDER]
    ).astype(jnp.int32)
    segment, position = jax.vmap(lambda item: slot_layout(item, slots))(lengths)
    cosine, sine = rotary_tables(position.reshape(-1), rotated, head_dim // 2)
    chain.settle(every, *[piece for piece, _ in token_pieces[4:7]])
    qkv_own, expand_own = split_columns(chain, own.reshape(HEADS * rows, -1), split)
    weight_expand, weight_qkv = gather(expand_own), gather(qkv_own)
    bias_out = bias_dense + bias_contract
    segment_column = segment.reshape(-1, 1)
    chain.settle(cosine, weight_out)

    def sum_begin(compute, blocked, known):
        terms = terms_of(chain, compute, slots, width, 1, blocked, known, (), False)
        return [swap(item, 0, plan) for item in terms]

    def sum_next(compute, blocked, known, got):
        own, of_x, of_y, left, right = terms_of(
            chain, compute, slots, width, 0, blocked, known, got, True
        )
        return own, of_x, of_y, swap(left, 1, plan), swap(right, 2, plan)

    def sum_last(own, *parts):
        to_x, to_y = pass_terms(chain, *parts)
        return own, swap(to_x, 1, plan), swap(to_y, 2, plan)

    low_one, low_two, normed = over_blocks(
        chain,
        norm_kernel,
        slots,
        token_pieces,
        [],
        [gain_one, shift_one, gain_two, shift_two],
        [(width, jnp.bfloat16)] * 3,
    )

    passed = swap(copied(chain, own_cotangent[2]), 2, plan)
    chain.settle(sine, segment_column, bias_qkv, bias_out)
    half = laid_together(
        chain, [own_cotangent[0], own_cotangent[2], own_cotangent[4], passed]
    )
    other_half = swap(half, 0, plan)
    group_cotangent = (half, other_half)

    active, slope = over_blocks(
        chain,
        expand_kernel,
        slots,
        [],
        [low_two],
        [bias_expand, weight_expand],
        [(hidden_units, jnp.bfloat16), (hidden_units, jnp.float32)],
    )
    grad_hidden, hidden_sum, cotangent_sum, weight_contract = over_blocks(
        chain,
        grad_hidden_kernel,
        slots,
        [],
        [slope],
        [],
        [(hidden_units, jnp.bfloat16)],
        [hidden_units, width],
        (weight_out, contract_runs),
        group_cotangent,
    )
    expand_got = reduce(input_terms(chain, normed, grad_hidden))

    attn, grad_qkv, qkv_sum, weight_dense = over_blocks(
        chain,
        lambda *refs: attend_kernel(head_dim, *refs),
        slots,
        [],
        [low_one, cosine, sine, segment_column],
        [segment, bias_qkv, weight_qkv],
        [(head_dim, jnp.bfloat16), (split, jnp.bfloat16)],
        [split],
        (weight_out, dense_runs),
        group_cotangent,
    )


    branch_of = branch_terms, [attn, active], [weight_dense, weight_contract]
    norm_of = (
        norm_grad_terms,
        [grad_qkv, grad_hidden],
        [weight_qkv, weight_expand, gain_one, gain_two],
    )
    qkv_got = reduce(input_terms(chain, normed, grad_qkv))
    branch_got = sum_begin(*branch_of)
    norm_got = sum_begin(*norm_of)
    branch = sum_next(*branch_of, branch_got)
    expand_got = exchange(expand_got.reshape(HEADS, rows, hidden_units))
    chain.settle(expand_got)
    output_got = reduce(output_terms(chain, active, attn, groups, group_cotangent))
    branch = sum_last(*branch)
    chain.settle(qkv_got)
    norm_parts = sum_next(*norm_of, norm_got)
    layer_out = finish_output(chain, tokens, *branch, bias_out)

    norm_parts = sum_last(*norm_parts)
    input_grad = finish_input(chain, cotangent, tokens, *norm_parts)
    contract_weight_grad, dense_grad = split_output(chain, output_got, units, rows)
    dense_weight_grad = lax.ppermute(dense_grad, "dp", from_slot).astype(jnp.float32)

    sums = jnp.concatenate([qkv_sum, hidden_sum, cotangent_sum], axis=1).reshape(-1, 128)
    for bit in outer_bits:
        sums = sums + swap(sums, bit, plan)
    own_lines = (split + hidden_units) // 128
    bias_out_grad = lax.dynamic_slice_in_dim(
        sums[own_lines:].reshape(-1), me * (width // count), width // count
    )
    sums = gather_small(sums[:own_lines], (0, 1, 2), me, plan)
    chain.settle(sums)
    sums = sums.reshape(HEADS, -1)
    qkv_sums, expand_sums = sums[:, :split], sums[:, split:]

    expand_weight_grad, ln2_gain_grad, ln2_bias_grad = unpack(
        chain, expand_places, expand_got, expand_sums, expand_weight, ln2_gain, ln2_bias
    )
    qkv_got = exchange(qkv_got.reshape(HEADS, rows, split))
    qkv_weight_grad, ln1_gain_grad, ln1_bias_grad = unpack(
        chain, qkv_places, qkv_got, qkv_sums, qkv_weight, ln1_gain, ln1_bias
    )
    qkv_bias_grad = qkv_sums.reshape(HEADS, 3, head_dim).transpose(1, 0, 2).reshape(3 * width)
    per = qkv_bias.shape[0]
    qkv_bias_grad = lax.dynamic_slice_in_dim(qkv_bias_grad, me * per, per)
    expand_bias_grad = lax.dynamic_slice(
        expand_sums, (slot, (me // HEADS) * units), (1, units)
    ).reshape(units)
    return (
        layer_out,
        input_grad,
        ln1_gain_grad,
        ln1_bias_grad,
        ln2_gain_grad,
        ln2_bias_grad,
        qkv_weight_grad,
        qkv_bias_grad,
        dense_weight_grad,
        bias_out_grad,
        expand_weight_grad,
        expand_bias_grad,
        contract_weight_grad,
        bias_out_grad,
    )


def solution(mesh):
    in_specs = (
        P("dp", None),
        P("dp", None),
        P("dp"),
        P("dp"),
        P("dp"),
        P("dp"),
        P("dp", None),
        P("dp"),
        P("dp", None),
        P("dp"),
        P("dp", None),
        P("dp"),
        P("dp", None),
        P("dp"),
        P("dp", None),
    )
    out_specs = (
        P("dp", None),
        P("dp", None),
        P("dp"),
        P("dp"),
        P("dp"),
        P("dp"),
        P("dp", None),
        P("dp"),
        P("dp", None),
        P("dp"),
        P("dp", None),
        P("dp"),
        P("dp", None),
        P("dp"),
    )
    plan = Plan(mesh.shape["dp"])

    def layer(*arrays):
        return per_device(plan, *arrays)

    return jax.shard_map(layer, mesh=mesh, in_specs=in_specs, out_specs=out_specs, check_vma=False)
```

```python
import math

import jax
import jax.numpy as jnp
from jax import lax
from jax.experimental import pallas as pl
from jax.experimental.pallas import tpu as pltpu
from jax.sharding import PartitionSpec as P


HEADS = 8

EPSILON = 1e-05
MASKED = -1e30
PAIRED = (((1,), (1,)), ((), ()))
LEADING = (((0,), (0,)), ((), ()))
VMEM_LIMIT = 60 * 2**20
ORDER = (0, 2, 4, 6, 1, 3, 5, 7)
LONG = 400_000_000_000
BRIEF = pl.CostEstimate(flops=1, bytes_accessed=1, transcendentals=0)


class Plan:
    def __init__(self, count):
        self.count = count
        self.bits = count.bit_length() - 1
        self.groups = count // HEADS

    def device(self, group, slot):
        return group * HEADS + slot

    def sharing(self):
        return [[self.device(g, s) for s in range(HEADS)] for g in range(self.groups)]

    def across(self):
        return [[self.device(g, s) for g in range(self.groups)] for s in range(HEADS)]

    def flip(self, bit):
        return [(d, d ^ (1 << bit)) for d in range(self.count)]


def swap(value, bit, plan):
    return lax.ppermute(value, "dp", plan.flip(bit))


def gather_small(value, bits, me, plan):
    rest = value.shape
    order = sorted(bits, reverse=True)
    value = value.reshape((1,) * len(bits) + rest)
    for bit in bits:
        got = swap(value, bit, plan)
        place = order.index(bit)
        value = jnp.where(
            (me >> bit) & 1 == 0,
            jnp.concatenate([value, got], axis=place),
            jnp.concatenate([got, value], axis=place),
        )
    return value.reshape((-1,) + rest)


def own_pieces(value, plan):
    return {0: value, 2: swap(value, 1, plan), 4: swap(value, 2, plan)}


def all_pieces(pieces, passed, bit, plan):
    pieces = dict(pieces)
    pieces[6] = swap(passed, bit, plan)
    for mask in (0, 2, 4, 6):
        pieces[mask | 1] = swap(pieces[mask], 0, plan)
    return [(pieces[mask], 0) for mask in ORDER]


class Chain:
    def __init__(self):
        self.waits = []

    def settle(self, *values):
        self.waits += values

    def launch(
        self,
        kernel,
        inputs,
        in_specs,
        outs,
        out_specs,
        grid=(1,),
        prefetch=(),
        estimate=1,
        **options,
    ):
        known = len(prefetch) + len(inputs)
        waits = self.waits

        def body(*refs):
            kernel(*refs[:known], *refs[known + len(waits) :])

        made = pl.pallas_call(
            body,
            grid_spec=pltpu.PrefetchScalarGridSpec(
                num_scalar_prefetch=len(prefetch),
                grid=grid,
                in_specs=in_specs + [pl.BlockSpec(memory_space=pl.ANY)] * len(waits),
                out_specs=out_specs,
                **options,
            ),
            out_shape=[jax.ShapeDtypeStruct(shape, kind) for shape, kind in outs],
            compiler_params=pltpu.CompilerParams(vmem_limit_bytes=VMEM_LIMIT),
            cost_estimate=pl.CostEstimate(flops=estimate, bytes_accessed=1, transcendentals=0),
        )(*prefetch, *inputs, *waits)
        self.waits = [made[0]]
        return made


def whole(item):
    return pl.BlockSpec(item.shape, lambda i, *_: (0,) * len(item.shape))


def slot_layout(lengths, slots):
    place = jnp.arange(slots, dtype=jnp.int32)
    ends = jnp.cumsum(lengths, dtype=jnp.int32)
    after = (place[:, None] >= ends[None, :]).astype(jnp.int32)
    segment = jnp.sum(after, axis=1, dtype=jnp.int32)
    offset = jnp.sum(after * lengths[None, :], axis=1, dtype=jnp.int32)
    return (segment, place - offset)


def rotary_tables(position, rotated, lanes):
    half = rotated // 2
    ladder = jnp.arange(half, dtype=jnp.float32) * (-math.log(10000.0) / half)
    angle = position.astype(jnp.float32)[:, None] * jnp.exp(ladder)[None, :]
    cosine, sine = jnp.cos(angle), jnp.sin(angle)
    rest = (position.shape[0], lanes - rotated)
    return (
        jnp.concatenate([cosine, cosine, jnp.ones(rest, jnp.float32)], axis=1),
        jnp.concatenate([-sine, sine, jnp.zeros(rest, jnp.float32)], axis=1),
    )


def norm_terms(value):
    centre = jnp.mean(value, axis=1, keepdims=True)
    spread = value - centre
    variance = jnp.mean(spread * spread, axis=1, keepdims=True)
    scale = lax.rsqrt(variance + EPSILON)
    return (spread * scale, scale)


def times(left, right):
    return jnp.dot(left, right, preferred_element_type=jnp.float32)


def times_leading(left, right):
    return lax.dot_general(left, right, LEADING, preferred_element_type=jnp.float32)


def times_paired(left, right):
    return lax.dot_general(left, right, PAIRED, preferred_element_type=jnp.float32)


def over_blocks(chain, kernel, slots, pieces, blocked, known, outs, sums=(), pair=()):
    count = HEADS

    def body(*refs):
        refs = list(refs)
        step = pl.program_id(0)
        if pieces or pair:
            held = refs.pop()
            for place, piece in enumerate(refs[: len(pieces) + len(pair)]):

                @pl.when(step == place if pieces else step // (count // 2) == place)
                def _(piece=piece):
                    held[...] = piece[...]

            refs = [held] + refs[len(pieces) + len(pair) :]
        kernel(*refs)

    def moving(width):
        return pl.BlockSpec((slots, width), lambda i: (i, 0))

    shapes = [((count * slots, width), kind) for width, kind in outs]
    shapes += [((1, width), jnp.float32) for width in sums]
    specs = [moving(width) for width, _ in outs]
    specs += [pl.BlockSpec((1, width), lambda i: (0, 0)) for width in sums]

    def half_of(item, place):
        half = count // 2
        return pl.BlockSpec(
            (slots, item.shape[1]), lambda i: (jnp.clip(i - place * half, 0, half - 1), 0)
        )

    options = {}
    if pieces or pair:
        item = pair[0] if pair else pieces[0][0]
        options["scratch_shapes"] = [pltpu.VMEM((slots, item.shape[1]), item.dtype)]
    return chain.launch(
        body,
        [*[item for item, _ in pieces], *pair, *blocked, *known],
        [
            pl.BlockSpec(
                (slots, item.shape[1]),
                lambda i, place=place: (place, 0),
                pipeline_mode=pl.Buffered(1),
            )
            for item, place in pieces
        ]
        + [half_of(item, place) for place, item in enumerate(pair)]
        + [moving(item.shape[1]) for item in blocked]
        + [whole(item) for item in known],
        shapes,
        specs,
        (count,),
        **options,
    )


def add_columns(out, value):
    total = jnp.sum(value.astype(jnp.float32), axis=0, keepdims=True)
    block = pl.program_id(0)

    @pl.when(block == 0)
    def _():
        out[...] = total

    @pl.when(block > 0)
    def _():
        out[...] += total


def terms_of(chain, compute, slots, width, place, blocked, known, added, split):
    extra = list(added)

    def kernel(*refs):
        values = [ref[...] for ref in refs[: len(blocked) + len(known)]]
        total = compute(*values)
        step = pl.program_id(0)
        outs = refs[len(values) + len(extra) :]
        if extra:
            one, two = [ref[...] for ref in refs[len(values) : len(values) + 2]]
            total += jnp.where(step < 2, one, two).astype(jnp.float32)
        if not split:
            for place, out in enumerate(outs):

                @pl.when(step // 2 == place)
                def _(out=out):
                    out[...] = total.astype(jnp.bfloat16)

            return
        for place, out in enumerate(outs[:3]):

            @pl.when(step == place)
            def _(out=out):
                out[...] = total.astype(jnp.bfloat16)

        @pl.when(step == 3)
        def _():
            outs[3][...] = total[:, : width // 2].astype(jnp.bfloat16)
            outs[4][...] = total[:, width // 2 :].astype(jnp.bfloat16)

    def half_of(place):
        return pl.BlockSpec((slots, width), lambda i: (jnp.clip(i - 2 * place, 0, 1), 0))

    if split:
        shapes = [(slots, width)] * 3 + [(slots, width // 2)] * 2
    else:
        shapes = [(2 * slots, width)] * 2
    return chain.launch(
        kernel,
        [*blocked, *known, *extra],
        [pl.BlockSpec((slots, item.shape[1]), lambda i: (i + 4 * place, 0)) for item in blocked]
        + [whole(item) for item in known]
        + [half_of(place) for place in range(len(extra))],
        [(shape, jnp.bfloat16) for shape in shapes],
        [
            pl.BlockSpec((slots, shape[1]), lambda i: (0, 0)) if split else half_of(place)
            for place, shape in enumerate(shapes)
        ],
        (4,),
    )


def pass_terms(chain, of_x, of_y, left, right):
    rows, width = of_x.shape
    half = width // 2

    def add(one, two):
        return (one.astype(jnp.float32) + two.astype(jnp.float32)).astype(jnp.bfloat16)

    def kernel(of_x, of_y, left, right, to_x, to_y):
        to_x[:, :half] = of_x[:, :half]
        to_x[:, half:] = add(of_x[:, half:], right[...])
        to_y[:, :half] = add(of_y[:, :half], left[...])
        to_y[:, half:] = of_y[:, half:]

    tile = rows // 2

    def spec(columns):
        return pl.BlockSpec((tile, columns), lambda i: (i, 0))

    return chain.launch(
        kernel,
        [of_x, of_y, left, right],
        [spec(width), spec(width), spec(half), spec(half)],
        [((rows, width), jnp.bfloat16)] * 2,
        [spec(width)] * 2,
        (2,),
    )


def split_output(chain, reduced, units, rows):
    width = reduced.shape[1]

    def kernel(reduced, contract, dense):
        contract[...] = reduced[:units].astype(jnp.float32)
        dense[...] = reduced[units:]

    shapes = [(units, width), (rows, width)]
    return chain.launch(
        kernel,
        [reduced],
        [whole(reduced)],
        list(zip(shapes, [jnp.float32, jnp.bfloat16])),
        [pl.BlockSpec(shape, lambda i: (0, 0)) for shape in shapes],
    )


def finish_input(chain, cotangent, tokens, own, one, two):
    slots, width = tokens.shape
    tile = slots // 4

    def kernel(cotangent, tokens, own, one, two, out):
        normed, scale = norm_terms(tokens[...].astype(jnp.float32))
        grad = own[...].astype(jnp.float32) + one[...].astype(jnp.float32)
        grad += two[...].astype(jnp.float32)
        along = jnp.mean(grad * normed, axis=1, keepdims=True)
        grad = grad - jnp.mean(grad, axis=1, keepdims=True) - normed * along
        out[...] = cotangent[...].astype(jnp.float32) + grad * scale

    spec = pl.BlockSpec((tile, width), lambda i: (i, 0))
    return chain.launch(
        kernel,
        [cotangent, tokens, own, one, two],
        [spec] * 5,
        [((slots, width), jnp.float32)],
        [spec],
        (slots // tile,),
    )[0]


def finish_output(chain, tokens, own, one, two, bias):
    slots, width = tokens.shape
    tile = slots // 4

    def kernel(tokens, own, one, two, bias, out):
        total = tokens[...].astype(jnp.float32) + own[...].astype(jnp.float32)
        total += one[...].astype(jnp.float32) + two[...].astype(jnp.float32)
        out[...] = (total + bias[...]).astype(jnp.bfloat16)

    spec = pl.BlockSpec((tile, width), lambda i: (i, 0))
    return chain.launch(
        kernel,
        [tokens, own, one, two, bias],
        [spec] * 4 + [whole(bias)],
        [((slots, width), jnp.bfloat16)],
        [spec],
        (slots // tile,),
        estimate=LONG,
    )[0]


def split_columns(chain, value, split):
    rows, width = value.shape
    tile = rows // 4

    def kernel(value, one, two):
        one[...] = value[:, :split]
        two[...] = value[:, split:]

    def spec(columns):
        return pl.BlockSpec((tile, columns), lambda i: (i, 0))

    sizes = [split, width - split]
    return chain.launch(
        kernel,
        [value],
        [spec(width)],
        [((rows, size), value.dtype) for size in sizes],
        [spec(size) for size in sizes],
        (4,),
    )


def laid_together(chain, values):
    rows, width = values[0].shape

    def kernel(*refs):
        for step, value in enumerate(refs[:-1]):

            @pl.when(pl.program_id(0) == step)
            def _(value=value):
                refs[-1][...] = value[...]

    return chain.launch(
        kernel,
        values,
        [
            pl.BlockSpec((rows, width), lambda i: (0, 0), pipeline_mode=pl.Buffered(1))
            for _ in values
        ],
        [((len(values) * rows, width), values[0].dtype)],
        [pl.BlockSpec((rows, width), lambda i: (i, 0))],
        (len(values),),
    )[0]


def part_rows(chain, gathered, groups, units, rows):
    width = gathered.shape[1]

    def kernel(gathered, contract, dense):
        contract[...] = gathered[:units]
        dense[...] = gathered[units:]

    def spec(many):
        return pl.BlockSpec((many, width), lambda i: (i, 0))

    return chain.launch(
        kernel,
        [gathered],
        [spec(units + rows)],
        [((groups * many, width), gathered.dtype) for many in (units, rows)],
        [spec(units), spec(rows)],
        (groups,),
    )


def copied(chain, value):
    def kernel(value, out):
        out[...] = value[...]

    spec = pl.BlockSpec((value.shape[0] // 4, value.shape[1]), lambda i: (i, 0))
    return chain.launch(kernel, [value], [spec], [(value.shape, value.dtype)], [spec], (4,))[0]


def turn(value, cosine, sine, half):
    lane = lax.broadcasted_iota(jnp.int32, value.shape, 1)
    lanes = value.shape[1]
    swapped = jnp.where(
        lane < half, pltpu.roll(value, lanes - half, 1), pltpu.roll(value, half, 1)
    )
    return value * cosine + swapped * sine


def turn_into(out, at, value, cosine, sine, half):
    lanes = cosine.shape[1]
    turned = turn(value[:, :lanes], cosine, sine, half)
    out[:, at : at + lanes] = turned.astype(jnp.bfloat16)
    out[:, at + lanes : at + value.shape[1]] = value[:, lanes:].astype(jnp.bfloat16)


def norm_kernel(tokens, gain_one, shift_one, gain_two, shift_two, low_one, low_two, low):
    normed, _ = norm_terms(tokens[...].astype(jnp.float32))
    low_one[...] = (normed * gain_one[...] + shift_one[...]).astype(jnp.bfloat16)
    low_two[...] = (normed * gain_two[...] + shift_two[...]).astype(jnp.bfloat16)
    low[...] = normed.astype(jnp.bfloat16)


def expand_kernel(x, bias, weight, active, slope):
    hidden = times(x[...], weight[...]) + bias[...]
    below = 0.5 * (1.0 + lax.erf(hidden * math.sqrt(0.5)))
    density = jnp.exp(-0.5 * hidden * hidden) * (1.0 / math.sqrt(2.0 * math.pi))
    active[...] = (hidden * below).astype(jnp.bfloat16)
    slope[...] = below + hidden * density


def grad_hidden_kernel(cotangent, slope, weight, out, out_sum, cotangent_sum):
    grad = (times_paired(cotangent[...], weight[...]) * slope[...]).astype(jnp.bfloat16)
    out[...] = grad
    add_columns(out_sum, grad)
    add_columns(cotangent_sum, cotangent[...])


def branch_terms(attn, active, dense, contract):
    return times(attn, dense) + times(active, contract)


def norm_grad_terms(grad_qkv, grad_hidden, qkv, expand, gain_one, gain_two):
    return times_paired(grad_qkv, qkv) * gain_one + times_paired(grad_hidden, expand) * gain_two


def attend_kernel(
    head_dim,
    cotangent,
    x,
    cosine,
    sine,
    segment,
    segments,
    bias,
    weight,
    dense,
    attn,
    grad_qkv,
    grad_sum,
):
    scale = 1.0 / math.sqrt(head_dim)
    half = head_dim // 8
    projected = times(x[...], weight[...]) + bias[...]
    for part in range(2):
        at = part * head_dim
        turn_into(grad_qkv, at, projected[:, at : at + head_dim], cosine[...], sine[...], half)
    query = grad_qkv[:, :head_dim]
    key = grad_qkv[:, head_dim : 2 * head_dim]
    value = projected[:, 2 * head_dim :].astype(jnp.bfloat16)
    grad_attn = times_paired(cotangent[...], dense[...]).astype(jnp.bfloat16)
    slots = query.shape[0]
    row = lax.broadcasted_iota(jnp.int32, (slots, slots), 0)
    column = lax.broadcasted_iota(jnp.int32, (slots, slots), 1)
    block = pl.program_id(0)
    allowed = (segment[...] == segments[pl.ds(block, 1), :]) & (column <= row)
    masked = jnp.where(allowed, times_paired(query, key) * scale, MASKED)
    raised = jnp.exp(masked - jnp.max(masked, axis=1, keepdims=True))
    weights = raised / jnp.sum(raised, axis=1, keepdims=True)
    probs = weights.astype(jnp.bfloat16)
    attn[...] = times(probs, value).astype(jnp.bfloat16)
    grad_probs = times_paired(grad_attn, value)
    grad_value = times_leading(probs, grad_attn)
    inner = jnp.sum(weights * grad_probs, axis=1, keepdims=True)
    grad_score = (weights * (grad_probs - inner)).astype(jnp.bfloat16)
    back = -sine[...]
    grad_query = times(grad_score, key) * scale
    turn_into(grad_qkv, 0, grad_query, cosine[...], back, half)
    grad_key = times_leading(grad_score, query) * scale
    turn_into(grad_qkv, head_dim, grad_key, cosine[...], back, half)
    grad_qkv[:, 2 * head_dim :] = grad_value.astype(jnp.bfloat16)
    add_columns(grad_sum, grad_qkv[...])


def input_terms(chain, normed, grad):
    depth, width = normed.shape
    columns = grad.shape[1]
    block = 256

    def kernel(left, right, out):
        out[...] = times_leading(left[...], right[...]).astype(jnp.bfloat16)

    return chain.launch(
        kernel,
        [normed, grad],
        [
            pl.BlockSpec((depth, block), lambda i: (0, i)),
            pl.BlockSpec((depth, columns), lambda i: (0, 0), pipeline_mode=pl.Buffered(1)),
        ],
        [((width, columns), jnp.bfloat16)],
        [pl.BlockSpec((block, columns), lambda i: (i, 0))],
        (width // block,),
    )[0]


def output_terms(chain, active, attn, groups, pair):
    depth, width = pair[0].shape
    tile = width // 4
    lefts = [active, attn]
    own = [item.shape[1] // groups for item in lefts]
    stride = sum(own)

    def kernel(active, attn, one, two, out):
        before = 0
        for left, many in zip((active, attn), own):
            terms = times_leading(left[:depth], one[...]) + times_leading(left[depth:], two[...])
            terms = terms.astype(jnp.bfloat16)
            for group in range(groups):
                at = group * stride + before
                out[at : at + many, :] = terms[group * many : (group + 1) * many]
            before = many

    return chain.launch(
        kernel,
        [active, attn, *pair],
        [
            pl.BlockSpec(item.shape, lambda i: (0, 0), pipeline_mode=pl.Buffered(1))
            for item in lefts
        ]
        + [pl.BlockSpec((depth, tile), lambda i: (0, i))] * 2,
        [((groups * stride, width), jnp.bfloat16)],
        [pl.BlockSpec((groups * stride, tile), lambda i: (0, i))],
        (width // tile,),
    )[0]


def pack(chain, arrays, moves, columns):
    rows = arrays[0].shape[0]

    def kernel(*refs):
        for slot, at, which, column, many in moves:
            refs[-1][slot, :, at : at + many] = refs[which][:, column : column + many]

    shape = (HEADS, rows, columns)
    return chain.launch(
        kernel,
        arrays,
        [whole(item) for item in arrays],
        [(shape, jnp.bfloat16)],
        [pl.BlockSpec(shape, lambda i: (0, 0, 0))],
    )[0]


def unpack(chain, places, got, sums, weight, gain, shift):
    rows, width = weight.shape
    gain = gain.astype(jnp.float32).reshape(rows, 1)
    shift = shift.astype(jnp.float32).reshape(rows, 1)

    lanes = min(128, places[0][3])

    def kernel(got, sums, weight, gain, shift, grad, gain_grad, shift_grad):
        by_gain = jnp.zeros((rows, lanes), jnp.float32)
        by_shift = jnp.zeros((rows, lanes), jnp.float32)
        for slot, start, at, many in places:
            terms = got[slot, :, start : start + many].astype(jnp.float32)
            total = sums[slot : slot + 1, start : start + many]
            parts = weight[:, at : at + many].astype(jnp.float32)
            grad[:, at : at + many] = terms * gain[...] + total * shift[...]
            for lane in range(0, many, lanes):
                span = slice(lane, lane + lanes)
                by_gain += parts[:, span] * terms[:, span]
                by_shift += parts[:, span] * total[:, span]
        gain_grad[...] = jnp.sum(by_gain.T, axis=0, keepdims=True)
        shift_grad[...] = jnp.sum(by_shift.T, axis=0, keepdims=True)

    inputs = [got, sums, weight, gain, shift]
    shapes = [(rows, width), (1, rows), (1, rows)]
    grad, gain_grad, shift_grad = chain.launch(
        kernel,
        inputs,
        [whole(item) for item in inputs],
        [(shape, jnp.float32) for shape in shapes],
        [pl.BlockSpec(shape, lambda i: (0, 0)) for shape in shapes],
    )
    return grad, gain_grad.reshape(rows), shift_grad.reshape(rows)


def per_device(
    plan,
    tokens,
    seq_lengths,
    ln1_gain,
    ln1_bias,
    ln2_gain,
    ln2_bias,
    qkv_weight,
    qkv_bias,
    dense_weight,
    dense_bias,
    expand_weight,
    expand_bias,
    contract_weight,
    contract_bias,
    cotangent,
):
    slots, width = tokens.shape
    rows = qkv_weight.shape[0]
    units = contract_weight.shape[0]
    count, groups = plan.count, plan.groups
    head_dim = width // HEADS
    rotated = head_dim // 4
    hidden_units = groups * units
    me = lax.axis_index("dp")
    slot = me % HEADS
    sharing, across = plan.sharing(), plan.across()
    outer_bits = tuple(range(3, plan.bits))
    chain = Chain()

    def gather(value):
        return lax.all_gather(value, "dp", axis=0, tiled=True, axis_index_groups=across)

    def reduce(value):
        return lax.psum_scatter(
            value, "dp", scatter_dimension=0, tiled=True, axis_index_groups=across
        )

    def exchange(value):
        return lax.all_to_all(value, "dp", 0, 0, tiled=True, axis_index_groups=sharing)

    to_slot = [(d, plan.device(d % groups, d // groups)) for d in range(count)]
    from_slot = [(target, source) for source, target in to_slot]
    dense_part = lax.ppermute(dense_weight, "dp", to_slot)
    out_part = jnp.concatenate([contract_weight, dense_part])
    weight_out = gather(out_part)
    chain.settle(out_part)

    own_tokens = own_pieces(tokens, plan)

    parts = [
        ln1_gain,
        ln1_bias,
        ln2_gain,
        ln2_bias,
        dense_bias,
        contract_bias,
        qkv_bias,
        expand_bias,
        seq_lengths[0].astype(jnp.bfloat16),
    ]
    sizes = [item.shape[0] for item in parts]
    lines = -(-sum(sizes) // 1024) * 8
    small = jnp.concatenate(parts + [jnp.zeros((lines * 128 - sum(sizes),), jnp.bfloat16)])
    every = gather_small(small.reshape(lines, 128), (1, 2, 0) + outer_bits, me, plan)
    every = every.reshape(count, lines * 128).astype(jnp.float32)

    expand_places = [
        (s, group * units, plan.device(group, s) * units, units)
        for s in range(HEADS)
        for group in range(groups)
    ]
    qkv_places = [
        (s, part * head_dim, part * width + s * head_dim, head_dim)
        for s in range(HEADS)
        for part in range(3)
    ]
    split = 3 * head_dim
    moves = [(s, at, 0, column, many) for s, at, column, many in qkv_places]
    moves += [(s, split + at, 1, column, many) for s, at, column, many in expand_places]
    own = exchange(pack(chain, [qkv_weight, expand_weight], moves, split + hidden_units))
    token_pieces = all_pieces(own_tokens, own_tokens[4], 1, plan)
    own_cotangent = own_pieces(cotangent, plan)
    taken, at = [], 0
    for size in sizes:
        taken.append(every[:, at : at + size])
        at += size
    gain_one, shift_one, gain_two, shift_two, bias_dense, bias_contract = [
        item.reshape(1, width) for item in taken[:6]
    ]
    bias_qkv = lax.dynamic_index_in_dim(
        taken[6].reshape(3, HEADS, head_dim), slot, 1, keepdims=False
    ).reshape(1, split)
    bias_expand = lax.dynamic_index_in_dim(
        taken[7].reshape(groups, HEADS, units), slot, 1, keepdims=False
    ).reshape(1, hidden_units)
    lengths = jnp.concatenate(
        [lax.dynamic_slice_in_dim(taken[8], me ^ mask, 1) for mask in ORDER]
    ).astype(jnp.int32)
    segment, position = jax.vmap(lambda item: slot_layout(item, slots))(lengths)
    cosine, sine = rotary_tables(position.reshape(-1), rotated, head_dim // 2)
    chain.settle(every, *[piece for piece, _ in token_pieces[4:7]])
    qkv_own, expand_own = split_columns(chain, own.reshape(HEADS * rows, -1), split)
    weight_expand, weight_qkv = gather(expand_own), gather(qkv_own)
    bias_out = bias_dense + bias_contract
    segment_column = segment.reshape(-1, 1)
    chain.settle(cosine, weight_out)

    def sum_begin(compute, blocked, known):
        terms = terms_of(chain, compute, slots, width, 1, blocked, known, (), False)
        return [swap(item, 0, plan) for item in terms]

    def sum_next(compute, blocked, known, got):
        own, of_x, of_y, left, right = terms_of(
            chain, compute, slots, width, 0, blocked, known, got, True
        )
        return own, of_x, of_y, swap(left, 1, plan), swap(right, 2, plan)

    def sum_last(own, *parts):
        to_x, to_y = pass_terms(chain, *parts)
        return own, swap(to_x, 1, plan), swap(to_y, 2, plan)

    low_one, low_two, normed = over_blocks(
        chain,
        norm_kernel,
        slots,
        token_pieces,
        [],
        [gain_one, shift_one, gain_two, shift_two],
        [(width, jnp.bfloat16)] * 3,
    )

    passed = swap(copied(chain, own_cotangent[2]), 2, plan)
    weight_contract, weight_dense = part_rows(chain, weight_out, groups, units, rows)
    chain.settle(sine, segment_column, bias_qkv, bias_out)
    half = laid_together(
        chain, [own_cotangent[0], own_cotangent[2], own_cotangent[4], passed]
    )
    other_half = swap(half, 0, plan)
    group_cotangent = (half, other_half)

    active, slope = over_blocks(
        chain,
        expand_kernel,
        slots,
        [],
        [low_two],
        [bias_expand, weight_expand],
        [(hidden_units, jnp.bfloat16), (hidden_units, jnp.float32)],
    )
    grad_hidden, hidden_sum, cotangent_sum = over_blocks(
        chain,
        grad_hidden_kernel,
        slots,
        [],
        [slope],
        [weight_contract],
        [(hidden_units, jnp.bfloat16)],
        [hidden_units, width],
        pair=group_cotangent,
    )
    expand_got = reduce(input_terms(chain, normed, grad_hidden))

    attn, grad_qkv, qkv_sum = over_blocks(
        chain,
        lambda *refs: attend_kernel(head_dim, *refs),
        slots,
        [],
        [low_one, cosine, sine, segment_column],
        [segment, bias_qkv, weight_qkv, weight_dense],
        [(head_dim, jnp.bfloat16), (split, jnp.bfloat16)],
        [split],
        pair=group_cotangent,
    )


    branch_of = branch_terms, [attn, active], [weight_dense, weight_contract]
    norm_of = (
        norm_grad_terms,
        [grad_qkv, grad_hidden],
        [weight_qkv, weight_expand, gain_one, gain_two],
    )
    qkv_got = reduce(input_terms(chain, normed, grad_qkv))
    branch_got = sum_begin(*branch_of)
    norm_got = sum_begin(*norm_of)
    branch = sum_next(*branch_of, branch_got)
    expand_got = exchange(expand_got.reshape(HEADS, rows, hidden_units))
    chain.settle(expand_got)
    output_got = reduce(output_terms(chain, active, attn, groups, group_cotangent))
    branch = sum_last(*branch)
    chain.settle(qkv_got)
    norm_parts = sum_next(*norm_of, norm_got)
    layer_out = finish_output(chain, tokens, *branch, bias_out)

    norm_parts = sum_last(*norm_parts)
    input_grad = finish_input(chain, cotangent, tokens, *norm_parts)
    contract_weight_grad, dense_grad = split_output(chain, output_got, units, rows)
    dense_weight_grad = lax.ppermute(dense_grad, "dp", from_slot).astype(jnp.float32)

    sums = jnp.concatenate([qkv_sum, hidden_sum, cotangent_sum], axis=1).reshape(-1, 128)
    for bit in outer_bits:
        sums = sums + swap(sums, bit, plan)
    own_lines = (split + hidden_units) // 128
    bias_out_grad = lax.dynamic_slice_in_dim(
        sums[own_lines:].reshape(-1), me * (width // count), width // count
    )
    sums = gather_small(sums[:own_lines], (0, 1, 2), me, plan)
    chain.settle(sums)
    sums = sums.reshape(HEADS, -1)
    qkv_sums, expand_sums = sums[:, :split], sums[:, split:]

    expand_weight_grad, ln2_gain_grad, ln2_bias_grad = unpack(
        chain, expand_places, expand_got, expand_sums, expand_weight, ln2_gain, ln2_bias
    )
    qkv_got = exchange(qkv_got.reshape(HEADS, rows, split))
    qkv_weight_grad, ln1_gain_grad, ln1_bias_grad = unpack(
        chain, qkv_places, qkv_got, qkv_sums, qkv_weight, ln1_gain, ln1_bias
    )
    qkv_bias_grad = qkv_sums.reshape(HEADS, 3, head_dim).transpose(1, 0, 2).reshape(3 * width)
    per = qkv_bias.shape[0]
    qkv_bias_grad = lax.dynamic_slice_in_dim(qkv_bias_grad, me * per, per)
    expand_bias_grad = lax.dynamic_slice(
        expand_sums, (slot, (me // HEADS) * units), (1, units)
    ).reshape(units)
    return (
        layer_out,
        input_grad,
        ln1_gain_grad,
        ln1_bias_grad,
        ln2_gain_grad,
        ln2_bias_grad,
        qkv_weight_grad,
        qkv_bias_grad,
        dense_weight_grad,
        bias_out_grad,
        expand_weight_grad,
        expand_bias_grad,
        contract_weight_grad,
        bias_out_grad,
    )


def solution(mesh):
    in_specs = (
        P("dp", None),
        P("dp", None),
        P("dp"),
        P("dp"),
        P("dp"),
        P("dp"),
        P("dp", None),
        P("dp"),
        P("dp", None),
        P("dp"),
        P("dp", None),
        P("dp"),
        P("dp", None),
        P("dp"),
        P("dp", None),
    )
    out_specs = (
        P("dp", None),
        P("dp", None),
        P("dp"),
        P("dp"),
        P("dp"),
        P("dp"),
        P("dp", None),
        P("dp"),
        P("dp", None),
        P("dp"),
        P("dp", None),
        P("dp"),
        P("dp", None),
        P("dp"),
    )
    plan = Plan(mesh.shape["dp"])

    def layer(*arrays):
        return per_device(plan, *arrays)

    return jax.shard_map(layer, mesh=mesh, in_specs=in_specs, out_specs=out_specs, check_vma=False)
```

```python
import math

import jax
import jax.numpy as jnp
from jax import lax
from jax.experimental import pallas as pl
from jax.experimental.pallas import tpu as pltpu
from jax.sharding import PartitionSpec as P


HEADS = 8

EPSILON = 1e-05
MASKED = -1e30
PAIRED = (((1,), (1,)), ((), ()))
LEADING = (((0,), (0,)), ((), ()))
VMEM_LIMIT = 60 * 2**20
ORDER = (0, 2, 4, 6, 1, 3, 5, 7)
LONG = 400_000_000_000
BRIEF = pl.CostEstimate(flops=1, bytes_accessed=1, transcendentals=0)


class Plan:
    def __init__(self, count):
        self.count = count
        self.bits = count.bit_length() - 1
        self.groups = count // HEADS

    def device(self, group, slot):
        return group * HEADS + slot

    def sharing(self):
        return [[self.device(g, s) for s in range(HEADS)] for g in range(self.groups)]

    def across(self):
        return [[self.device(g, s) for g in range(self.groups)] for s in range(HEADS)]

    def flip(self, bit):
        return [(d, d ^ (1 << bit)) for d in range(self.count)]


def swap(value, bit, plan):
    return lax.ppermute(value, "dp", plan.flip(bit))


def gather_small(value, bits, me, plan):
    rest = value.shape
    order = sorted(bits, reverse=True)
    value = value.reshape((1,) * len(bits) + rest)
    for bit in bits:
        got = swap(value, bit, plan)
        place = order.index(bit)
        value = jnp.where(
            (me >> bit) & 1 == 0,
            jnp.concatenate([value, got], axis=place),
            jnp.concatenate([got, value], axis=place),
        )
    return value.reshape((-1,) + rest)


def own_pieces(value, plan):
    return {0: value, 2: swap(value, 1, plan), 4: swap(value, 2, plan)}


def all_pieces(pieces, passed, bit, plan):
    pieces = dict(pieces)
    pieces[6] = swap(passed, bit, plan)
    for mask in (0, 2, 4, 6):
        pieces[mask | 1] = swap(pieces[mask], 0, plan)
    return [(pieces[mask], 0) for mask in ORDER]


class Chain:
    def __init__(self):
        self.waits = []

    def settle(self, *values):
        self.waits += values

    def launch(
        self,
        kernel,
        inputs,
        in_specs,
        outs,
        out_specs,
        grid=(1,),
        prefetch=(),
        estimate=1,
        **options,
    ):
        known = len(prefetch) + len(inputs)
        waits = self.waits

        def body(*refs):
            kernel(*refs[:known], *refs[known + len(waits) :])

        made = pl.pallas_call(
            body,
            grid_spec=pltpu.PrefetchScalarGridSpec(
                num_scalar_prefetch=len(prefetch),
                grid=grid,
                in_specs=in_specs + [pl.BlockSpec(memory_space=pl.ANY)] * len(waits),
                out_specs=out_specs,
                **options,
            ),
            out_shape=[jax.ShapeDtypeStruct(shape, kind) for shape, kind in outs],
            compiler_params=pltpu.CompilerParams(vmem_limit_bytes=VMEM_LIMIT),
            cost_estimate=pl.CostEstimate(flops=estimate, bytes_accessed=1, transcendentals=0),
        )(*prefetch, *inputs, *waits)
        self.waits = [made[0]]
        return made


def whole(item):
    return pl.BlockSpec(item.shape, lambda i, *_: (0,) * len(item.shape))


def slot_layout(lengths, slots):
    place = jnp.arange(slots, dtype=jnp.int32)
    ends = jnp.cumsum(lengths, dtype=jnp.int32)
    after = (place[:, None] >= ends[None, :]).astype(jnp.int32)
    segment = jnp.sum(after, axis=1, dtype=jnp.int32)
    offset = jnp.sum(after * lengths[None, :], axis=1, dtype=jnp.int32)
    return (segment, place - offset)


def rotary_tables(position, rotated, lanes):
    half = rotated // 2
    ladder = jnp.arange(half, dtype=jnp.float32) * (-math.log(10000.0) / half)
    angle = position.astype(jnp.float32)[:, None] * jnp.exp(ladder)[None, :]
    cosine, sine = jnp.cos(angle), jnp.sin(angle)
    rest = (position.shape[0], lanes - rotated)
    return (
        jnp.concatenate([cosine, cosine, jnp.ones(rest, jnp.float32)], axis=1),
        jnp.concatenate([-sine, sine, jnp.zeros(rest, jnp.float32)], axis=1),
    )


def norm_terms(value):
    centre = jnp.mean(value, axis=1, keepdims=True)
    spread = value - centre
    variance = jnp.mean(spread * spread, axis=1, keepdims=True)
    scale = lax.rsqrt(variance + EPSILON)
    return (spread * scale, scale)


def times(left, right):
    return jnp.dot(left, right, preferred_element_type=jnp.float32)


def times_leading(left, right):
    return lax.dot_general(left, right, LEADING, preferred_element_type=jnp.float32)


def times_paired(left, right):
    return lax.dot_general(left, right, PAIRED, preferred_element_type=jnp.float32)


def over_blocks(chain, kernel, slots, pieces, blocked, known, outs, sums=(), pair=()):
    count = HEADS

    def body(*refs):
        refs = list(refs)
        step = pl.program_id(0)
        if pieces or pair:
            held = refs.pop()
            for place, piece in enumerate(refs[: len(pieces) + len(pair)]):

                @pl.when(step == place if pieces else step // (count // 2) == place)
                def _(piece=piece):
                    held[...] = piece[...]

            refs = [held] + refs[len(pieces) + len(pair) :]
        kernel(*refs)

    def moving(width):
        return pl.BlockSpec((slots, width), lambda i: (i, 0))

    shapes = [((count * slots, width), kind) for width, kind in outs]
    shapes += [((1, width), jnp.float32) for width in sums]
    specs = [moving(width) for width, _ in outs]
    specs += [pl.BlockSpec((1, width), lambda i: (0, 0)) for width in sums]

    def half_of(item, place):
        half = count // 2
        return pl.BlockSpec(
            (slots, item.shape[1]), lambda i: (jnp.clip(i - place * half, 0, half - 1), 0)
        )

    options = {}
    if pieces or pair:
        item = pair[0] if pair else pieces[0][0]
        options["scratch_shapes"] = [pltpu.VMEM((slots, item.shape[1]), item.dtype)]
    return chain.launch(
        body,
        [*[item for item, _ in pieces], *pair, *blocked, *known],
        [
            pl.BlockSpec(
                (slots, item.shape[1]),
                lambda i, place=place: (place, 0),
                pipeline_mode=pl.Buffered(1),
            )
            for item, place in pieces
        ]
        + [half_of(item, place) for place, item in enumerate(pair)]
        + [moving(item.shape[1]) for item in blocked]
        + [whole(item) for item in known],
        shapes,
        specs,
        (count,),
        **options,
    )


def add_columns(out, value):
    total = jnp.sum(value.astype(jnp.float32), axis=0, keepdims=True)
    block = pl.program_id(0)

    @pl.when(block == 0)
    def _():
        out[...] = total

    @pl.when(block > 0)
    def _():
        out[...] += total


def terms_of(chain, compute, slots, width, place, blocked, known, added, split):
    extra = list(added)

    def kernel(*refs):
        values = [ref[...] for ref in refs[: len(blocked) + len(known)]]
        total = compute(*values)
        step = pl.program_id(0)
        outs = refs[len(values) + len(extra) :]
        if extra:
            one, two = [ref[...] for ref in refs[len(values) : len(values) + 2]]
            total += jnp.where(step < 2, one, two).astype(jnp.float32)
        if not split:
            for place, out in enumerate(outs):

                @pl.when(step // 2 == place)
                def _(out=out):
                    out[...] = total.astype(jnp.bfloat16)

            return
        for place, out in enumerate(outs[:3]):

            @pl.when(step == place)
            def _(out=out):
                out[...] = total.astype(jnp.bfloat16)

        @pl.when(step == 3)
        def _():
            outs[3][...] = total[:, : width // 2].astype(jnp.bfloat16)
            outs[4][...] = total[:, width // 2 :].astype(jnp.bfloat16)

    def half_of(place):
        return pl.BlockSpec((slots, width), lambda i: (jnp.clip(i - 2 * place, 0, 1), 0))

    if split:
        shapes = [(slots, width)] * 3 + [(slots, width // 2)] * 2
    else:
        shapes = [(2 * slots, width)] * 2
    return chain.launch(
        kernel,
        [*blocked, *known, *extra],
        [pl.BlockSpec((slots, item.shape[1]), lambda i: (i + 4 * place, 0)) for item in blocked]
        + [whole(item) for item in known]
        + [half_of(place) for place in range(len(extra))],
        [(shape, jnp.bfloat16) for shape in shapes],
        [
            pl.BlockSpec((slots, shape[1]), lambda i: (0, 0)) if split else half_of(place)
            for place, shape in enumerate(shapes)
        ],
        (4,),
    )


def pass_terms(chain, of_x, of_y, left, right):
    rows, width = of_x.shape
    half = width // 2

    def add(one, two):
        return (one.astype(jnp.float32) + two.astype(jnp.float32)).astype(jnp.bfloat16)

    def kernel(of_x, of_y, left, right, to_x, to_y):
        to_x[:, :half] = of_x[:, :half]
        to_x[:, half:] = add(of_x[:, half:], right[...])
        to_y[:, :half] = add(of_y[:, :half], left[...])
        to_y[:, half:] = of_y[:, half:]

    tile = rows // 2

    def spec(columns):
        return pl.BlockSpec((tile, columns), lambda i: (i, 0))

    return chain.launch(
        kernel,
        [of_x, of_y, left, right],
        [spec(width), spec(width), spec(half), spec(half)],
        [((rows, width), jnp.bfloat16)] * 2,
        [spec(width)] * 2,
        (2,),
    )


def split_output(chain, reduced, units, rows):
    width = reduced.shape[1]

    def kernel(reduced, contract, dense):
        contract[...] = reduced[:units].astype(jnp.float32)
        dense[...] = reduced[units:]

    shapes = [(units, width), (rows, width)]
    return chain.launch(
        kernel,
        [reduced],
        [whole(reduced)],
        list(zip(shapes, [jnp.float32, jnp.bfloat16])),
        [pl.BlockSpec(shape, lambda i: (0, 0)) for shape in shapes],
    )


def finish_input(chain, cotangent, tokens, own, one, two):
    slots, width = tokens.shape
    tile = slots // 4

    def kernel(cotangent, tokens, own, one, two, out):
        normed, scale = norm_terms(tokens[...].astype(jnp.float32))
        grad = own[...].astype(jnp.float32) + one[...].astype(jnp.float32)
        grad += two[...].astype(jnp.float32)
        along = jnp.mean(grad * normed, axis=1, keepdims=True)
        grad = grad - jnp.mean(grad, axis=1, keepdims=True) - normed * along
        out[...] = cotangent[...].astype(jnp.float32) + grad * scale

    spec = pl.BlockSpec((tile, width), lambda i: (i, 0))
    return chain.launch(
        kernel,
        [cotangent, tokens, own, one, two],
        [spec] * 5,
        [((slots, width), jnp.float32)],
        [spec],
        (slots // tile,),
    )[0]


def finish_output(chain, tokens, own, one, two, bias):
    slots, width = tokens.shape
    tile = slots // 4

    def kernel(tokens, own, one, two, bias, out):
        total = tokens[...].astype(jnp.float32) + own[...].astype(jnp.float32)
        total += one[...].astype(jnp.float32) + two[...].astype(jnp.float32)
        out[...] = (total + bias[...]).astype(jnp.bfloat16)

    spec = pl.BlockSpec((tile, width), lambda i: (i, 0))
    return chain.launch(
        kernel,
        [tokens, own, one, two, bias],
        [spec] * 4 + [whole(bias)],
        [((slots, width), jnp.bfloat16)],
        [spec],
        (slots // tile,),
        estimate=LONG,
    )[0]


def split_columns(chain, value, split):
    rows, width = value.shape
    tile = rows // 4

    def kernel(value, one, two):
        one[...] = value[:, :split]
        two[...] = value[:, split:]

    def spec(columns):
        return pl.BlockSpec((tile, columns), lambda i: (i, 0))

    sizes = [split, width - split]
    return chain.launch(
        kernel,
        [value],
        [spec(width)],
        [((rows, size), value.dtype) for size in sizes],
        [spec(size) for size in sizes],
        (4,),
    )


def laid_together(chain, values):
    rows, width = values[0].shape

    def kernel(*refs):
        for step, value in enumerate(refs[:-1]):

            @pl.when(pl.program_id(0) == step)
            def _(value=value):
                refs[-1][...] = value[...]

    return chain.launch(
        kernel,
        values,
        [
            pl.BlockSpec((rows, width), lambda i: (0, 0), pipeline_mode=pl.Buffered(1))
            for _ in values
        ],
        [((len(values) * rows, width), values[0].dtype)],
        [pl.BlockSpec((rows, width), lambda i: (i, 0))],
        (len(values),),
    )[0]


def part_rows(chain, gathered, groups, units, rows):
    width = gathered.shape[1]

    def kernel(gathered, contract, dense):
        contract[...] = gathered[:units]
        dense[...] = gathered[units:]

    def spec(many):
        return pl.BlockSpec((many, width), lambda i: (i, 0))

    return chain.launch(
        kernel,
        [gathered],
        [spec(units + rows)],
        [((groups * many, width), gathered.dtype) for many in (units, rows)],
        [spec(units), spec(rows)],
        (groups,),
    )


def copied(chain, value):
    def kernel(value, out):
        out[...] = value[...]

    spec = pl.BlockSpec((value.shape[0] // 4, value.shape[1]), lambda i: (i, 0))
    return chain.launch(kernel, [value], [spec], [(value.shape, value.dtype)], [spec], (4,))[0]


def turn(value, cosine, sine, half):
    lane = lax.broadcasted_iota(jnp.int32, value.shape, 1)
    lanes = value.shape[1]
    swapped = jnp.where(
        lane < half, pltpu.roll(value, lanes - half, 1), pltpu.roll(value, half, 1)
    )
    return value * cosine + swapped * sine


def turn_into(out, at, value, cosine, sine, half):
    lanes = cosine.shape[1]
    turned = turn(value[:, :lanes], cosine, sine, half)
    out[:, at : at + lanes] = turned.astype(jnp.bfloat16)
    out[:, at + lanes : at + value.shape[1]] = value[:, lanes:].astype(jnp.bfloat16)


def norm_kernel(tokens, gain_one, shift_one, gain_two, shift_two, low_one, low_two, low):
    normed, _ = norm_terms(tokens[...].astype(jnp.float32))
    low_one[...] = (normed * gain_one[...] + shift_one[...]).astype(jnp.bfloat16)
    low_two[...] = (normed * gain_two[...] + shift_two[...]).astype(jnp.bfloat16)
    low[...] = normed.astype(jnp.bfloat16)


def expand_kernel(x, bias, weight, active, slope):
    hidden = times(x[...], weight[...]) + bias[...]
    below = 0.5 * (1.0 + lax.erf(hidden * math.sqrt(0.5)))
    density = jnp.exp(-0.5 * hidden * hidden) * (1.0 / math.sqrt(2.0 * math.pi))
    active[...] = (hidden * below).astype(jnp.bfloat16)
    slope[...] = below + hidden * density


def grad_hidden_kernel(cotangent, slope, weight, out, out_sum, cotangent_sum):
    grad = (times_paired(cotangent[...], weight[...]) * slope[...]).astype(jnp.bfloat16)
    out[...] = grad
    add_columns(out_sum, grad)
    add_columns(cotangent_sum, cotangent[...])


def branch_terms(attn, active, dense, contract):
    return times(attn, dense) + times(active, contract)


def norm_grad_terms(grad_qkv, grad_hidden, qkv, expand, gain_one, gain_two):
    return times_paired(grad_qkv, qkv) * gain_one + times_paired(grad_hidden, expand) * gain_two


def attend_kernel(
    head_dim,
    cotangent,
    x,
    cosine,
    sine,
    segment,
    segments,
    bias,
    weight,
    dense,
    attn,
    grad_qkv,
    grad_sum,
):
    scale = 1.0 / math.sqrt(head_dim)
    half = head_dim // 8
    projected = times(x[...], weight[...]) + bias[...]
    for part in range(2):
        at = part * head_dim
        turn_into(grad_qkv, at, projected[:, at : at + head_dim], cosine[...], sine[...], half)
    query = grad_qkv[:, :head_dim]
    key = grad_qkv[:, head_dim : 2 * head_dim]
    value = projected[:, 2 * head_dim :].astype(jnp.bfloat16)
    grad_attn = times_paired(cotangent[...], dense[...]).astype(jnp.bfloat16)
    slots = query.shape[0]
    row = lax.broadcasted_iota(jnp.int32, (slots, slots), 0)
    column = lax.broadcasted_iota(jnp.int32, (slots, slots), 1)
    block = pl.program_id(0)
    allowed = (segment[...] == segments[pl.ds(block, 1), :]) & (column <= row)
    masked = jnp.where(allowed, times_paired(query, key) * scale, MASKED)
    raised = jnp.exp(masked - jnp.max(masked, axis=1, keepdims=True))
    weights = raised / jnp.sum(raised, axis=1, keepdims=True)
    probs = weights.astype(jnp.bfloat16)
    attn[...] = times(probs, value).astype(jnp.bfloat16)
    grad_probs = times_paired(grad_attn, value)
    grad_value = times_leading(probs, grad_attn)
    inner = jnp.sum(weights * grad_probs, axis=1, keepdims=True)
    grad_score = (weights * (grad_probs - inner)).astype(jnp.bfloat16)
    back = -sine[...]
    grad_query = times(grad_score, key) * scale
    turn_into(grad_qkv, 0, grad_query, cosine[...], back, half)
    grad_key = times_leading(grad_score, query) * scale
    turn_into(grad_qkv, head_dim, grad_key, cosine[...], back, half)
    grad_qkv[:, 2 * head_dim :] = grad_value.astype(jnp.bfloat16)
    add_columns(grad_sum, grad_qkv[...])


def input_terms(chain, normed, grad):
    depth, width = normed.shape
    columns = grad.shape[1]
    block = 256

    def kernel(left, right, out):
        out[...] = times_leading(left[...], right[...]).astype(jnp.bfloat16)

    return chain.launch(
        kernel,
        [normed, grad],
        [
            pl.BlockSpec((depth, block), lambda i: (0, i)),
            pl.BlockSpec((depth, columns), lambda i: (0, 0), pipeline_mode=pl.Buffered(1)),
        ],
        [((width, columns), jnp.bfloat16)],
        [pl.BlockSpec((block, columns), lambda i: (i, 0))],
        (width // block,),
    )[0]


def output_terms(chain, active, attn, groups, pair):
    depth, width = pair[0].shape
    tile = width // 4
    lefts = [active, attn]
    own = [item.shape[1] // groups for item in lefts]
    stride = sum(own)

    def kernel(active, attn, one, two, out):
        before = 0
        for left, many in zip((active, attn), own):
            terms = times_leading(left[:depth], one[...]) + times_leading(left[depth:], two[...])
            terms = terms.astype(jnp.bfloat16)
            for group in range(groups):
                at = group * stride + before
                out[at : at + many, :] = terms[group * many : (group + 1) * many]
            before = many

    return chain.launch(
        kernel,
        [active, attn, *pair],
        [
            pl.BlockSpec(item.shape, lambda i: (0, 0), pipeline_mode=pl.Buffered(1))
            for item in lefts
        ]
        + [pl.BlockSpec((depth, tile), lambda i: (0, i))] * 2,
        [((groups * stride, width), jnp.bfloat16)],
        [pl.BlockSpec((groups * stride, tile), lambda i: (0, i))],
        (width // tile,),
    )[0]


def pack(chain, arrays, moves, columns):
    rows = arrays[0].shape[0]

    def kernel(*refs):
        for slot, at, which, column, many in moves:
            refs[-1][slot, :, at : at + many] = refs[which][:, column : column + many]

    shape = (HEADS, rows, columns)
    return chain.launch(
        kernel,
        arrays,
        [whole(item) for item in arrays],
        [(shape, jnp.bfloat16)],
        [pl.BlockSpec(shape, lambda i: (0, 0, 0))],
    )[0]


def unpack(chain, places, got, sums, weight, gain, shift):
    rows, width = weight.shape
    gain = gain.astype(jnp.float32).reshape(rows, 1)
    shift = shift.astype(jnp.float32).reshape(rows, 1)

    lanes = min(128, places[0][3])

    def kernel(got, sums, weight, gain, shift, grad, gain_grad, shift_grad):
        by_gain = jnp.zeros((rows, lanes), jnp.float32)
        by_shift = jnp.zeros((rows, lanes), jnp.float32)
        for slot, start, at, many in places:
            terms = got[slot, :, start : start + many].astype(jnp.float32)
            total = sums[slot : slot + 1, start : start + many]
            parts = weight[:, at : at + many].astype(jnp.float32)
            grad[:, at : at + many] = terms * gain[...] + total * shift[...]
            for lane in range(0, many, lanes):
                span = slice(lane, lane + lanes)
                by_gain += parts[:, span] * terms[:, span]
                by_shift += parts[:, span] * total[:, span]
        gain_grad[...] = jnp.sum(by_gain.T, axis=0, keepdims=True)
        shift_grad[...] = jnp.sum(by_shift.T, axis=0, keepdims=True)

    inputs = [got, sums, weight, gain, shift]
    shapes = [(rows, width), (1, rows), (1, rows)]
    grad, gain_grad, shift_grad = chain.launch(
        kernel,
        inputs,
        [whole(item) for item in inputs],
        [(shape, jnp.float32) for shape in shapes],
        [pl.BlockSpec(shape, lambda i: (0, 0)) for shape in shapes],
    )
    return grad, gain_grad.reshape(rows), shift_grad.reshape(rows)


def per_device(
    plan,
    tokens,
    seq_lengths,
    ln1_gain,
    ln1_bias,
    ln2_gain,
    ln2_bias,
    qkv_weight,
    qkv_bias,
    dense_weight,
    dense_bias,
    expand_weight,
    expand_bias,
    contract_weight,
    contract_bias,
    cotangent,
):
    slots, width = tokens.shape
    rows = qkv_weight.shape[0]
    units = contract_weight.shape[0]
    count, groups = plan.count, plan.groups
    head_dim = width // HEADS
    rotated = head_dim // 4
    hidden_units = groups * units
    me = lax.axis_index("dp")
    slot = me % HEADS
    sharing, across = plan.sharing(), plan.across()
    outer_bits = tuple(range(3, plan.bits))
    chain = Chain()

    def gather(value):
        return lax.all_gather(value, "dp", axis=0, tiled=True, axis_index_groups=across)

    def reduce(value):
        return lax.psum_scatter(
            value, "dp", scatter_dimension=0, tiled=True, axis_index_groups=across
        )

    def exchange(value):
        return lax.all_to_all(value, "dp", 0, 0, tiled=True, axis_index_groups=sharing)

    to_slot = [(d, plan.device(d % groups, d // groups)) for d in range(count)]
    from_slot = [(target, source) for source, target in to_slot]
    dense_part = lax.ppermute(dense_weight, "dp", to_slot)
    out_part = jnp.concatenate([contract_weight, dense_part])
    weight_out = gather(out_part)
    chain.settle(out_part)

    own_tokens = own_pieces(tokens, plan)

    parts = [
        ln1_gain,
        ln1_bias,
        ln2_gain,
        ln2_bias,
        dense_bias,
        contract_bias,
        qkv_bias,
        expand_bias,
        seq_lengths[0].astype(jnp.bfloat16),
    ]
    sizes = [item.shape[0] for item in parts]
    lines = -(-sum(sizes) // 1024) * 8
    small = jnp.concatenate(parts + [jnp.zeros((lines * 128 - sum(sizes),), jnp.bfloat16)])
    every = gather_small(small.reshape(lines, 128), (1, 2, 0) + outer_bits, me, plan)
    every = every.reshape(count, lines * 128).astype(jnp.float32)

    expand_places = [
        (s, group * units, plan.device(group, s) * units, units)
        for s in range(HEADS)
        for group in range(groups)
    ]
    qkv_places = [
        (s, part * head_dim, part * width + s * head_dim, head_dim)
        for s in range(HEADS)
        for part in range(3)
    ]
    split = 3 * head_dim
    moves = [(s, at, 0, column, many) for s, at, column, many in qkv_places]
    moves += [(s, split + at, 1, column, many) for s, at, column, many in expand_places]
    own = exchange(pack(chain, [qkv_weight, expand_weight], moves, split + hidden_units))
    token_pieces = all_pieces(own_tokens, own_tokens[4], 1, plan)
    own_cotangent = own_pieces(cotangent, plan)
    taken, at = [], 0
    for size in sizes:
        taken.append(every[:, at : at + size])
        at += size
    gain_one, shift_one, gain_two, shift_two, bias_dense, bias_contract = [
        item.reshape(1, width) for item in taken[:6]
    ]
    bias_qkv = lax.dynamic_index_in_dim(
        taken[6].reshape(3, HEADS, head_dim), slot, 1, keepdims=False
    ).reshape(1, split)
    bias_expand = lax.dynamic_index_in_dim(
        taken[7].reshape(groups, HEADS, units), slot, 1, keepdims=False
    ).reshape(1, hidden_units)
    lengths = jnp.concatenate(
        [lax.dynamic_slice_in_dim(taken[8], me ^ mask, 1) for mask in ORDER]
    ).astype(jnp.int32)
    segment, position = jax.vmap(lambda item: slot_layout(item, slots))(lengths)
    cosine, sine = rotary_tables(position.reshape(-1), rotated, head_dim // 2)
    chain.settle(every, *[piece for piece, _ in token_pieces[4:7]])
    qkv_own, expand_own = split_columns(chain, own.reshape(HEADS * rows, -1), split)
    weight_expand, weight_qkv = gather(expand_own), gather(qkv_own)
    bias_out = bias_dense + bias_contract
    segment_column = segment.reshape(-1, 1)
    chain.settle(cosine, weight_out)

    def sum_begin(compute, blocked, known):
        terms = terms_of(chain, compute, slots, width, 1, blocked, known, (), False)
        return [swap(item, 0, plan) for item in terms]

    def sum_next(compute, blocked, known, got):
        own, of_x, of_y, left, right = terms_of(
            chain, compute, slots, width, 0, blocked, known, got, True
        )
        return own, of_x, of_y, swap(left, 1, plan), swap(right, 2, plan)

    def sum_last(own, *parts):
        to_x, to_y = pass_terms(chain, *parts)
        return own, swap(to_x, 1, plan), swap(to_y, 2, plan)

    low_one, low_two, normed = over_blocks(
        chain,
        norm_kernel,
        slots,
        token_pieces,
        [],
        [gain_one, shift_one, gain_two, shift_two],
        [(width, jnp.bfloat16)] * 3,
    )

    passed = swap(copied(chain, own_cotangent[2]), 2, plan)
    weight_contract, weight_dense = part_rows(chain, weight_out, groups, units, rows)
    chain.settle(sine, segment_column, bias_qkv, bias_out)
    half = laid_together(
        chain, [own_cotangent[0], own_cotangent[2], own_cotangent[4], passed]
    )
    other_half = swap(half, 0, plan)
    group_cotangent = (half, other_half)

    active, slope = over_blocks(
        chain,
        expand_kernel,
        slots,
        [],
        [low_two],
        [bias_expand, weight_expand],
        [(hidden_units, jnp.bfloat16), (hidden_units, jnp.float32)],
    )
    grad_hidden, hidden_sum, cotangent_sum = over_blocks(
        chain,
        grad_hidden_kernel,
        slots,
        [],
        [slope],
        [weight_contract],
        [(hidden_units, jnp.bfloat16)],
        [hidden_units, width],
        pair=group_cotangent,
    )
    expand_got = reduce(input_terms(chain, normed, grad_hidden))

    attn, grad_qkv, qkv_sum = over_blocks(
        chain,
        lambda *refs: attend_kernel(head_dim, *refs),
        slots,
        [],
        [low_one, cosine, sine, segment_column],
        [segment, bias_qkv, weight_qkv, weight_dense],
        [(head_dim, jnp.bfloat16), (split, jnp.bfloat16)],
        [split],
        pair=group_cotangent,
    )


    branch_of = branch_terms, [attn, active], [weight_dense, weight_contract]
    norm_of = (
        norm_grad_terms,
        [grad_qkv, grad_hidden],
        [weight_qkv, weight_expand, gain_one, gain_two],
    )
    qkv_got = reduce(input_terms(chain, normed, grad_qkv))
    branch_got = sum_begin(*branch_of)
    norm_got = sum_begin(*norm_of)
    branch = sum_next(*branch_of, branch_got)
    expand_got = exchange(expand_got.reshape(HEADS, rows, hidden_units))
    chain.settle(expand_got)
    output_got = reduce(output_terms(chain, active, attn, groups, group_cotangent))
    branch = sum_last(*branch)
    chain.settle(qkv_got)
    norm_parts = sum_next(*norm_of, norm_got)
    layer_out = finish_output(chain, tokens, *branch, bias_out)

    norm_parts = sum_last(*norm_parts)
    contract_weight_grad, dense_grad = split_output(chain, output_got, units, rows)
    dense_weight_grad = lax.ppermute(dense_grad, "dp", from_slot).astype(jnp.float32)

    sums = jnp.concatenate([qkv_sum, hidden_sum, cotangent_sum], axis=1).reshape(-1, 128)
    for bit in outer_bits:
        sums = sums + swap(sums, bit, plan)
    own_lines = (split + hidden_units) // 128
    bias_out_grad = lax.dynamic_slice_in_dim(
        sums[own_lines:].reshape(-1), me * (width // count), width // count
    )
    sums = gather_small(sums[:own_lines], (0, 1, 2), me, plan)
    chain.settle(sums)
    sums = sums.reshape(HEADS, -1)
    qkv_sums, expand_sums = sums[:, :split], sums[:, split:]

    expand_weight_grad, ln2_gain_grad, ln2_bias_grad = unpack(
        chain, expand_places, expand_got, expand_sums, expand_weight, ln2_gain, ln2_bias
    )
    input_grad = finish_input(chain, cotangent, tokens, *norm_parts)
    qkv_got = exchange(qkv_got.reshape(HEADS, rows, split))
    qkv_weight_grad, ln1_gain_grad, ln1_bias_grad = unpack(
        chain, qkv_places, qkv_got, qkv_sums, qkv_weight, ln1_gain, ln1_bias
    )
    qkv_bias_grad = qkv_sums.reshape(HEADS, 3, head_dim).transpose(1, 0, 2).reshape(3 * width)
    per = qkv_bias.shape[0]
    qkv_bias_grad = lax.dynamic_slice_in_dim(qkv_bias_grad, me * per, per)
    expand_bias_grad = lax.dynamic_slice(
        expand_sums, (slot, (me // HEADS) * units), (1, units)
    ).reshape(units)
    return (
        layer_out,
        input_grad,
        ln1_gain_grad,
        ln1_bias_grad,
        ln2_gain_grad,
        ln2_bias_grad,
        qkv_weight_grad,
        qkv_bias_grad,
        dense_weight_grad,
        bias_out_grad,
        expand_weight_grad,
        expand_bias_grad,
        contract_weight_grad,
        bias_out_grad,
    )


def solution(mesh):
    in_specs = (
        P("dp", None),
        P("dp", None),
        P("dp"),
        P("dp"),
        P("dp"),
        P("dp"),
        P("dp", None),
        P("dp"),
        P("dp", None),
        P("dp"),
        P("dp", None),
        P("dp"),
        P("dp", None),
        P("dp"),
        P("dp", None),
    )
    out_specs = (
        P("dp", None),
        P("dp", None),
        P("dp"),
        P("dp"),
        P("dp"),
        P("dp"),
        P("dp", None),
        P("dp"),
        P("dp", None),
        P("dp"),
        P("dp", None),
        P("dp"),
        P("dp", None),
        P("dp"),
    )
    plan = Plan(mesh.shape["dp"])

    def layer(*arrays):
        return per_device(plan, *arrays)

    return jax.shard_map(layer, mesh=mesh, in_specs=in_specs, out_specs=out_specs, check_vma=False)
```
